32 devices in a mesh: mem: 16 (over z, x, core), lat: 2 (over y).
Axes of the slice: x: 2, y: 2, z: 4, core: 2. Of those that a mesh axis runs over, the one named last changes fastest.
Arguments:
- perturb: bfloat16 [3, 3, 48, 32, 8, 256], P(None, None, 'mem', None, 'lat'), may hold values from -0.875 to 0.875
- alpha_init: float32 [48, 32, 8, 256], P('mem', None, 'lat'), may hold values from -6 to 6
- innovation: float32 [288, 8, 256], P('mem', 'lat'), may hold values from -6 to 6
- obs_weight: float32 [288, 8, 256], P('mem', 'lat'), may hold values from 0.5 to 2
- coef: float32 [2, 8, 256], P(None, 'lat'), may hold values from 0.12 to 0.24
- obs_mask: int32 [3, 2, 64], P(None, 'lat'), may hold values 0 or 1
Outputs:
- alpha_out: float32 [48, 32, 8, 256], P('mem', None, 'lat')
- misfit: float32 [288, 8, 256], P('mem', 'lat')
The draws below stay inside these ranges and needn't reach their ends.
All inputs are finite; a program needn't handle non-finite values. No bound on the sum of `obs_mask` on one device may be relied on, other than what follows from the above.
Results may differ from the reference program's by a relative error of at most 0.0003.
Values sent between devices are 32-bit elements; how exact they have to be, the bound alone decides.
No kernel may reach another device: no remote copies, remote signals or barrier semaphores. Data moves between devices by JAX's collectives and lax.ppermute only.
A program may use at most 64 MiB of HBM per device.

```python
import math
import jax
import jax.numpy as jnp
from jax import lax

SLOTS = 3
VARS = 3
LEV = 32
LON = 256
ITERS = 2
DIFF_STEPS = 4
TILE = 4
LAT = 8
MEMBERS = 48
SVL = 288


def place_ends(array, stream_key, low, top_value):
    index_at = [jax.random.randint(jax.random.fold_in(stream_key, axis), (), 0, length) for axis, length in enumerate(array.shape)]
    longest = array.shape.index(max(array.shape))
    beside = index_at[:longest] + [(index_at[longest] + 1) % array.shape[longest]] + index_at[longest + 1:]
    return array.at[tuple(index_at)].set(low).at[tuple(beside)].set(top_value)


def level_of(key, extent, cuts, low, largest):
    factor_of, own = 1.0, jax.random.fold_in(key, 6)
    for position, parts in cuts:
        draws = jnp.exp(jax.random.uniform(jax.random.fold_in(own, position), (parts,), jnp.float32, low / len(cuts), largest / len(cuts)))
        factor_of = factor_of * jnp.repeat(draws, extent[position] // parts).reshape([-1 if axis == position else 1 for axis in range(len(extent))])
    return factor_of


def noise(stream_key, dims, scale, bound, shards=(), kind=jnp.bfloat16):
    drawn = scale * jax.random.normal(stream_key, dims, jnp.float32)
    if shards:
        drawn = drawn * level_of(stream_key, dims, shards, -0.22, 0.18)
    return jnp.clip(drawn, -bound, bound).astype(kind)


def setup_inputs(seed: int = 0) -> dict:
    key_of = jax.random.split(jax.random.key(seed), 7)
    return {
        "perturb": noise(key_of[0], (SLOTS, VARS, MEMBERS, LEV, LAT, LON), MEMBERS ** -0.5, 0.875, ((2, 16), (4, 2))),
        "alpha_init": noise(key_of[1], (MEMBERS, LEV, LAT, LON), 1.0, 6.0, ((0, 16), (2, 2)), jnp.float32),
        "innovation": noise(key_of[2], (SVL, LAT, LON), 1.0, 6.0, ((0, 16), (1, 2)), jnp.float32),
        "obs_weight": jnp.clip(jnp.exp(math.log(2.0) - 1.3862944 * jax.random.uniform(key_of[3], (SVL, LAT, LON), jnp.float32) ** level_of(key_of[3], (SVL, LAT, LON), ((0, 16), (1, 2)), -0.2, 0.2)), 0.5, 2.0),
        "coef": jnp.clip(jnp.exp(math.log(0.24) - 0.6931472 * jax.random.uniform(key_of[4], (2, LAT, LON), jnp.float32) ** level_of(key_of[4], (2, LAT, LON), ((1, 2),), -0.2, 0.2)), 0.12, 0.24),
        "obs_mask": place_ends((jax.random.randint(key_of[5], (SLOTS, LAT // TILE, LON // TILE), 0, 3) < 2).astype(jnp.int32), jax.random.fold_in(key_of[5], 1), 0, 1),
    }


def face_weights(coef):
    klat = coef[0]
    klon = coef[1]
    zero_row = jnp.zeros_like(klat[:1])
    north_face = 0.5 * (klat + jnp.concatenate([zero_row, klat[:-1]], axis=0))
    south_face = 0.5 * (klat + jnp.concatenate([klat[1:], zero_row], axis=0))
    east_face = 0.5 * (klon + jnp.roll(klon, -1, axis=1))
    west_face = 0.5 * (klon + jnp.roll(klon, 1, axis=1))
    return north_face, south_face, east_face, west_face


def diffuse_once(layer_field, face_list, valid_rows):
    north_face, south_face, east_face, west_face = face_list
    zero_row = jnp.zeros_like(layer_field[..., :1, :])
    above = jnp.concatenate([zero_row, layer_field[..., :-1, :]], axis=-2)
    below = jnp.concatenate([layer_field[..., 1:, :], zero_row], axis=-2)
    east_val = jnp.roll(layer_field, -1, axis=-1)
    west_val = jnp.roll(layer_field, 1, axis=-1)
    updated = layer_field + north_face * (above - layer_field) + south_face * (below - layer_field)
    updated = updated + east_face * (east_val - layer_field) + west_face * (west_val - layer_field)
    return updated * valid_rows


def diffuse_field(layer_field, face_list):
    for sweep in range(DIFF_STEPS):
        layer_field = diffuse_once(layer_field, face_list, jnp.float32(1.0))
    return layer_field


def reference(perturb, alpha_init, innovation, obs_weight, coef, obs_mask):
    face_list = face_weights(coef)
    tile_mask = jnp.repeat(jnp.repeat(obs_mask, TILE, axis=1), TILE, axis=2).astype(jnp.float32)
    row_gain = obs_weight * jnp.repeat(tile_mask, VARS * LEV, axis=0)
    alpha = alpha_init
    misfit = jnp.zeros((SVL, LAT, LON), jnp.float32)
    for sweep in range(ITERS):
        spread = diffuse_field(alpha, face_list)

        def add_member(member, total):
            piece = lax.dynamic_index_in_dim(perturb, member, 2, keepdims=False).astype(jnp.float32)
            member_field = lax.dynamic_index_in_dim(spread, member, 0, keepdims=False)
            return total + piece * member_field[None, None]

        increment = lax.fori_loop(0, MEMBERS, add_member, jnp.zeros((SLOTS, VARS, LEV, LAT, LON), jnp.float32))
        misfit = row_gain * (increment.reshape(SVL, LAT, LON) - innovation)
        misfit_rows = misfit.reshape(SLOTS, VARS, LEV, LAT, LON)

        def member_adjoint(member):
            piece = lax.dynamic_index_in_dim(perturb, member, 2, keepdims=False).astype(jnp.float32)
            return jnp.sum(piece * misfit_rows, axis=(0, 1))

        adjoint = lax.map(member_adjoint, jnp.arange(MEMBERS, dtype=jnp.int32))
        alpha = alpha - 0.3 * (alpha + diffuse_field(adjoint, face_list))
    return alpha, misfit
```

```python
import functools

import jax
import jax.numpy as jnp
from jax import lax
from jax.experimental import pallas as pl
from jax.experimental.pallas import tpu as pltpu
from jax.sharding import PartitionSpec as P

ITERS = 2
DIFF_STEPS = 4
TILE = 4


def with_halo(cells, sides, width):
    for axis, dim in sides:
        count = lax.axis_size(axis)
        ends = count - 1
        head = lax.slice_in_dim(cells, 0, width, axis=dim)
        tail = lax.slice_in_dim(cells, cells.shape[dim] - width, cells.shape[dim], axis=dim)
        cells = jnp.concatenate(
            [
                lax.ppermute(tail, axis, [(i, (i + 1) % count) for i in range(ends)]),
                cells,
                lax.ppermute(head, axis, [((i + 1) % count, i) for i in range(ends)]),
            ],
            axis=dim,
        )
    return cells


def face_weights(coef):
    klat = coef[0]
    klon = coef[1]
    zero_row = jnp.zeros_like(klat[:1])
    north_face = 0.5 * (klat + jnp.concatenate([zero_row, klat[:-1]], axis=0))
    south_face = 0.5 * (klat + jnp.concatenate([klat[1:], zero_row], axis=0))
    east_face = 0.5 * (klon + jnp.roll(klon, -1, axis=1))
    west_face = 0.5 * (klon + jnp.roll(klon, 1, axis=1))
    return (north_face, south_face, east_face, west_face)


def diffuse_once(layer_field, face_list, valid_rows):
    north_face, south_face, east_face, west_face = face_list
    zero_row = jnp.zeros_like(layer_field[..., :1, :])
    above = jnp.concatenate([zero_row, layer_field[..., :-1, :]], axis=-2)
    below = jnp.concatenate([layer_field[..., 1:, :], zero_row], axis=-2)
    east_val = jnp.roll(layer_field, -1, axis=-1)
    west_val = jnp.roll(layer_field, 1, axis=-1)
    updated = layer_field + north_face * (above - layer_field) + south_face * (below - layer_field)
    updated = updated + east_face * (east_val - layer_field) + west_face * (west_val - layer_field)
    return updated * valid_rows


def rim_rows(all_faces):
    return tuple((face for face in all_faces))


def valid_mask(margin, band_rows):
    global_row = (
        lax.axis_index("lat") * band_rows
        + jnp.arange(band_rows + 2 * margin, dtype=jnp.int32)
        - margin
    )
    total_rows = band_rows * lax.axis_size("lat")
    inside = jnp.logical_and(global_row >= 0, global_row < total_rows)
    return inside.astype(jnp.float32)[:, None]


def diffuse_field(layer_field, all_faces, band_rows):
    face_list = rim_rows(all_faces)
    valid_rows = valid_mask(DIFF_STEPS, band_rows)
    extended = with_halo(layer_field, (("lat", 2),), DIFF_STEPS)
    for sweep in range(DIFF_STEPS):
        extended = diffuse_once(extended, face_list, valid_rows)
    return extended[..., DIFF_STEPS : DIFF_STEPS + band_rows, :]


def shards(perturb, alpha_init, innovation, obs_weight, coef, obs_mask):
    slot_count, var_count, members, levels, band_rows, lon_cells = perturb.shape
    owned_rows = innovation.shape[0]
    coef_ext = with_halo(coef, (("lat", 1),), DIFF_STEPS)
    all_faces = face_weights(coef_ext)
    tile_mask = jnp.repeat(jnp.repeat(obs_mask, TILE, axis=1), TILE, axis=2).astype(jnp.float32)
    first_row = lax.axis_index("mem") * owned_rows
    slot_of_row = (first_row + jnp.arange(owned_rows, dtype=jnp.int32)) // (var_count * levels)
    one_hot = (slot_of_row[:, None] == jnp.arange(slot_count, dtype=jnp.int32)[None, :]).astype(
        jnp.float32
    )
    row_mask = jnp.sum(one_hot[:, :, None, None] * tile_mask[None], axis=1)
    row_gain = obs_weight * row_mask
    alpha = alpha_init
    misfit = jnp.zeros_like(innovation)
    for sweep in range(ITERS):
        spread = diffuse_field(alpha, all_faces, band_rows)
        partial_sum = jnp.sum(perturb.astype(jnp.float32) * spread[None, None], axis=2)
        partial_sum = partial_sum.reshape(slot_count * var_count * levels, band_rows, lon_cells)
        increment = lax.psum_scatter(partial_sum, "mem", scatter_dimension=0, tiled=True)
        misfit = row_gain * (increment - innovation)
        gathered = lax.all_gather(misfit, "mem", axis=0, tiled=True)
        misfit_rows = gathered.reshape(slot_count, var_count, levels, band_rows, lon_cells)
        adjoint = jnp.sum(perturb.astype(jnp.float32) * misfit_rows[:, :, None], axis=(0, 1))
        alpha = alpha - 0.3 * (alpha + diffuse_field(adjoint, all_faces, band_rows))
    return (alpha, misfit)


LANES = 128
SUBLANES = 8
CHIPS = 8
CORES = 2
GROUP = CHIPS * CORES


def fold(cells):
    lead, (rows, cols) = cells.shape[:-2], cells.shape[-2:]
    parts = cells.reshape(*lead, rows, cols // LANES, LANES).swapaxes(-3, -2)
    return parts.reshape(*lead, rows * cols // LANES, LANES)


def fits(mesh, perturb, innovation):
    slot_count, var_count, members, levels, rows, lon_cells = perturb.shape
    mem, lat = mesh.shape["mem"], mesh.shape["lat"]
    if lat != 2 or mem % (2 * CHIPS // lat * CORES) or mem // (CHIPS // lat * CORES) != 2:
        return False
    if rows != lat * TILE or DIFF_STEPS > TILE or TILE * lon_cells != SUBLANES * LANES:
        return False
    total = slot_count * var_count * levels
    if members % mem or levels % GROUP or total % mem or total // mem > levels:
        return False
    return held_pairs(slot_count * var_count, levels) is not None


def held_pairs(fields, levels):
    halves = ([], [])
    for chunk in range(levels // GROUP):
        for field in range(fields):
            rows = [field * levels + chunk * GROUP + member for member in range(GROUP)]
            sides = {2 * row // (fields * levels) for row in rows}
            if len(sides) != 1:
                return None
            halves[sides.pop()].append((field, chunk))
    return halves if len(halves[0]) == len(halves[1]) else None


def flat_offset(chip, core):
    return ((chip >> 1) << 2) | (core << 1) | (chip & 1)


def shift_by(mask, cells):
    axes = ("mem", "lat")
    count = lax.axis_size("mem") * lax.axis_size("lat")
    return lax.ppermute(cells, axes, [(i, i ^ mask) for i in range(count)])


class Sizes:
    def __init__(self, perturb, owned_rows):
        slots, variables, members, levels = perturb.shape[:4]
        self.vars = variables
        self.fields = slots * variables
        self.members = members
        self.levels = levels
        self.owned = owned_rows
        self.chunks = levels // GROUP
        self.planes = self.fields * members
        self.rows = self.planes + members + 2
        self.held = held_pairs(self.fields, levels)
        self.sums = self.chunks * self.fields * 2
        self.gains = len(self.held[0]) * 2


def row_in_block(size, level, mem_index):
    row = lax.rem(level + size.levels * size.owned - lax.rem(size.owned * mem_index, size.levels), size.levels)
    return row, row < size.owned, lax.div(size.owned * mem_index + row, size.levels)


def pack_kernel(size, flat_ref, perturb_ref, alpha_ref, innov_ref, weight_ref, mask_ref, *outs):
    flat = flat_ref[0]
    own = lax.rem(flat, GROUP)
    mem_index = lax.div(flat, 2)
    for chip in range(CHIPS):
        for core in range(CORES):
            for chunk in range(size.chunks):
                out = outs[chip].at[chunk] if core == 0 else outs[CHIPS].at[chip, chunk]
                level = lax.bitwise_xor(own, flat_offset(chip, core)) + chunk * GROUP
                out[0 : size.planes] = perturb_ref[:, level].astype(jnp.float32)
                out[size.planes : size.planes + size.members] = alpha_ref[:, level]
                row, inside, field = row_in_block(size, level, mem_index)
                row = jnp.minimum(row, size.owned - 1)
                slot = jnp.minimum(lax.div(field, size.vars), mask_ref.shape[0] - 1)
                kept = jnp.where(inside, 1.0, 0.0).astype(jnp.float32)
                out[size.rows - 2] = innov_ref[row] * kept
                out[size.rows - 1] = weight_ref[row] * mask_ref[slot] * kept


def roll(cells, shift, axis):
    return pltpu.roll(cells, shift, axis=cells.ndim + axis)


def neighbours(own, other, edges):
    row0, row3, lane0, lane_last = edges
    turned = roll(own, SUBLANES // 2, -2)
    across = roll(other, SUBLANES // 2, -2)
    above = roll(jnp.where(row3, across, own), 1, -2)
    below = roll(jnp.where(row0, across, own), SUBLANES - 1, -2)
    east = roll(jnp.where(lane0, turned, own), LANES - 1, -1)
    west = roll(jnp.where(lane_last, turned, own), 1, -1)
    return above, below, east, west


def stencils(flat, near_ref, far_ref):
    shape = (SUBLANES, LANES)
    line = lax.rem(lax.broadcasted_iota(jnp.int32, shape, 0), TILE)
    lane = lax.broadcasted_iota(jnp.int32, shape, 1)
    edges = (line == 0, line == TILE - 1, lane == 0, lane == LANES - 1)
    band = lax.rem(flat, 2)
    weights = []
    for half, (own_ref, other_ref) in enumerate(((near_ref, far_ref), (far_ref, near_ref))):
        here = lax.bitwise_xor(band, half)
        open_top = jnp.where(jnp.logical_and(edges[0], here == 0), 0.0, 1.0).astype(jnp.float32)
        open_end = jnp.where(jnp.logical_and(edges[1], here == 1), 0.0, 1.0).astype(jnp.float32)
        above, below, _, _ = neighbours(own_ref[0], other_ref[0], edges)
        _, _, east, west = neighbours(own_ref[1], other_ref[1], edges)
        north = 0.5 * (own_ref[0] + above * open_top)
        south = 0.5 * (own_ref[0] + below * open_end)
        east = 0.5 * (own_ref[1] + east)
        west = 0.5 * (own_ref[1] + west)
        centre = 1.0 - north - south - east - west
        weights.append((centre, north * open_top, south * open_end, east, west))
    return edges, weights


def diffuse_pair(near, far, stencil):
    edges, weights = stencil
    for _ in range(DIFF_STEPS):
        pair = []
        for (own, other), (centre, north, south, east, west) in zip(((near, far), (far, near)), weights):
            above, below, right, left = neighbours(own, other, edges)
            pair.append(centre * own + north * above + south * below + east * right + west * left)
        near, far = pair
    return near, far


def piece(pieces, chip, core):
    return pieces[chip * CORES + core]


def add_products(size, pieces, chunk, pair, spread, sums):
    for half in range(2):
        for core in range(CORES):
            ref = piece(pieces, 2 * pair + half, core)
            for field in range(size.fields):
                for member in range(size.members):
                    term = ref[chunk, field * size.members + member] * spread[half][core * size.members + member]
                    known = sums[half][field]
                    sums[half][field] = term if known is None else known + term
    return sums


def adjoint_of(size, pieces, chunk, pair, misfit):
    halves = []
    for half in range(2):
        found = []
        for core in range(CORES):
            ref = piece(pieces, 2 * pair + half, core)
            for member in range(size.members):
                total = None
                for field in range(size.fields):
                    term = ref[chunk, field * size.members + member] * misfit[half][field]
                    total = term if total is None else total + term
                found.append(total)
        halves.append(jnp.stack(found))
    return halves


def first_alpha(size, pieces, chunk, pair):
    rows = slice(size.planes, size.planes + size.members)
    return [
        jnp.concatenate([piece(pieces, 2 * pair + half, core)[chunk, rows] for core in range(CORES)])
        for half in range(2)
    ]


def first_kernel(size, flat_ref, near_ref, far_ref, *refs):
    pieces, (sum_ref, gain_ref, innov_ref) = refs[:GROUP], refs[GROUP:]
    flat = flat_ref[0]
    stencil = stencils(flat, near_ref, far_ref)
    mem_index = lax.div(flat, 2)
    side = lax.div(flat, GROUP)
    gain_ref[...] = jnp.zeros_like(gain_ref)
    innov_ref[...] = jnp.zeros_like(innov_ref)
    for chunk in range(size.chunks):
        level = lax.rem(flat, GROUP) + chunk * GROUP
        for chip in range(0, CHIPS, 2):
            for core in range(CORES):
                source = lax.bitwise_xor(mem_index, (chip & 6) | core)
                _, inside, field = row_in_block(size, level, source)

                @pl.when(inside)
                def _(chip=chip, core=core, chunk=chunk, field=field):
                    for half in range(2):
                        ref = piece(pieces, chip + half, core)
                        innov_ref[chunk, field, half] = ref[chunk, size.rows - 2]
                        gain_ref[chunk, field, half] = ref[chunk, size.rows - 1]

    for chunk in range(size.chunks):
        sums = [[None] * size.fields for _ in range(2)]
        for pair in range(CHIPS // 2):
            spread = diffuse_pair(*first_alpha(size, pieces, chunk, pair), stencil)
            add_products(size, pieces, chunk, pair, spread, sums)
        for field in range(size.fields):
            for half in range(2):
                sum_ref[(chunk * size.fields + field) * 2 + half] = sums[half][field] - innov_ref[chunk, field, half]
    for place, (first, second) in enumerate(zip(*size.held)):
        field = jnp.where(side == 0, first[0], second[0])
        chunk = jnp.where(side == 0, first[1], second[1])
        sum_ref[pl.ds(size.sums + 2 * place, 2)] = gain_ref[chunk, field]


def misfit_of(size, chunk, gain_ref, mine_ref, theirs_ref):
    halves = []
    for half in range(2):
        rows = []
        for field in range(size.fields):
            at = (chunk * size.fields + field) * 2 + half
            rows.append(gain_ref[chunk, field, half] * (mine_ref[at] + theirs_ref[at]))
        halves.append(rows)
    return halves


def middle_kernel(size, flat_ref, near_ref, far_ref, mine_ref, theirs_ref, held_ref, innov_ref, *refs):
    pieces, (sum_ref, gain_ref, alpha_ref) = refs[:GROUP], refs[GROUP:]
    flat = flat_ref[0]
    side = lax.div(flat, GROUP)
    stencil = stencils(flat, near_ref, far_ref)
    gain_ref[...] = held_ref[...]
    for place, (first, second) in enumerate(zip(*size.held)):
        field = jnp.where(side == 0, second[0], first[0])
        chunk = jnp.where(side == 0, second[1], first[1])
        gain_ref[chunk, field] = theirs_ref[pl.ds(size.sums + 2 * place, 2)]
    for chunk in range(size.chunks):
        misfit = misfit_of(size, chunk, gain_ref, mine_ref, theirs_ref)
        sums = [[None] * size.fields for _ in range(2)]
        for pair in range(CHIPS // 2):
            change = diffuse_pair(*adjoint_of(size, pieces, chunk, pair, misfit), stencil)
            before = first_alpha(size, pieces, chunk, pair)
            alpha = [old - 0.3 * (old + new) for old, new in zip(before, change)]
            for half in range(2):
                alpha_ref[chunk, pair, half] = alpha[half]
            add_products(size, pieces, chunk, pair, diffuse_pair(*alpha, stencil), sums)
        for field in range(size.fields):
            for half in range(2):
                sum_ref[(chunk * size.fields + field) * 2 + half] = sums[half][field] - innov_ref[chunk, field, half]


def last_kernel(size, flat_ref, near_ref, far_ref, mine_ref, theirs_ref, gain_ref, alpha_ref, *refs):
    pieces, outs = refs[:GROUP], refs[GROUP : GROUP + CHIPS + 1]
    misfit_ref = refs[-1]
    flat = flat_ref[0]
    mem_index = lax.div(flat, 2)
    stencil = stencils(flat, near_ref, far_ref)
    for chunk in range(size.chunks):
        misfit = misfit_of(size, chunk, gain_ref, mine_ref, theirs_ref)
        for half in range(2):
            for field in range(size.fields):
                misfit_ref[chunk, half, field] = misfit[half][field]
        level = lax.rem(flat, GROUP) + chunk * GROUP
        base = chunk * (size.members + 1)
        for pair in range(CHIPS // 2):
            change = diffuse_pair(*adjoint_of(size, pieces, chunk, pair, misfit), stencil)
            for half in range(2):
                old = alpha_ref[chunk, pair, half]
                alpha = old - 0.3 * (old + change[half])
                chip = 2 * pair + half
                for core in range(CORES):
                    out = outs[chip] if core == 0 else outs[CHIPS].at[chip]
                    out[base : base + size.members] = alpha[core * size.members : (core + 1) * size.members]
                    target = lax.bitwise_xor(mem_index, (chip & 6) | core)
                    _, _, field = row_in_block(size, level, target)
                    out[base + size.members] = misfit_ref[chunk, half, jnp.minimum(field, size.fields - 1)]


def unfold_into(out, at, block):
    rows = block.shape[-2] // 2
    out[at + (slice(None), slice(0, LANES))] = block[..., :rows, :]
    out[at + (slice(None), slice(LANES, 2 * LANES))] = block[..., rows:, :]


def place_kernel(size, flat_ref, *refs):
    pieces, (alpha_ref, misfit_ref) = refs[:GROUP], refs[GROUP:]
    flat = flat_ref[0]
    mem_index = lax.div(flat, 2)
    for chip in range(CHIPS):
        for core in range(CORES):
            ref = piece(pieces, chip, core)
            for chunk in range(size.chunks):
                base = chunk * (size.members + 1)
                level = lax.bitwise_xor(lax.rem(flat, GROUP), flat_offset(chip, core)) + chunk * GROUP
                for member in range(size.members):
                    unfold_into(alpha_ref, (member, level), ref[base + member])
                row, inside, _ = row_in_block(size, level, mem_index)

                @pl.when(inside)
                def _(ref=ref, base=base, row=row):
                    unfold_into(misfit_ref, (row,), ref[base + size.members])


def call(kernel, size, outs, operands, scratch=()):
    specs = [pl.BlockSpec(memory_space=pltpu.SMEM)] + [pl.BlockSpec(memory_space=pltpu.VMEM)] * (len(operands) - 1)
    return pl.pallas_call(
        functools.partial(kernel, size),
        out_shape=[jax.ShapeDtypeStruct(shape, jnp.float32) for shape in outs],
        in_specs=specs,
        out_specs=[pl.BlockSpec(memory_space=pltpu.VMEM)] * len(outs),
        scratch_shapes=scratch,
        compiler_params=pltpu.CompilerParams(vmem_limit_bytes=24 * 1024 * 1024),
    )(*operands)


def exchange_chips(kept, crossed):
    pieces = [None] * GROUP
    for part, core in ((kept, 0), (crossed, 1)):
        pieces[core] = part[0]
        for chip in (7, 1, 2, 4, 3, 5, 6):
            pieces[chip * CORES + core] = shift_by(flat_offset(chip, 0), part[chip])
    return pieces


def level_shards(perturb, alpha_init, innovation, obs_weight, coef, obs_mask):
    size = Sizes(perturb, innovation.shape[0])
    levels, rows, lon_cells = perturb.shape[3:]
    block = (SUBLANES, LANES)
    flat = (lax.axis_index("mem") * lax.axis_size("lat") + lax.axis_index("lat")).astype(jnp.int32).reshape(1)
    near = fold(coef)
    far = shift_by(1, near)
    tile_mask = jnp.repeat(jnp.repeat(obs_mask, TILE, axis=1), TILE, axis=2).astype(jnp.float32)
    packed = call(
        pack_kernel,
        size,
        [(size.chunks, size.rows, *block)] * CHIPS + [(CHIPS, size.chunks, size.rows, *block)],
        (
            flat,
            fold(perturb).reshape(size.planes, levels, *block),
            fold(alpha_init),
            fold(innovation),
            fold(obs_weight),
            fold(tile_mask),
        ),
    )
    crossed = shift_by(CORES, packed[CHIPS])
    pieces = exchange_chips(packed[:CHIPS], [crossed[chip] for chip in range(CHIPS)])
    common = (flat, near, far)
    per_field = (size.chunks, size.fields, 2, *block)
    mine, held, innov = call(
        first_kernel, size, [(size.sums + size.gains, *block), per_field, per_field], common + tuple(pieces)
    )
    theirs = shift_by(GROUP, mine)
    alpha_shape = (size.chunks, CHIPS // 2, 2, CORES * size.members, *block)
    mine, gain, alpha = call(
        middle_kernel,
        size,
        [(size.sums, *block), per_field, alpha_shape],
        common + (mine, theirs, held, innov) + tuple(pieces),
    )
    theirs = shift_by(GROUP, mine)
    back = size.chunks * (size.members + 1)
    done = call(
        last_kernel,
        size,
        [(back, *block)] * CHIPS + [(CHIPS, back, *block)],
        common + (mine, theirs, gain, alpha) + tuple(pieces),
        [pltpu.VMEM((size.chunks, 2, size.fields, *block), jnp.float32)],
    )
    crossed = shift_by(CORES, done[CHIPS])
    pieces = exchange_chips(done[:CHIPS], [crossed[chip] for chip in range(CHIPS)])
    return tuple(
        call(
            place_kernel,
            size,
            [(size.members, levels, rows, lon_cells), (size.owned, rows, lon_cells)],
            (flat,) + tuple(pieces),
        )
    )


def solution(mesh):
    in_specs = (
        P(None, None, "mem", None, "lat", None),
        P("mem", None, "lat", None),
        P("mem", "lat", None),
        P("mem", "lat", None),
        P(None, "lat", None),
        P(None, "lat", None),
    )
    out_specs = (P("mem", None, "lat", None), P("mem", "lat", None))

    def run(*args):
        body = level_shards if fits(mesh, args[0], args[2]) else shards
        return jax.shard_map(body, mesh=mesh, in_specs=in_specs, out_specs=out_specs, check_vma=False)(*args)

    return run
```

```python
import functools
import math

import jax
import jax.numpy as jnp
from jax import lax
from jax.experimental import pallas as pl
from jax.experimental.pallas import tpu as pltpu
from jax.sharding import PartitionSpec as P

ITERS = 2
DIFF_STEPS = 4
TILE = 4


def with_halo(cells, sides, width):
    for axis, dim in sides:
        count = lax.axis_size(axis)
        ends = count - 1
        head = lax.slice_in_dim(cells, 0, width, axis=dim)
        tail = lax.slice_in_dim(cells, cells.shape[dim] - width, cells.shape[dim], axis=dim)
        cells = jnp.concatenate(
            [
                lax.ppermute(tail, axis, [(i, (i + 1) % count) for i in range(ends)]),
                cells,
                lax.ppermute(head, axis, [((i + 1) % count, i) for i in range(ends)]),
            ],
            axis=dim,
        )
    return cells


def face_weights(coef):
    klat = coef[0]
    klon = coef[1]
    zero_row = jnp.zeros_like(klat[:1])
    north_face = 0.5 * (klat + jnp.concatenate([zero_row, klat[:-1]], axis=0))
    south_face = 0.5 * (klat + jnp.concatenate([klat[1:], zero_row], axis=0))
    east_face = 0.5 * (klon + jnp.roll(klon, -1, axis=1))
    west_face = 0.5 * (klon + jnp.roll(klon, 1, axis=1))
    return (north_face, south_face, east_face, west_face)


def diffuse_once(layer_field, face_list, valid_rows):
    north_face, south_face, east_face, west_face = face_list
    zero_row = jnp.zeros_like(layer_field[..., :1, :])
    above = jnp.concatenate([zero_row, layer_field[..., :-1, :]], axis=-2)
    below = jnp.concatenate([layer_field[..., 1:, :], zero_row], axis=-2)
    east_val = jnp.roll(layer_field, -1, axis=-1)
    west_val = jnp.roll(layer_field, 1, axis=-1)
    updated = layer_field + north_face * (above - layer_field) + south_face * (below - layer_field)
    updated = updated + east_face * (east_val - layer_field) + west_face * (west_val - layer_field)
    return updated * valid_rows


def rim_rows(all_faces):
    return tuple((face for face in all_faces))


def valid_mask(margin, band_rows):
    global_row = (
        lax.axis_index("lat") * band_rows
        + jnp.arange(band_rows + 2 * margin, dtype=jnp.int32)
        - margin
    )
    total_rows = band_rows * lax.axis_size("lat")
    inside = jnp.logical_and(global_row >= 0, global_row < total_rows)
    return inside.astype(jnp.float32)[:, None]


def diffuse_field(layer_field, all_faces, band_rows):
    face_list = rim_rows(all_faces)
    valid_rows = valid_mask(DIFF_STEPS, band_rows)
    extended = with_halo(layer_field, (("lat", 2),), DIFF_STEPS)
    for sweep in range(DIFF_STEPS):
        extended = diffuse_once(extended, face_list, valid_rows)
    return extended[..., DIFF_STEPS : DIFF_STEPS + band_rows, :]


def shards(perturb, alpha_init, innovation, obs_weight, coef, obs_mask):
    slot_count, var_count, members, levels, band_rows, lon_cells = perturb.shape
    owned_rows = innovation.shape[0]
    coef_ext = with_halo(coef, (("lat", 1),), DIFF_STEPS)
    all_faces = face_weights(coef_ext)
    tile_mask = jnp.repeat(jnp.repeat(obs_mask, TILE, axis=1), TILE, axis=2).astype(jnp.float32)
    first_row = lax.axis_index("mem") * owned_rows
    slot_of_row = (first_row + jnp.arange(owned_rows, dtype=jnp.int32)) // (var_count * levels)
    one_hot = (slot_of_row[:, None] == jnp.arange(slot_count, dtype=jnp.int32)[None, :]).astype(
        jnp.float32
    )
    row_mask = jnp.sum(one_hot[:, :, None, None] * tile_mask[None], axis=1)
    row_gain = obs_weight * row_mask
    alpha = alpha_init
    misfit = jnp.zeros_like(innovation)
    for sweep in range(ITERS):
        spread = diffuse_field(alpha, all_faces, band_rows)
        partial_sum = jnp.sum(perturb.astype(jnp.float32) * spread[None, None], axis=2)
        partial_sum = partial_sum.reshape(slot_count * var_count * levels, band_rows, lon_cells)
        increment = lax.psum_scatter(partial_sum, "mem", scatter_dimension=0, tiled=True)
        misfit = row_gain * (increment - innovation)
        gathered = lax.all_gather(misfit, "mem", axis=0, tiled=True)
        misfit_rows = gathered.reshape(slot_count, var_count, levels, band_rows, lon_cells)
        adjoint = jnp.sum(perturb.astype(jnp.float32) * misfit_rows[:, :, None], axis=(0, 1))
        alpha = alpha - 0.3 * (alpha + diffuse_field(adjoint, all_faces, band_rows))
    return (alpha, misfit)


LANES = 128
SUBLANES = 8
CHIPS = 8
CORES = 2
GROUP = CHIPS * CORES
EARLY = (1, 6, 2, 5)
LATE = (4, 3, 7)


def fold(cells):
    lead, (rows, cols) = cells.shape[:-2], cells.shape[-2:]
    parts = cells.reshape(*lead, rows, cols // LANES, LANES).swapaxes(-3, -2)
    return parts.reshape(*lead, rows * cols // LANES, LANES)


def fits(mesh, perturb, innovation):
    slot_count, var_count, members, levels, rows, lon_cells = perturb.shape
    mem, lat = mesh.shape["mem"], mesh.shape["lat"]
    if lat != 2 or mem != 2 * GROUP // lat:
        return False
    if rows != lat * TILE or DIFF_STEPS > TILE or TILE * lon_cells != SUBLANES * LANES:
        return False
    total = slot_count * var_count * levels
    if members % mem or levels % GROUP or total % mem or total // mem > levels:
        return False
    return held_fields(slot_count * var_count, levels) is not None


def held_fields(fields, levels):
    chunks = []
    for chunk in range(levels // GROUP):
        halves = ([], [])
        for field in range(fields):
            rows = [field * levels + chunk * GROUP + place for place in range(GROUP)]
            sides = {2 * row // (fields * levels) for row in rows}
            if len(sides) != 1:
                return None
            halves[sides.pop()].append(field)
        if not halves[0] or not halves[1]:
            return None
        longest = max(len(half) for half in halves)
        chunks.append([half + half[-1:] * (longest - len(half)) for half in halves])
    return chunks


def flat_offset(chip, core):
    return ((chip >> 1) << 2) | (core << 1) | (chip & 1)


def shift_by(mask, cells):
    axes = ("mem", "lat")
    count = lax.axis_size("mem") * lax.axis_size("lat")
    return lax.ppermute(cells, axes, [(i, i ^ mask) for i in range(count)])


class Sizes:
    def __init__(self, perturb, owned_rows):
        slots, variables, members, levels = perturb.shape[:4]
        self.slots = slots
        self.vars = variables
        self.fields = slots * variables
        self.members = members
        self.levels = levels
        self.owned = owned_rows
        self.chunks = levels // GROUP
        self.planes = self.fields * members
        self.rows = self.planes + members + 2
        self.all_rows = self.chunks * self.rows
        self.held = held_fields(self.fields, levels)
        self.sums = self.fields * 2


def row_in_block(size, level, mem_index):
    row = lax.rem(level + size.levels * size.owned - lax.rem(size.owned * mem_index, size.levels), size.levels)
    return row, row < size.owned, lax.div(size.owned * mem_index + row, size.levels)


def pack_target(size, outs, chip, core):
    if chip == 0:
        return outs[core]
    if chip in EARLY:
        return outs[2 + EARLY.index(chip)].at[core]
    place = LATE.index(chip)
    return outs[2 + len(EARLY) + place] if core == 0 else outs[-1].at[place]


def pack_kernel(size, flat_ref, perturb_hbm, alpha_hbm, innov_hbm, weight_hbm, mask_ref, near_ref, *refs):
    outs, scratch = refs[:-7], refs[-7:]
    perturb_ref, alpha_ref, innov_ref, weight_ref, tiles_ref, plane_sems, sems = scratch
    flat = flat_ref[0]
    own = lax.rem(flat, GROUP)
    mem_index = lax.div(flat, 2)
    step = size.fields
    plane_copies = [
        pltpu.make_async_copy(
            perturb_hbm.at[pl.ds(part * step, step)], perturb_ref.at[pl.ds(part * step, step)], plane_sems.at[part]
        )
        for part in range(size.members)
    ]
    copies = [
        pltpu.make_async_copy(source, target, sems.at[place])
        for place, (source, target) in enumerate(
            ((alpha_hbm, alpha_ref), (innov_hbm, innov_ref), (weight_hbm, weight_ref))
        )
    ]
    for copy in plane_copies + copies:
        copy.start()
    tiles = mask_ref.shape[-1]
    shape = (tiles, tiles * TILE)
    spread_out = lax.broadcasted_iota(jnp.int32, shape, 0) == lax.div(lax.broadcasted_iota(jnp.int32, shape, 1), TILE)
    line = lax.broadcasted_iota(jnp.int32, (SUBLANES, LANES), 0)
    for slot in range(size.slots):
        cells = jnp.dot(
            mask_ref[slot].astype(jnp.float32), spread_out.astype(jnp.float32), preferred_element_type=jnp.float32
        )
        tiles_ref[slot] = jnp.where(line < TILE, cells[:, :LANES], cells[:, LANES:])
    coef_out = outs[2 + EARLY.index(1)]
    coef_out[0, size.all_rows] = near_ref[0]
    coef_out[1, size.all_rows] = near_ref[1]
    places = [(chip, core, chunk) for chip in range(CHIPS) for core in range(CORES) for chunk in range(size.chunks)]

    def level_of(chip, core, chunk):
        return lax.bitwise_xor(own, flat_offset(chip, core)) + chunk * GROUP

    for part in range(size.members):
        plane_copies[part].wait()
        for chip, core, chunk in places:
            planes = perturb_ref[part * step : (part + 1) * step, level_of(chip, core, chunk)]
            base = chunk * size.rows + part * step
            pack_target(size, outs, chip, core)[base : base + step] = planes.astype(jnp.float32)
    for copy in copies:
        copy.wait()
    for chip, core, chunk in places:
        out = pack_target(size, outs, chip, core)
        level = level_of(chip, core, chunk)
        base = chunk * size.rows + size.planes
        out[base : base + size.members] = alpha_ref[:, level]
        row, inside, field = row_in_block(size, level, mem_index)
        row = jnp.minimum(row, size.owned - 1)
        slot = jnp.minimum(lax.div(field, size.vars), size.slots - 1)
        kept = jnp.where(inside, 1.0, 0.0).astype(jnp.float32)
        out[base + size.members] = innov_ref[row] * kept
        out[base + size.members + 1] = weight_ref[row] * tiles_ref[slot] * kept


class Pieces:
    def __init__(self, size, refs):
        self.size = size
        self.refs = refs
        self.far_ref = refs[2 + EARLY.index(1)]

    def at(self, chip, core):
        if chip == 0:
            return self.refs[core], ()
        if chip in EARLY:
            place = EARLY.index(chip)
            return (self.refs[2 + place], (0,)) if core == 0 else (self.refs[2 + len(EARLY)], (place,))
        return self.refs[3 + len(EARLY) + LATE.index(chip)], (core,)

    def block(self, chip, core, chunk, row):
        ref, lead = self.at(chip, core)
        return ref[lead + (chunk * self.size.rows + row,)]

    def alpha(self, chip, core, chunk):
        ref, lead = self.at(chip, core)
        base = chunk * self.size.rows + self.size.planes
        return ref[lead + (slice(base, base + self.size.members),)]

    def far(self):
        return [self.far_ref[part, self.size.all_rows] for part in range(2)]


def roll(cells, shift, axis):
    return pltpu.roll(cells, shift, axis=cells.ndim + axis)


def neighbours(own, other, edges):
    row0, row3, lane0, lane_last = edges
    turned = roll(own, SUBLANES // 2, -2)
    across = roll(other, SUBLANES // 2, -2)
    above = roll(jnp.where(row3, across, own), 1, -2)
    below = roll(jnp.where(row0, across, own), SUBLANES - 1, -2)
    east = roll(jnp.where(lane0, turned, own), LANES - 1, -1)
    west = roll(jnp.where(lane_last, turned, own), 1, -1)
    return above, below, east, west


def stencils(flat, near, far):
    shape = (SUBLANES, LANES)
    line = lax.rem(lax.broadcasted_iota(jnp.int32, shape, 0), TILE)
    lane = lax.broadcasted_iota(jnp.int32, shape, 1)
    edges = (line == 0, line == TILE - 1, lane == 0, lane == LANES - 1)
    band = lax.rem(flat, 2)
    weights = []
    for half, (own, other) in enumerate(((near, far), (far, near))):
        here = lax.bitwise_xor(band, half)
        open_top = jnp.where(jnp.logical_and(edges[0], here == 0), 0.0, 1.0).astype(jnp.float32)
        open_end = jnp.where(jnp.logical_and(edges[1], here == 1), 0.0, 1.0).astype(jnp.float32)
        above, below, _, _ = neighbours(own[0], other[0], edges)
        _, _, east, west = neighbours(own[1], other[1], edges)
        north = 0.5 * (own[0] + above * open_top)
        south = 0.5 * (own[0] + below * open_end)
        east = 0.5 * (own[1] + east)
        west = 0.5 * (own[1] + west)
        centre = 1.0 - north - south - east - west
        weights.append((centre, north * open_top, south * open_end, east, west))
    return edges, weights


def diffuse_pair(near, far, stencil):
    edges, weights = stencil
    for _ in range(DIFF_STEPS):
        pair = []
        for (own, other), (centre, north, south, east, west) in zip(((near, far), (far, near)), weights):
            above, below, right, left = neighbours(own, other, edges)
            pair.append(centre * own + north * above + south * below + east * right + west * left)
        near, far = pair
    return near, far


def add_products(size, pieces, chunk, pair, spread, sums):
    for half in range(2):
        for core in range(CORES):
            for field in range(size.fields):
                for member in range(size.members):
                    plane = pieces.block(2 * pair + half, core, chunk, field * size.members + member)
                    term = plane * spread[half][core * size.members + member]
                    known = sums[half][field]
                    sums[half][field] = term if known is None else known + term


def adjoint_of(size, pieces, chunk, pair, misfit):
    halves = []
    for half in range(2):
        found = []
        for core in range(CORES):
            for member in range(size.members):
                total = None
                for field in range(size.fields):
                    plane = pieces.block(2 * pair + half, core, chunk, field * size.members + member)
                    term = plane * misfit[half][field]
                    total = term if total is None else total + term
                found.append(total)
        halves.append(jnp.stack(found))
    return halves


def first_alpha(pieces, chunk, pair):
    return [
        jnp.concatenate([pieces.alpha(2 * pair + half, core, chunk) for core in range(CORES)]) for half in range(2)
    ]


def first_kernel(chunk, size, flat_ref, near_ref, *refs):
    pieces, (sum_ref, gain_ref, innov_ref) = Pieces(size, refs[:-3]), refs[-3:]
    flat = flat_ref[0]
    stencil = stencils(flat, [near_ref[0], near_ref[1]], pieces.far())
    mem_index = lax.div(flat, 2)
    side = lax.div(flat, GROUP)
    gain_ref[...] = jnp.zeros_like(gain_ref)
    innov_ref[...] = jnp.zeros_like(innov_ref)
    level = lax.rem(flat, GROUP) + chunk * GROUP
    for chip in range(0, CHIPS, 2):
        for core in range(CORES):
            source = lax.bitwise_xor(mem_index, (chip & 6) | core)
            _, inside, field = row_in_block(size, level, source)

            @pl.when(inside)
            def _(chip=chip, core=core, field=field):
                for half in range(2):
                    innov_ref[field, half] = pieces.block(chip + half, core, chunk, size.rows - 2)
                    gain_ref[field, half] = pieces.block(chip + half, core, chunk, size.rows - 1)

    for place, (first, second) in enumerate(zip(*size.held[chunk])):
        field = jnp.where(side == 0, first, second)
        sum_ref[pl.ds(size.sums + 2 * place, 2)] = gain_ref[field]
    sums = [[None] * size.fields for _ in range(2)]
    for pair in range(CHIPS // 2):
        spread = diffuse_pair(*first_alpha(pieces, chunk, pair), stencil)
        add_products(size, pieces, chunk, pair, spread, sums)
    for field in range(size.fields):
        for half in range(2):
            sum_ref[field * 2 + half] = sums[half][field] - innov_ref[field, half]


def misfit_of(size, gain_ref, mine_ref, theirs_ref):
    return [
        [
            gain_ref[field, half] * (mine_ref[field * 2 + half] + theirs_ref[field * 2 + half])
            for field in range(size.fields)
        ]
        for half in range(2)
    ]


def middle_kernel(chunk, size, flat_ref, near_ref, mine_ref, theirs_ref, held_ref, innov_ref, *refs):
    pieces, (sum_ref, gain_ref, alpha_ref) = Pieces(size, refs[:-3]), refs[-3:]
    flat = flat_ref[0]
    side = lax.div(flat, GROUP)
    stencil = stencils(flat, [near_ref[0], near_ref[1]], pieces.far())
    gain_ref[...] = held_ref[...]
    for place, (first, second) in enumerate(zip(*size.held[chunk])):
        field = jnp.where(side == 0, second, first)
        gain_ref[field] = theirs_ref[pl.ds(size.sums + 2 * place, 2)]
    misfit = misfit_of(size, gain_ref, mine_ref, theirs_ref)
    sums = [[None] * size.fields for _ in range(2)]
    for pair in range(CHIPS // 2):
        change = diffuse_pair(*adjoint_of(size, pieces, chunk, pair, misfit), stencil)
        before = first_alpha(pieces, chunk, pair)
        alpha = [old - 0.3 * (old + new) for old, new in zip(before, change)]
        for half in range(2):
            alpha_ref[pair, half] = alpha[half]
        add_products(size, pieces, chunk, pair, diffuse_pair(*alpha, stencil), sums)
    for field in range(size.fields):
        for half in range(2):
            sum_ref[field * 2 + half] = sums[half][field] - innov_ref[field, half]


def last_kernel(chunk, size, flat_ref, near_ref, mine_ref, theirs_ref, gain_ref, alpha_ref, *refs):
    refs, (out_ref, misfit_ref) = refs[:-2], refs[-2:]
    flat = flat_ref[0]
    own = lax.rem(flat, GROUP)
    mem_index = lax.div(flat, 2)
    base = chunk * (size.members + 1)
    if chunk:
        out_ref[:, :base] = refs[0][...]
        refs = refs[1:]
    pieces = Pieces(size, refs)
    stencil = stencils(flat, [near_ref[0], near_ref[1]], pieces.far())
    misfit = misfit_of(size, gain_ref, mine_ref, theirs_ref)
    for half in range(2):
        for field in range(size.fields):
            misfit_ref[half, field] = misfit[half][field]
    level = own + chunk * GROUP
    for pair in range(CHIPS // 2):
        change = diffuse_pair(*adjoint_of(size, pieces, chunk, pair, misfit), stencil)
        for half in range(2):
            old = alpha_ref[pair, half]
            alpha = old - 0.3 * (old + change[half])
            chip = 2 * pair + half
            for core in range(CORES):
                target = lax.bitwise_xor(own, flat_offset(chip, core))
                out_ref[target, base : base + size.members] = alpha[core * size.members : (core + 1) * size.members]
                _, _, field = row_in_block(size, level, lax.bitwise_xor(mem_index, (chip & 6) | core))
                out_ref[target, base + size.members] = misfit_ref[half, jnp.minimum(field, size.fields - 1)]


def unfold_into(out, at, block):
    rows = block.shape[-2] // 2
    out[at + (slice(None), slice(0, LANES))] = block[..., :rows, :]
    out[at + (slice(None), slice(LANES, 2 * LANES))] = block[..., rows:, :]


def place_kernel(size, flat_ref, back_ref, alpha_ref, misfit_ref):
    mem_index = lax.div(flat_ref[0], 2)
    for source in range(GROUP):
        for chunk in range(size.chunks):
            base = chunk * (size.members + 1)
            level = source + chunk * GROUP
            for member in range(size.members):
                unfold_into(alpha_ref, (member, level), back_ref[source, base + member])
            row, inside, _ = row_in_block(size, level, mem_index)

            @pl.when(inside)
            def _(source=source, base=base, row=row):
                unfold_into(misfit_ref, (row,), back_ref[source, base + size.members])


def call(kernel, outs, operands, scratch=(), spaces=None, limit=24):
    spaces = spaces or [pltpu.VMEM] * len(operands)
    moved = 4 * sum(math.prod(shape) for shape in outs) + sum(x.size * x.dtype.itemsize for x in operands)
    return pl.pallas_call(
        kernel,
        out_shape=[jax.ShapeDtypeStruct(shape, jnp.float32) for shape in outs],
        in_specs=[pl.BlockSpec(memory_space=space) for space in [pltpu.SMEM] + spaces[1:]],
        out_specs=[pl.BlockSpec(memory_space=pltpu.VMEM)] * len(outs),
        scratch_shapes=scratch,
        cost_estimate=pl.CostEstimate(flops=moved, bytes_accessed=moved, transcendentals=0),
        compiler_params=pltpu.CompilerParams(vmem_limit_bytes=limit * 1024 * 1024),
    )(*operands)


def spread_levels(size, flat, near, perturb, alpha_init, innovation, obs_weight, obs_mask):
    levels = size.levels
    block = (SUBLANES, LANES)
    one = (size.all_rows, *block)
    early_shapes = [(CORES, size.all_rows + (chip == 1), *block) for chip in EARLY]
    packed = call(
        functools.partial(pack_kernel, size),
        [one, one] + early_shapes + [one] * len(LATE) + [(len(LATE), *one)],
        (
            flat,
            fold(perturb).reshape(size.planes, levels, *block),
            fold(alpha_init),
            fold(innovation),
            fold(obs_weight),
            obs_mask,
            near,
        ),
        [
            pltpu.VMEM((size.planes, levels, *block), jnp.bfloat16),
            pltpu.VMEM((size.members, levels, *block), jnp.float32),
            pltpu.VMEM((size.owned, *block), jnp.float32),
            pltpu.VMEM((size.owned, *block), jnp.float32),
            pltpu.VMEM((size.slots, *block), jnp.float32),
            pltpu.SemaphoreType.DMA((size.members,)),
            pltpu.SemaphoreType.DMA((3,)),
        ],
        [pltpu.SMEM] + [pltpu.HBM] * 4 + [pltpu.VMEM] * 2,
    )
    kept, early, late, late_out = packed[:2], packed[2:6], packed[6:9], packed[9]
    crossed = shift_by(CORES, late_out)
    late = [jnp.stack([cells, crossed[place]]) for place, cells in enumerate(late)]
    own_crossed = shift_by(CORES, kept[1])
    got = [shift_by(flat_offset(chip, 0), cells) for chip, cells in zip(EARLY, early)]
    got[0], got[1], late[0], late[1] = lax.optimization_barrier((got[0], got[1], late[0], late[1]))
    got_late = [shift_by(flat_offset(chip, 0), cells) for chip, cells in zip(LATE[:2], late[:2])]
    got[2], got[3], late[2] = lax.optimization_barrier((got[2], got[3], late[2]))
    got_late.append(shift_by(flat_offset(LATE[2], 0), late[2]))
    early_crossed = shift_by(CORES, jnp.stack([cells[1, : size.all_rows] for cells in got]))
    return (kept[0], own_crossed, *got, early_crossed, *got_late)


def level_shards(perturb, alpha_init, innovation, obs_weight, coef, obs_mask):
    size = Sizes(perturb, innovation.shape[0])
    levels, rows, lon_cells = perturb.shape[3:]
    block = (SUBLANES, LANES)
    flat = (lax.axis_index("mem") * lax.axis_size("lat") + lax.axis_index("lat")).astype(jnp.int32).reshape(1)
    near = fold(coef)
    pieces = spread_levels(size, flat, near, perturb, alpha_init, innovation, obs_weight, obs_mask)
    common = (flat, near)
    per_field = (size.fields, 2, *block)
    alpha_shape = (CHIPS // 2, 2, CORES * size.members, *block)
    chunks = range(size.chunks)
    first, second, back = [], [], None
    for chunk in chunks:
        sent = size.sums + 2 * len(size.held[chunk][0])
        mine, held, innov = call(
            functools.partial(first_kernel, chunk, size),
            [(sent, *block), per_field, per_field],
            common + pieces,
        )
        first.append((mine, shift_by(GROUP, mine), held, innov))
    for chunk in chunks:
        mine, gain, alpha = call(
            functools.partial(middle_kernel, chunk, size),
            [(size.sums, *block), per_field, alpha_shape],
            common + first[chunk] + pieces,
        )
        second.append((mine, shift_by(GROUP, mine), gain, alpha))
    for chunk in chunks:
        (back,) = call(
            functools.partial(last_kernel, chunk, size),
            [(GROUP, (chunk + 1) * (size.members + 1), *block)],
            common + second[chunk] + (() if back is None else (back,)) + pieces,
            [pltpu.VMEM((2, size.fields, *block), jnp.float32)],
        )
    groups = [[half * GROUP + place for place in range(GROUP)] for half in range(2)]
    back = lax.all_to_all(back, ("mem", "lat"), 0, 0, axis_index_groups=groups, tiled=True)
    return tuple(
        call(
            functools.partial(place_kernel, size),
            [(size.members, levels, rows, lon_cells), (size.owned, rows, lon_cells)],
            (flat, back),
        )
    )


def solution(mesh):
    in_specs = (
        P(None, None, "mem", None, "lat", None),
        P("mem", None, "lat", None),
        P("mem", "lat", None),
        P("mem", "lat", None),
        P(None, "lat", None),
        P(None, "lat", None),
    )
    out_specs = (P("mem", None, "lat", None), P("mem", "lat", None))

    def run(*args):
        body = level_shards if fits(mesh, args[0], args[2]) else shards
        return jax.shard_map(body, mesh=mesh, in_specs=in_specs, out_specs=out_specs, check_vma=False)(*args)

    return run
```

```python
import functools
import math

import jax
import jax.numpy as jnp
from jax import lax
from jax.experimental import pallas as pl
from jax.experimental.pallas import tpu as pltpu
from jax.sharding import PartitionSpec as P

ITERS = 2
DIFF_STEPS = 4
TILE = 4


def with_halo(cells, sides, width):
    for axis, dim in sides:
        count = lax.axis_size(axis)
        ends = count - 1
        head = lax.slice_in_dim(cells, 0, width, axis=dim)
        tail = lax.slice_in_dim(cells, cells.shape[dim] - width, cells.shape[dim], axis=dim)
        cells = jnp.concatenate(
            [
                lax.ppermute(tail, axis, [(i, (i + 1) % count) for i in range(ends)]),
                cells,
                lax.ppermute(head, axis, [((i + 1) % count, i) for i in range(ends)]),
            ],
            axis=dim,
        )
    return cells


def face_weights(coef):
    klat = coef[0]
    klon = coef[1]
    zero_row = jnp.zeros_like(klat[:1])
    north_face = 0.5 * (klat + jnp.concatenate([zero_row, klat[:-1]], axis=0))
    south_face = 0.5 * (klat + jnp.concatenate([klat[1:], zero_row], axis=0))
    east_face = 0.5 * (klon + jnp.roll(klon, -1, axis=1))
    west_face = 0.5 * (klon + jnp.roll(klon, 1, axis=1))
    return (north_face, south_face, east_face, west_face)


def diffuse_once(layer_field, face_list, valid_rows):
    north_face, south_face, east_face, west_face = face_list
    zero_row = jnp.zeros_like(layer_field[..., :1, :])
    above = jnp.concatenate([zero_row, layer_field[..., :-1, :]], axis=-2)
    below = jnp.concatenate([layer_field[..., 1:, :], zero_row], axis=-2)
    east_val = jnp.roll(layer_field, -1, axis=-1)
    west_val = jnp.roll(layer_field, 1, axis=-1)
    updated = layer_field + north_face * (above - layer_field) + south_face * (below - layer_field)
    updated = updated + east_face * (east_val - layer_field) + west_face * (west_val - layer_field)
    return updated * valid_rows


def rim_rows(all_faces):
    return tuple((face for face in all_faces))


def valid_mask(margin, band_rows):
    global_row = (
        lax.axis_index("lat") * band_rows
        + jnp.arange(band_rows + 2 * margin, dtype=jnp.int32)
        - margin
    )
    total_rows = band_rows * lax.axis_size("lat")
    inside = jnp.logical_and(global_row >= 0, global_row < total_rows)
    return inside.astype(jnp.float32)[:, None]


def diffuse_field(layer_field, all_faces, band_rows):
    face_list = rim_rows(all_faces)
    valid_rows = valid_mask(DIFF_STEPS, band_rows)
    extended = with_halo(layer_field, (("lat", 2),), DIFF_STEPS)
    for sweep in range(DIFF_STEPS):
        extended = diffuse_once(extended, face_list, valid_rows)
    return extended[..., DIFF_STEPS : DIFF_STEPS + band_rows, :]


def shards(perturb, alpha_init, innovation, obs_weight, coef, obs_mask):
    slot_count, var_count, members, levels, band_rows, lon_cells = perturb.shape
    owned_rows = innovation.shape[0]
    coef_ext = with_halo(coef, (("lat", 1),), DIFF_STEPS)
    all_faces = face_weights(coef_ext)
    tile_mask = jnp.repeat(jnp.repeat(obs_mask, TILE, axis=1), TILE, axis=2).astype(jnp.float32)
    first_row = lax.axis_index("mem") * owned_rows
    slot_of_row = (first_row + jnp.arange(owned_rows, dtype=jnp.int32)) // (var_count * levels)
    one_hot = (slot_of_row[:, None] == jnp.arange(slot_count, dtype=jnp.int32)[None, :]).astype(
        jnp.float32
    )
    row_mask = jnp.sum(one_hot[:, :, None, None] * tile_mask[None], axis=1)
    row_gain = obs_weight * row_mask
    alpha = alpha_init
    misfit = jnp.zeros_like(innovation)
    for sweep in range(ITERS):
        spread = diffuse_field(alpha, all_faces, band_rows)
        partial_sum = jnp.sum(perturb.astype(jnp.float32) * spread[None, None], axis=2)
        partial_sum = partial_sum.reshape(slot_count * var_count * levels, band_rows, lon_cells)
        increment = lax.psum_scatter(partial_sum, "mem", scatter_dimension=0, tiled=True)
        misfit = row_gain * (increment - innovation)
        gathered = lax.all_gather(misfit, "mem", axis=0, tiled=True)
        misfit_rows = gathered.reshape(slot_count, var_count, levels, band_rows, lon_cells)
        adjoint = jnp.sum(perturb.astype(jnp.float32) * misfit_rows[:, :, None], axis=(0, 1))
        alpha = alpha - 0.3 * (alpha + diffuse_field(adjoint, all_faces, band_rows))
    return (alpha, misfit)


LANES = 128
SUBLANES = 8
CHIPS = 8
CORES = 2
GROUP = CHIPS * CORES
EARLY = (1, 6, 2, 5)
LATE = (4, 3, 7)


def fold(cells):
    lead, (rows, cols) = cells.shape[:-2], cells.shape[-2:]
    parts = cells.reshape(*lead, rows, cols // LANES, LANES).swapaxes(-3, -2)
    return parts.reshape(*lead, rows * cols // LANES, LANES)


def fits(mesh, perturb, innovation):
    slot_count, var_count, members, levels, rows, lon_cells = perturb.shape
    mem, lat = mesh.shape["mem"], mesh.shape["lat"]
    if lat != 2 or mem != 2 * GROUP // lat:
        return False
    if rows != lat * TILE or DIFF_STEPS > TILE or TILE * lon_cells != SUBLANES * LANES:
        return False
    total = slot_count * var_count * levels
    if members % mem or levels % GROUP or total % mem or total // mem > levels:
        return False
    return held_fields(slot_count * var_count, levels) is not None


def held_fields(fields, levels):
    chunks = []
    for chunk in range(levels // GROUP):
        halves = ([], [])
        for field in range(fields):
            rows = [field * levels + chunk * GROUP + place for place in range(GROUP)]
            sides = {2 * row // (fields * levels) for row in rows}
            if len(sides) != 1:
                return None
            halves[sides.pop()].append(field)
        if not halves[0] or not halves[1]:
            return None
        longest = max(len(half) for half in halves)
        chunks.append([half + half[-1:] * (longest - len(half)) for half in halves])
    return chunks


def flat_offset(chip, core):
    return ((chip >> 1) << 2) | (core << 1) | (chip & 1)


def shift_by(mask, cells):
    axes = ("mem", "lat")
    count = lax.axis_size("mem") * lax.axis_size("lat")
    return lax.ppermute(cells, axes, [(i, i ^ mask) for i in range(count)])


class Sizes:
    def __init__(self, perturb, owned_rows):
        slots, variables, members, levels = perturb.shape[:4]
        self.slots = slots
        self.vars = variables
        self.fields = slots * variables
        self.members = members
        self.levels = levels
        self.owned = owned_rows
        self.chunks = levels // GROUP
        self.planes = self.fields * members
        self.extras = members + 2
        self.lead_rows = self.planes + self.chunks * self.extras
        self.all_rows = self.lead_rows + (self.chunks - 1) * self.planes
        self.held = held_fields(self.fields, levels)
        self.sums = self.fields * 2
        self.sent_gains = 2 * sum(len(half[0]) for half in self.held)

    def planes_at(self, chunk):
        return self.lead_rows + (chunk - 1) * self.planes if chunk else 0

    def extras_at(self, chunk):
        return self.planes + chunk * self.extras


def row_in_block(size, level, mem_index):
    row = lax.rem(level + size.levels * size.owned - lax.rem(size.owned * mem_index, size.levels), size.levels)
    return row, row < size.owned, lax.div(size.owned * mem_index + row, size.levels)


def pack_target(size, outs, chip, core):
    if chip == 0:
        return outs[core]
    if chip in EARLY:
        return outs[2 + EARLY.index(chip)].at[core]
    place = LATE.index(chip)
    return outs[2 + len(EARLY) + place] if core == 0 else outs[-1].at[place]


def pack_kernel(size, flat_ref, perturb_hbm, alpha_hbm, innov_hbm, weight_hbm, mask_hbm, near_hbm, *refs):
    outs, scratch = refs[:-9], refs[-9:]
    perturb_ref, alpha_ref, innov_ref, weight_ref, mask_ref, near_ref, tiles_ref, plane_sems, sems = scratch
    flat = flat_ref[0]
    own = lax.rem(flat, GROUP)
    mem_index = lax.div(flat, 2)
    step = size.fields
    plane_copies = [
        pltpu.make_async_copy(
            perturb_hbm.at[pl.ds(part * step, step)], perturb_ref.at[pl.ds(part * step, step)], plane_sems.at[part]
        )
        for part in range(size.members)
    ]
    copies = [
        pltpu.make_async_copy(source, target, sems.at[place])
        for place, (source, target) in enumerate(
            (
                (mask_hbm, mask_ref),
                (near_hbm, near_ref),
                (alpha_hbm, alpha_ref),
                (innov_hbm, innov_ref),
                (weight_hbm, weight_ref),
            )
        )
    ]
    for copy in plane_copies + copies:
        copy.start()
    copies[0].wait()
    copies[1].wait()
    tiles = mask_ref.shape[-1]
    shape = (tiles, tiles * TILE)
    spread_out = lax.broadcasted_iota(jnp.int32, shape, 0) == lax.div(lax.broadcasted_iota(jnp.int32, shape, 1), TILE)
    line = lax.broadcasted_iota(jnp.int32, (SUBLANES, LANES), 0)
    for slot in range(size.slots):
        cells = jnp.dot(
            mask_ref[slot].astype(jnp.float32), spread_out.astype(jnp.float32), preferred_element_type=jnp.float32
        )
        tiles_ref[slot] = jnp.where(line < TILE, cells[:, :LANES], cells[:, LANES:])
    coef_out = outs[2 + EARLY.index(1)]
    coef_out[0, size.all_rows] = near_ref[0]
    coef_out[1, size.all_rows] = near_ref[1]
    places = [(chip, core, chunk) for chip in range(CHIPS) for core in range(CORES) for chunk in range(size.chunks)]

    def level_of(chip, core, chunk):
        return lax.bitwise_xor(own, flat_offset(chip, core)) + chunk * GROUP

    for part in range(size.members):
        plane_copies[part].wait()
        for chip, core, chunk in places:
            planes = perturb_ref[part * step : (part + 1) * step, level_of(chip, core, chunk)]
            base = size.planes_at(chunk) + part * step
            pack_target(size, outs, chip, core)[base : base + step] = planes.astype(jnp.float32)
    for copy in copies[2:]:
        copy.wait()
    for chip, core, chunk in places:
        out = pack_target(size, outs, chip, core)
        level = level_of(chip, core, chunk)
        base = size.extras_at(chunk)
        out[base : base + size.members] = alpha_ref[:, level]
        row, inside, field = row_in_block(size, level, mem_index)
        row = jnp.minimum(row, size.owned - 1)
        slot = jnp.minimum(lax.div(field, size.vars), size.slots - 1)
        kept = jnp.where(inside, 1.0, 0.0).astype(jnp.float32)
        out[base + size.members] = innov_ref[row] * kept
        out[base + size.members + 1] = weight_ref[row] * tiles_ref[slot] * kept


class Pieces:
    def __init__(self, size, chunk, refs):
        self.size = size
        self.chunk = chunk
        self.refs = refs
        self.far_ref = refs[2 + EARLY.index(1)]

    def place(self, chip, core):
        if chip == 0:
            return self.refs[core], (), True
        if chip in EARLY:
            place = EARLY.index(chip)
            if core == 0:
                return self.refs[2 + place], (0,), True
            return self.refs[2 + len(EARLY)], (place,), True
        return self.refs[3 + len(EARLY) + LATE.index(chip)], (core,), False

    def plane(self, chip, core, row):
        ref, lead, whole = self.place(chip, core)
        if not whole and self.chunk:
            ref = self.refs[3 + len(EARLY) + len(LATE) + LATE.index(chip)]
        base = self.size.planes_at(self.chunk) if whole else 0
        return ref[lead + (base + row,)]

    def extra(self, chip, core, chunk, row):
        ref, lead, _ = self.place(chip, core)
        return ref[lead + (self.size.extras_at(chunk) + row,)]

    def alpha(self, chip, core):
        ref, lead, _ = self.place(chip, core)
        base = self.size.extras_at(self.chunk)
        return ref[lead + (slice(base, base + self.size.members),)]

    def far(self):
        return [self.far_ref[part, self.size.all_rows] for part in range(2)]


def roll(cells, shift, axis):
    return pltpu.roll(cells, shift, axis=cells.ndim + axis)


def neighbours(own, other, edges):
    row0, row3, lane0, lane_last = edges
    turned = roll(own, SUBLANES // 2, -2)
    across = roll(other, SUBLANES // 2, -2)
    above = roll(jnp.where(row3, across, own), 1, -2)
    below = roll(jnp.where(row0, across, own), SUBLANES - 1, -2)
    east = roll(jnp.where(lane0, turned, own), LANES - 1, -1)
    west = roll(jnp.where(lane_last, turned, own), 1, -1)
    return above, below, east, west


def stencils(flat, near, far):
    shape = (SUBLANES, LANES)
    line = lax.rem(lax.broadcasted_iota(jnp.int32, shape, 0), TILE)
    lane = lax.broadcasted_iota(jnp.int32, shape, 1)
    edges = (line == 0, line == TILE - 1, lane == 0, lane == LANES - 1)
    band = lax.rem(flat, 2)
    weights = []
    for half, (own, other) in enumerate(((near, far), (far, near))):
        here = lax.bitwise_xor(band, half)
        open_top = jnp.where(jnp.logical_and(edges[0], here == 0), 0.0, 1.0).astype(jnp.float32)
        open_end = jnp.where(jnp.logical_and(edges[1], here == 1), 0.0, 1.0).astype(jnp.float32)
        above, below, _, _ = neighbours(own[0], other[0], edges)
        _, _, east, west = neighbours(own[1], other[1], edges)
        north = 0.5 * (own[0] + above * open_top)
        south = 0.5 * (own[0] + below * open_end)
        east = 0.5 * (own[1] + east)
        west = 0.5 * (own[1] + west)
        centre = 1.0 - north - south - east - west
        weights.append((centre, north * open_top, south * open_end, east, west))
    return edges, weights


def diffuse_pair(near, far, stencil):
    edges, weights = stencil
    for _ in range(DIFF_STEPS):
        pair = []
        for (own, other), (centre, north, south, east, west) in zip(((near, far), (far, near)), weights):
            above, below, right, left = neighbours(own, other, edges)
            pair.append(centre * own + north * above + south * below + east * right + west * left)
        near, far = pair
    return near, far


def add_products(size, pieces, pair, spread, sums):
    for half in range(2):
        for core in range(CORES):
            for field in range(size.fields):
                for member in range(size.members):
                    plane = pieces.plane(2 * pair + half, core, field * size.members + member)
                    term = plane * spread[half][core * size.members + member]
                    known = sums[half][field]
                    sums[half][field] = term if known is None else known + term


def adjoint_of(size, pieces, pair, misfit):
    halves = []
    for half in range(2):
        found = []
        for core in range(CORES):
            for member in range(size.members):
                total = None
                for field in range(size.fields):
                    plane = pieces.plane(2 * pair + half, core, field * size.members + member)
                    term = plane * misfit[half][field]
                    total = term if total is None else total + term
                found.append(total)
        halves.append(jnp.stack(found))
    return halves


def first_alpha(pieces, pair):
    return [
        jnp.concatenate([pieces.alpha(2 * pair + half, core) for core in range(CORES)]) for half in range(2)
    ]


def gather_slots(size, pieces, mem_index, own, gain_ref, innov_ref):
    gain_ref[...] = jnp.zeros_like(gain_ref)
    innov_ref[...] = jnp.zeros_like(innov_ref)
    for chunk in range(size.chunks):
        for chip in range(0, CHIPS, 2):
            for core in range(CORES):
                source = lax.bitwise_xor(mem_index, (chip & 6) | core)
                _, inside, field = row_in_block(size, own + chunk * GROUP, source)

                @pl.when(inside)
                def _(chip=chip, core=core, chunk=chunk, field=field):
                    for half in range(2):
                        innov_ref[chunk, field, half] = pieces.extra(chip + half, core, chunk, size.members)
                        gain_ref[chunk, field, half] = pieces.extra(chip + half, core, chunk, size.members + 1)


def gain_places(size):
    row, found = size.sums, []
    for chunk, halves in enumerate(size.held):
        for first, second in zip(*halves):
            found.append((row, chunk, first, second))
            row += 2
    return found


def first_kernel(chunk, size, flat_ref, near_ref, *refs):
    if chunk:
        innov_ref, sum_ref = refs[0], refs[-1]
        pieces = Pieces(size, chunk, refs[1:-1])
    else:
        sum_ref, gain_ref, innov_ref = refs[-3:]
        pieces = Pieces(size, chunk, refs[:-3])
    flat = flat_ref[0]
    stencil = stencils(flat, [near_ref[0], near_ref[1]], pieces.far())
    if not chunk:
        side = lax.div(flat, GROUP)
        gather_slots(size, pieces, lax.div(flat, 2), lax.rem(flat, GROUP), gain_ref, innov_ref)
        for row, part, first, second in gain_places(size):
            sum_ref[pl.ds(row, 2)] = gain_ref[part, jnp.where(side == 0, first, second)]
    sums = [[None] * size.fields for _ in range(2)]
    for pair in range(CHIPS // 2):
        spread = diffuse_pair(*first_alpha(pieces, pair), stencil)
        add_products(size, pieces, pair, spread, sums)
    for field in range(size.fields):
        for half in range(2):
            sum_ref[field * 2 + half] = sums[half][field] - innov_ref[chunk, field, half]


def misfit_of(size, chunk, gain_ref, mine_ref, theirs_ref):
    return [
        [
            gain_ref[chunk, field, half] * (mine_ref[field * 2 + half] + theirs_ref[field * 2 + half])
            for field in range(size.fields)
        ]
        for half in range(2)
    ]


def middle_kernel(chunk, size, flat_ref, near_ref, mine_ref, theirs_ref, gain_in_ref, innov_ref, *refs):
    if chunk:
        gain_ref, (sum_ref, alpha_ref) = gain_in_ref, refs[-2:]
        pieces = Pieces(size, chunk, refs[:-2])
    else:
        sum_ref, alpha_ref, gain_ref = refs[-3:]
        pieces = Pieces(size, chunk, refs[:-3])
    flat = flat_ref[0]
    stencil = stencils(flat, [near_ref[0], near_ref[1]], pieces.far())
    if not chunk:
        side = lax.div(flat, GROUP)
        gain_ref[...] = gain_in_ref[...]
        for row, part, first, second in gain_places(size):
            gain_ref[part, jnp.where(side == 0, second, first)] = theirs_ref[pl.ds(row, 2)]
    misfit = misfit_of(size, chunk, gain_ref, mine_ref, theirs_ref)
    sums = [[None] * size.fields for _ in range(2)]
    for pair in range(CHIPS // 2):
        change = diffuse_pair(*adjoint_of(size, pieces, pair, misfit), stencil)
        before = first_alpha(pieces, pair)
        alpha = [old - 0.3 * (old + new) for old, new in zip(before, change)]
        for half in range(2):
            alpha_ref[pair, half] = alpha[half]
        add_products(size, pieces, pair, diffuse_pair(*alpha, stencil), sums)
    for field in range(size.fields):
        for half in range(2):
            sum_ref[field * 2 + half] = sums[half][field] - innov_ref[chunk, field, half]


def last_kernel(chunk, size, flat_ref, near_ref, mine_ref, theirs_ref, gain_ref, alpha_ref, *refs):
    refs, (out_ref, misfit_ref) = refs[:-2], refs[-2:]
    flat = flat_ref[0]
    own = lax.rem(flat, GROUP)
    mem_index = lax.div(flat, 2)
    base = chunk * (size.members + 1)
    if chunk:
        out_ref[:, :base] = refs[0][...]
        refs = refs[1:]
    pieces = Pieces(size, chunk, refs)
    stencil = stencils(flat, [near_ref[0], near_ref[1]], pieces.far())
    misfit = misfit_of(size, chunk, gain_ref, mine_ref, theirs_ref)
    for half in range(2):
        for field in range(size.fields):
            misfit_ref[half, field] = misfit[half][field]
    level = own + chunk * GROUP
    for pair in range(CHIPS // 2):
        change = diffuse_pair(*adjoint_of(size, pieces, pair, misfit), stencil)
        for half in range(2):
            old = alpha_ref[pair, half]
            alpha = old - 0.3 * (old + change[half])
            chip = 2 * pair + half
            for core in range(CORES):
                target = lax.bitwise_xor(own, flat_offset(chip, core))
                out_ref[target, base : base + size.members] = alpha[core * size.members : (core + 1) * size.members]
                _, _, field = row_in_block(size, level, lax.bitwise_xor(mem_index, (chip & 6) | core))
                out_ref[target, base + size.members] = misfit_ref[half, jnp.minimum(field, size.fields - 1)]


def unfold_into(out, at, block):
    rows = block.shape[-2] // 2
    out[at + (slice(None), slice(0, LANES))] = block[..., :rows, :]
    out[at + (slice(None), slice(LANES, 2 * LANES))] = block[..., rows:, :]


def place_kernel(size, flat_ref, back_ref, alpha_ref, misfit_ref):
    mem_index = lax.div(flat_ref[0], 2)
    for source in range(GROUP):
        for chunk in range(size.chunks):
            base = chunk * (size.members + 1)
            level = source + chunk * GROUP
            for member in range(size.members):
                unfold_into(alpha_ref, (member, level), back_ref[source, base + member])
            row, inside, _ = row_in_block(size, level, mem_index)

            @pl.when(inside)
            def _(source=source, base=base, row=row):
                unfold_into(misfit_ref, (row,), back_ref[source, base + size.members])


def call(kernel, outs, operands, scratch=(), spaces=None, limit=24):
    spaces = spaces or [pltpu.VMEM] * len(operands)
    moved = 4 * sum(math.prod(shape) for shape in outs) + sum(x.size * x.dtype.itemsize for x in operands)
    return pl.pallas_call(
        kernel,
        out_shape=[jax.ShapeDtypeStruct(shape, jnp.float32) for shape in outs],
        in_specs=[pl.BlockSpec(memory_space=space) for space in [pltpu.SMEM] + spaces[1:]],
        out_specs=[pl.BlockSpec(memory_space=pltpu.VMEM)] * len(outs),
        scratch_shapes=scratch,
        cost_estimate=pl.CostEstimate(flops=moved, bytes_accessed=moved, transcendentals=0),
        compiler_params=pltpu.CompilerParams(vmem_limit_bytes=limit * 1024 * 1024),
    )(*[in_hbm(x) if space is pltpu.HBM else x for x, space in zip(operands, spaces)])


def in_hbm(cells):
    return pltpu.with_memory_space_constraint(cells, pltpu.HBM)


def spread_levels(size, flat, near, perturb, alpha_init, innovation, obs_weight, obs_mask):
    levels = size.levels
    block = (SUBLANES, LANES)
    one = (size.all_rows, *block)
    early_shapes = [(CORES, size.all_rows + (chip == 1), *block) for chip in EARLY]
    packed = call(
        functools.partial(pack_kernel, size),
        [one, one] + early_shapes + [one] * len(LATE) + [(len(LATE), *one)],
        (
            flat,
            fold(perturb).reshape(size.planes, levels, *block),
            fold(alpha_init),
            fold(innovation),
            fold(obs_weight),
            obs_mask,
            near,
        ),
        [
            pltpu.VMEM((size.planes, levels, *block), jnp.bfloat16),
            pltpu.VMEM((size.members, levels, *block), jnp.float32),
            pltpu.VMEM((size.owned, *block), jnp.float32),
            pltpu.VMEM((size.owned, *block), jnp.float32),
            pltpu.VMEM(obs_mask.shape, jnp.int32),
            pltpu.VMEM(near.shape, jnp.float32),
            pltpu.VMEM((size.slots, *block), jnp.float32),
            pltpu.SemaphoreType.DMA((size.members,)),
            pltpu.SemaphoreType.DMA((5,)),
        ],
        [pltpu.SMEM] + [pltpu.HBM] * 6,
    )
    kept, early, late, late_out = packed[:2], packed[2:6], packed[6:9], packed[9]
    crossed = shift_by(CORES, late_out)
    own_crossed = shift_by(CORES, kept[1])
    got = [shift_by(flat_offset(chip, 0), cells) for chip, cells in zip(EARLY, early)]
    got_late = []
    for chunk in range(size.chunks):
        base = size.planes_at(chunk)
        rows = slice(base, base + (size.planes if chunk else size.lead_rows))
        parts = [jnp.stack([cells[rows], crossed[place, rows]]) for place, cells in enumerate(late)]
        if chunk == 0:
            got[0], got[1], parts[0], parts[1] = lax.optimization_barrier((got[0], got[1], parts[0], parts[1]))
            got[2], got[3], parts[2] = lax.optimization_barrier((got[2], got[3], parts[2]))
        else:
            got[0], got[1], got[2], got[3], *parts = lax.optimization_barrier((*got, *parts))
        got_late.append(tuple(shift_by(flat_offset(chip, 0), cells) for chip, cells in zip(LATE, parts)))
    early_crossed = shift_by(CORES, jnp.stack([cells[1, : size.all_rows] for cells in got]))
    shared = (kept[0], own_crossed, *got, early_crossed)
    return [shared + got_late[0] + (got_late[chunk] if chunk else ()) for chunk in range(size.chunks)]


def level_shards(perturb, alpha_init, innovation, obs_weight, coef, obs_mask):
    size = Sizes(perturb, innovation.shape[0])
    levels, rows, lon_cells = perturb.shape[3:]
    block = (SUBLANES, LANES)
    flat = (lax.axis_index("mem") * lax.axis_size("lat") + lax.axis_index("lat")).astype(jnp.int32).reshape(1)
    near = fold(coef)
    pieces = spread_levels(size, flat, near, perturb, alpha_init, innovation, obs_weight, obs_mask)
    common = (flat, near)
    all_fields = (size.chunks, size.fields, 2, *block)
    alpha_shape = (CHIPS // 2, 2, CORES * size.members, *block)
    chunks = range(size.chunks)
    first, second, back, held, innov, gain = [], [], None, None, None, None
    for chunk in chunks:
        kernel = functools.partial(first_kernel, chunk, size)
        if chunk:
            (mine,) = call(kernel, [(size.sums, *block)], common + (innov,) + pieces[chunk])
        else:
            shapes = [(size.sums + size.sent_gains, *block), all_fields, all_fields]
            mine, held, innov = call(kernel, shapes, common + pieces[chunk])
        first.append((mine, shift_by(GROUP, mine)))
    for chunk in chunks:
        kernel = functools.partial(middle_kernel, chunk, size)
        shapes = [(size.sums, *block), alpha_shape] + ([] if chunk else [all_fields])
        operands = common + first[chunk] + (gain if chunk else held, innov) + pieces[chunk]
        mine, alpha, *rest = call(kernel, shapes, operands)
        gain = gain if chunk else rest[0]
        second.append((mine, shift_by(GROUP, mine), gain, alpha))
    for chunk in chunks:
        (back,) = call(
            functools.partial(last_kernel, chunk, size),
            [(GROUP, (chunk + 1) * (size.members + 1), *block)],
            common + second[chunk] + (() if back is None else (back,)) + pieces[chunk],
            [pltpu.VMEM((2, size.fields, *block), jnp.float32)],
        )
    groups = [[half * GROUP + place for place in range(GROUP)] for half in range(2)]
    back = lax.all_to_all(back, ("mem", "lat"), 0, 0, axis_index_groups=groups, tiled=True)
    return tuple(
        call(
            functools.partial(place_kernel, size),
            [(size.members, levels, rows, lon_cells), (size.owned, rows, lon_cells)],
            (flat, back),
        )
    )


def solution(mesh):
    in_specs = (
        P(None, None, "mem", None, "lat", None),
        P("mem", None, "lat", None),
        P("mem", "lat", None),
        P("mem", "lat", None),
        P(None, "lat", None),
        P(None, "lat", None),
    )
    out_specs = (P("mem", None, "lat", None), P("mem", "lat", None))

    def run(*args):
        body = level_shards if fits(mesh, args[0], args[2]) else shards
        return jax.shard_map(body, mesh=mesh, in_specs=in_specs, out_specs=out_specs, check_vma=False)(*args)

    return run
```

```python
import functools
import math

import jax
import jax.numpy as jnp
from jax import lax
from jax.experimental import pallas as pl
from jax.experimental.pallas import tpu as pltpu
from jax.sharding import PartitionSpec as P

ITERS = 2
DIFF_STEPS = 4
TILE = 4


def with_halo(cells, sides, width):
    for axis, dim in sides:
        count = lax.axis_size(axis)
        ends = count - 1
        head = lax.slice_in_dim(cells, 0, width, axis=dim)
        tail = lax.slice_in_dim(cells, cells.shape[dim] - width, cells.shape[dim], axis=dim)
        cells = jnp.concatenate(
            [
                lax.ppermute(tail, axis, [(i, (i + 1) % count) for i in range(ends)]),
                cells,
                lax.ppermute(head, axis, [((i + 1) % count, i) for i in range(ends)]),
            ],
            axis=dim,
        )
    return cells


def face_weights(coef):
    klat = coef[0]
    klon = coef[1]
    zero_row = jnp.zeros_like(klat[:1])
    north_face = 0.5 * (klat + jnp.concatenate([zero_row, klat[:-1]], axis=0))
    south_face = 0.5 * (klat + jnp.concatenate([klat[1:], zero_row], axis=0))
    east_face = 0.5 * (klon + jnp.roll(klon, -1, axis=1))
    west_face = 0.5 * (klon + jnp.roll(klon, 1, axis=1))
    return (north_face, south_face, east_face, west_face)


def diffuse_once(layer_field, face_list, valid_rows):
    north_face, south_face, east_face, west_face = face_list
    zero_row = jnp.zeros_like(layer_field[..., :1, :])
    above = jnp.concatenate([zero_row, layer_field[..., :-1, :]], axis=-2)
    below = jnp.concatenate([layer_field[..., 1:, :], zero_row], axis=-2)
    east_val = jnp.roll(layer_field, -1, axis=-1)
    west_val = jnp.roll(layer_field, 1, axis=-1)
    updated = layer_field + north_face * (above - layer_field) + south_face * (below - layer_field)
    updated = updated + east_face * (east_val - layer_field) + west_face * (west_val - layer_field)
    return updated * valid_rows


def rim_rows(all_faces):
    return tuple((face for face in all_faces))


def valid_mask(margin, band_rows):
    global_row = (
        lax.axis_index("lat") * band_rows
        + jnp.arange(band_rows + 2 * margin, dtype=jnp.int32)
        - margin
    )
    total_rows = band_rows * lax.axis_size("lat")
    inside = jnp.logical_and(global_row >= 0, global_row < total_rows)
    return inside.astype(jnp.float32)[:, None]


def diffuse_field(layer_field, all_faces, band_rows):
    face_list = rim_rows(all_faces)
    valid_rows = valid_mask(DIFF_STEPS, band_rows)
    extended = with_halo(layer_field, (("lat", 2),), DIFF_STEPS)
    for sweep in range(DIFF_STEPS):
        extended = diffuse_once(extended, face_list, valid_rows)
    return extended[..., DIFF_STEPS : DIFF_STEPS + band_rows, :]


def shards(perturb, alpha_init, innovation, obs_weight, coef, obs_mask):
    slot_count, var_count, members, levels, band_rows, lon_cells = perturb.shape
    owned_rows = innovation.shape[0]
    coef_ext = with_halo(coef, (("lat", 1),), DIFF_STEPS)
    all_faces = face_weights(coef_ext)
    tile_mask = jnp.repeat(jnp.repeat(obs_mask, TILE, axis=1), TILE, axis=2).astype(jnp.float32)
    first_row = lax.axis_index("mem") * owned_rows
    slot_of_row = (first_row + jnp.arange(owned_rows, dtype=jnp.int32)) // (var_count * levels)
    one_hot = (slot_of_row[:, None] == jnp.arange(slot_count, dtype=jnp.int32)[None, :]).astype(
        jnp.float32
    )
    row_mask = jnp.sum(one_hot[:, :, None, None] * tile_mask[None], axis=1)
    row_gain = obs_weight * row_mask
    alpha = alpha_init
    misfit = jnp.zeros_like(innovation)
    for sweep in range(ITERS):
        spread = diffuse_field(alpha, all_faces, band_rows)
        partial_sum = jnp.sum(perturb.astype(jnp.float32) * spread[None, None], axis=2)
        partial_sum = partial_sum.reshape(slot_count * var_count * levels, band_rows, lon_cells)
        increment = lax.psum_scatter(partial_sum, "mem", scatter_dimension=0, tiled=True)
        misfit = row_gain * (increment - innovation)
        gathered = lax.all_gather(misfit, "mem", axis=0, tiled=True)
        misfit_rows = gathered.reshape(slot_count, var_count, levels, band_rows, lon_cells)
        adjoint = jnp.sum(perturb.astype(jnp.float32) * misfit_rows[:, :, None], axis=(0, 1))
        alpha = alpha - 0.3 * (alpha + diffuse_field(adjoint, all_faces, band_rows))
    return (alpha, misfit)


LANES = 128
SUBLANES = 8
CHIPS = 8
CORES = 2
GROUP = CHIPS * CORES
EARLY = (1, 6, 2, 5)
LATE = (4, 3, 7)


def fold(cells):
    lead, (rows, cols) = cells.shape[:-2], cells.shape[-2:]
    parts = cells.reshape(*lead, rows, cols // LANES, LANES).swapaxes(-3, -2)
    return parts.reshape(*lead, rows * cols // LANES, LANES)


def fits(mesh, perturb, innovation):
    slot_count, var_count, members, levels, rows, lon_cells = perturb.shape
    mem, lat = mesh.shape["mem"], mesh.shape["lat"]
    if lat != 2 or mem != 2 * GROUP // lat:
        return False
    if rows != lat * TILE or DIFF_STEPS > TILE or TILE * lon_cells != SUBLANES * LANES:
        return False
    total = slot_count * var_count * levels
    if members % mem or levels % GROUP or total % mem or total // mem > levels:
        return False
    return held_fields(slot_count * var_count, levels) is not None


def held_fields(fields, levels):
    chunks = []
    for chunk in range(levels // GROUP):
        halves = ([], [])
        for field in range(fields):
            rows = [field * levels + chunk * GROUP + place for place in range(GROUP)]
            sides = {2 * row // (fields * levels) for row in rows}
            if len(sides) != 1:
                return None
            halves[sides.pop()].append(field)
        if not halves[0] or not halves[1]:
            return None
        longest = max(len(half) for half in halves)
        chunks.append([half + half[-1:] * (longest - len(half)) for half in halves])
    return chunks


def flat_offset(chip, core):
    return ((chip >> 1) << 2) | (core << 1) | (chip & 1)


def shift_by(mask, cells):
    axes = ("mem", "lat")
    count = lax.axis_size("mem") * lax.axis_size("lat")
    return lax.ppermute(cells, axes, [(i, i ^ mask) for i in range(count)])


class Sizes:
    def __init__(self, perturb, owned_rows):
        slots, variables, members, levels = perturb.shape[:4]
        self.slots = slots
        self.vars = variables
        self.fields = slots * variables
        self.members = members
        self.levels = levels
        self.owned = owned_rows
        self.chunks = levels // GROUP
        self.planes = self.fields * members
        self.extras = members + 2
        self.lead_rows = self.planes + self.chunks * self.extras
        self.all_rows = self.lead_rows + (self.chunks - 1) * self.planes
        self.held = held_fields(self.fields, levels)
        self.sums = self.fields * 2
        self.sent_gains = 2 * sum(len(half[0]) for half in self.held)

    def planes_at(self, chunk):
        return self.lead_rows + (chunk - 1) * self.planes if chunk else 0

    def extras_at(self, chunk):
        return self.planes + chunk * self.extras


def row_in_block(size, level, mem_index):
    row = lax.rem(level + size.levels * size.owned - lax.rem(size.owned * mem_index, size.levels), size.levels)
    return row, row < size.owned, lax.div(size.owned * mem_index + row, size.levels)


def pack_shapes(size, chips):
    one = (size.all_rows, SUBLANES, LANES)
    shapes = []
    for chip in chips:
        if chip == 0:
            shapes += [one, one]
        elif chip in EARLY:
            shapes.append((CORES, size.all_rows + (chip == 1), SUBLANES, LANES))
        else:
            shapes.append(one)
    return shapes + [(len(LATE), *one)] * (LATE[0] in chips)


def pack_target(outs, chips, chip, core):
    place = chips.index(chip) + (0 in chips[: chips.index(chip)])
    if chip == 0:
        return outs[place + core]
    if chip in EARLY:
        return outs[place].at[core]
    return outs[place] if core == 0 else outs[-1].at[LATE.index(chip)]


def pack_kernel(size, chips, flat_ref, perturb_hbm, alpha_hbm, innov_hbm, weight_hbm, mask_hbm, near_hbm, *refs):
    outs, scratch = refs[:-10], refs[-10:]
    perturb_ref, alpha_ref, innov_ref, weight_ref, mask_ref, near_ref, tiles_ref, plane_sems, alpha_sems, sems = scratch
    flat = flat_ref[0]
    own = lax.rem(flat, GROUP)
    mem_index = lax.div(flat, 2)
    places = [(chip, core, chunk) for chip in chips for core in range(CORES) for chunk in range(size.chunks)]
    levels = [lax.bitwise_xor(own, flat_offset(chip, core)) + chunk * GROUP for chip, core, chunk in places]
    plane_copies = [
        pltpu.make_async_copy(perturb_hbm.at[:, level], perturb_ref.at[place], plane_sems.at[place])
        for place, level in enumerate(levels)
    ]
    alpha_copies = [
        pltpu.make_async_copy(alpha_hbm.at[:, level], alpha_ref.at[place], alpha_sems.at[place])
        for place, level in enumerate(levels)
    ]
    pairs = ((mask_hbm, mask_ref), (near_hbm, near_ref), (innov_hbm, innov_ref), (weight_hbm, weight_ref))
    copies = [pltpu.make_async_copy(source, target, sems.at[place]) for place, (source, target) in enumerate(pairs)]
    for copy in plane_copies + copies + alpha_copies:
        copy.start()
    copies[0].wait()
    tiles = mask_ref.shape[-1]
    shape = (tiles, tiles * TILE)
    spread_out = lax.broadcasted_iota(jnp.int32, shape, 0) == lax.div(lax.broadcasted_iota(jnp.int32, shape, 1), TILE)
    line = lax.broadcasted_iota(jnp.int32, (SUBLANES, LANES), 0)
    for slot in range(size.slots):
        cells = jnp.dot(
            mask_ref[slot].astype(jnp.float32), spread_out.astype(jnp.float32), preferred_element_type=jnp.float32
        )
        tiles_ref[slot] = jnp.where(line < TILE, cells[:, :LANES], cells[:, LANES:])
    copies[1].wait()
    if 1 in chips:
        coef_out = outs[chips.index(1)]
        coef_out[0, size.all_rows] = near_ref[0]
        coef_out[1, size.all_rows] = near_ref[1]
    for place, (chip, core, chunk) in enumerate(places):
        plane_copies[place].wait()
        base = size.planes_at(chunk)
        pack_target(outs, chips, chip, core)[base : base + size.planes] = perturb_ref[place].astype(jnp.float32)
    copies[2].wait()
    copies[3].wait()
    for place, (chip, core, chunk) in enumerate(places):
        out = pack_target(outs, chips, chip, core)
        base = size.extras_at(chunk)
        alpha_copies[place].wait()
        out[base : base + size.members] = alpha_ref[place]
        row, inside, field = row_in_block(size, levels[place], mem_index)
        row = jnp.minimum(row, size.owned - 1)
        slot = jnp.minimum(lax.div(field, size.vars), size.slots - 1)
        kept = jnp.where(inside, 1.0, 0.0).astype(jnp.float32)
        out[base + size.members] = innov_ref[row] * kept
        out[base + size.members + 1] = weight_ref[row] * tiles_ref[slot] * kept


class Pieces:
    def __init__(self, size, chunk, refs):
        self.size = size
        self.chunk = chunk
        self.refs = refs
        self.far_ref = refs[2 + EARLY.index(1)]

    def place(self, chip, core):
        if chip == 0:
            return self.refs[core], (), True
        if chip in EARLY:
            place = EARLY.index(chip)
            if core == 0:
                return self.refs[2 + place], (0,), True
            return self.refs[2 + len(EARLY)], (place,), True
        return self.refs[3 + len(EARLY) + LATE.index(chip)], (core,), False

    def plane(self, chip, core, row):
        ref, lead, whole = self.place(chip, core)
        if not whole and self.chunk:
            ref = self.refs[3 + len(EARLY) + len(LATE) + LATE.index(chip)]
        base = self.size.planes_at(self.chunk) if whole else 0
        return ref[lead + (base + row,)]

    def extra(self, chip, core, chunk, row):
        ref, lead, _ = self.place(chip, core)
        return ref[lead + (self.size.extras_at(chunk) + row,)]

    def alpha(self, chip, core):
        ref, lead, _ = self.place(chip, core)
        base = self.size.extras_at(self.chunk)
        return ref[lead + (slice(base, base + self.size.members),)]

    def far(self):
        return [self.far_ref[part, self.size.all_rows] for part in range(2)]


def roll(cells, shift, axis):
    return pltpu.roll(cells, shift, axis=cells.ndim + axis)


def neighbours(own, other, edges):
    row0, row3, lane0, lane_last = edges
    turned = roll(own, SUBLANES // 2, -2)
    across = roll(other, SUBLANES // 2, -2)
    above = roll(jnp.where(row3, across, own), 1, -2)
    below = roll(jnp.where(row0, across, own), SUBLANES - 1, -2)
    east = roll(jnp.where(lane0, turned, own), LANES - 1, -1)
    west = roll(jnp.where(lane_last, turned, own), 1, -1)
    return above, below, east, west


def stencils(flat, near, far):
    shape = (SUBLANES, LANES)
    line = lax.rem(lax.broadcasted_iota(jnp.int32, shape, 0), TILE)
    lane = lax.broadcasted_iota(jnp.int32, shape, 1)
    edges = (line == 0, line == TILE - 1, lane == 0, lane == LANES - 1)
    band = lax.rem(flat, 2)
    weights = []
    for half, (own, other) in enumerate(((near, far), (far, near))):
        here = lax.bitwise_xor(band, half)
        open_top = jnp.where(jnp.logical_and(edges[0], here == 0), 0.0, 1.0).astype(jnp.float32)
        open_end = jnp.where(jnp.logical_and(edges[1], here == 1), 0.0, 1.0).astype(jnp.float32)
        above, below, _, _ = neighbours(own[0], other[0], edges)
        _, _, east, west = neighbours(own[1], other[1], edges)
        north = 0.5 * (own[0] + above * open_top)
        south = 0.5 * (own[0] + below * open_end)
        east = 0.5 * (own[1] + east)
        west = 0.5 * (own[1] + west)
        centre = 1.0 - north - south - east - west
        weights.append((centre, north * open_top, south * open_end, east, west))
    return edges, weights


def diffuse_pair(near, far, stencil):
    edges, weights = stencil
    for _ in range(DIFF_STEPS):
        pair = []
        for (own, other), (centre, north, south, east, west) in zip(((near, far), (far, near)), weights):
            above, below, right, left = neighbours(own, other, edges)
            pair.append(centre * own + north * above + south * below + east * right + west * left)
        near, far = pair
    return near, far


def add_products(size, pieces, pair, spread, sums):
    for half in range(2):
        for core in range(CORES):
            for field in range(size.fields):
                for member in range(size.members):
                    plane = pieces.plane(2 * pair + half, core, field * size.members + member)
                    term = plane * spread[half][core * size.members + member]
                    known = sums[half][field]
                    sums[half][field] = term if known is None else known + term


def adjoint_of(size, pieces, pair, misfit):
    halves = []
    for half in range(2):
        found = []
        for core in range(CORES):
            for member in range(size.members):
                total = None
                for field in range(size.fields):
                    plane = pieces.plane(2 * pair + half, core, field * size.members + member)
                    term = plane * misfit[half][field]
                    total = term if total is None else total + term
                found.append(total)
        halves.append(jnp.stack(found))
    return halves


def first_alpha(pieces, pair):
    return [
        jnp.concatenate([pieces.alpha(2 * pair + half, core) for core in range(CORES)]) for half in range(2)
    ]


def gather_slots(size, pieces, mem_index, own, gain_ref, innov_ref):
    gain_ref[...] = jnp.zeros_like(gain_ref)
    innov_ref[...] = jnp.zeros_like(innov_ref)
    for chunk in range(size.chunks):
        for chip in range(0, CHIPS, 2):
            for core in range(CORES):
                source = lax.bitwise_xor(mem_index, (chip & 6) | core)
                _, inside, field = row_in_block(size, own + chunk * GROUP, source)

                @pl.when(inside)
                def _(chip=chip, core=core, chunk=chunk, field=field):
                    for half in range(2):
                        innov_ref[chunk, field, half] = pieces.extra(chip + half, core, chunk, size.members)
                        gain_ref[chunk, field, half] = pieces.extra(chip + half, core, chunk, size.members + 1)


def gain_places(size):
    row, found = size.sums, []
    for chunk, halves in enumerate(size.held):
        for first, second in zip(*halves):
            found.append((row, chunk, first, second))
            row += 2
    return found


def first_kernel(chunk, size, flat_ref, near_ref, *refs):
    if chunk:
        innov_ref, sum_ref = refs[0], refs[-1]
        pieces = Pieces(size, chunk, refs[1:-1])
    else:
        sum_ref, gain_ref, innov_ref = refs[-3:]
        pieces = Pieces(size, chunk, refs[:-3])
    flat = flat_ref[0]
    stencil = stencils(flat, [near_ref[0], near_ref[1]], pieces.far())
    if not chunk:
        side = lax.div(flat, GROUP)
        gather_slots(size, pieces, lax.div(flat, 2), lax.rem(flat, GROUP), gain_ref, innov_ref)
        for row, part, first, second in gain_places(size):
            sum_ref[pl.ds(row, 2)] = gain_ref[part, jnp.where(side == 0, first, second)]
    sums = [[None] * size.fields for _ in range(2)]
    for pair in range(CHIPS // 2):
        spread = diffuse_pair(*first_alpha(pieces, pair), stencil)
        add_products(size, pieces, pair, spread, sums)
    for field in range(size.fields):
        for half in range(2):
            sum_ref[field * 2 + half] = sums[half][field] - innov_ref[chunk, field, half]


def misfit_of(size, chunk, gain_ref, mine_ref, theirs_ref):
    return [
        [
            gain_ref[chunk, field, half] * (mine_ref[field * 2 + half] + theirs_ref[field * 2 + half])
            for field in range(size.fields)
        ]
        for half in range(2)
    ]


def middle_kernel(chunk, size, flat_ref, near_ref, mine_ref, theirs_ref, gain_in_ref, innov_ref, *refs):
    if chunk:
        gain_ref, (sum_ref, alpha_ref) = gain_in_ref, refs[-2:]
        pieces = Pieces(size, chunk, refs[:-2])
    else:
        sum_ref, alpha_ref, gain_ref = refs[-3:]
        pieces = Pieces(size, chunk, refs[:-3])
    flat = flat_ref[0]
    stencil = stencils(flat, [near_ref[0], near_ref[1]], pieces.far())
    if not chunk:
        side = lax.div(flat, GROUP)
        gain_ref[...] = gain_in_ref[...]
        for row, part, first, second in gain_places(size):
            gain_ref[part, jnp.where(side == 0, second, first)] = theirs_ref[pl.ds(row, 2)]
    misfit = misfit_of(size, chunk, gain_ref, mine_ref, theirs_ref)
    sums = [[None] * size.fields for _ in range(2)]
    for pair in range(CHIPS // 2):
        change = diffuse_pair(*adjoint_of(size, pieces, pair, misfit), stencil)
        before = first_alpha(pieces, pair)
        alpha = [old - 0.3 * (old + new) for old, new in zip(before, change)]
        for half in range(2):
            alpha_ref[pair, half] = alpha[half]
        add_products(size, pieces, pair, diffuse_pair(*alpha, stencil), sums)
    for field in range(size.fields):
        for half in range(2):
            sum_ref[field * 2 + half] = sums[half][field] - innov_ref[chunk, field, half]


def last_kernel(chunk, size, flat_ref, near_ref, mine_ref, theirs_ref, gain_ref, alpha_ref, *refs):
    refs, (out_ref, misfit_ref) = refs[:-2], refs[-2:]
    flat = flat_ref[0]
    own = lax.rem(flat, GROUP)
    mem_index = lax.div(flat, 2)
    base = chunk * (size.members + 1)
    if chunk:
        out_ref[:, :base] = refs[0][...]
        refs = refs[1:]
    pieces = Pieces(size, chunk, refs)
    stencil = stencils(flat, [near_ref[0], near_ref[1]], pieces.far())
    misfit = misfit_of(size, chunk, gain_ref, mine_ref, theirs_ref)
    for half in range(2):
        for field in range(size.fields):
            misfit_ref[half, field] = misfit[half][field]
    level = own + chunk * GROUP
    for pair in range(CHIPS // 2):
        change = diffuse_pair(*adjoint_of(size, pieces, pair, misfit), stencil)
        for half in range(2):
            old = alpha_ref[pair, half]
            alpha = old - 0.3 * (old + change[half])
            chip = 2 * pair + half
            for core in range(CORES):
                target = lax.bitwise_xor(own, flat_offset(chip, core))
                out_ref[target, base : base + size.members] = alpha[core * size.members : (core + 1) * size.members]
                _, _, field = row_in_block(size, level, lax.bitwise_xor(mem_index, (chip & 6) | core))
                out_ref[target, base + size.members] = misfit_ref[half, jnp.minimum(field, size.fields - 1)]


def unfold_into(out, at, block):
    rows = block.shape[-2] // 2
    out[at + (slice(None), slice(0, LANES))] = block[..., :rows, :]
    out[at + (slice(None), slice(LANES, 2 * LANES))] = block[..., rows:, :]


def place_kernel(size, flat_ref, back_ref, alpha_ref, misfit_ref):
    mem_index = lax.div(flat_ref[0], 2)
    for source in range(GROUP):
        for chunk in range(size.chunks):
            base = chunk * (size.members + 1)
            level = source + chunk * GROUP
            for member in range(size.members):
                unfold_into(alpha_ref, (member, level), back_ref[source, base + member])
            row, inside, _ = row_in_block(size, level, mem_index)

            @pl.when(inside)
            def _(source=source, base=base, row=row):
                unfold_into(misfit_ref, (row,), back_ref[source, base + size.members])


def call(kernel, outs, operands, scratch=(), spaces=None, limit=24):
    spaces = spaces or [pltpu.VMEM] * len(operands)
    moved = 4 * sum(math.prod(shape) for shape in outs) + sum(x.size * x.dtype.itemsize for x in operands)
    return pl.pallas_call(
        kernel,
        out_shape=[jax.ShapeDtypeStruct(shape, jnp.float32) for shape in outs],
        in_specs=[pl.BlockSpec(memory_space=space) for space in [pltpu.SMEM] + spaces[1:]],
        out_specs=[pl.BlockSpec(memory_space=pltpu.VMEM)] * len(outs),
        scratch_shapes=scratch,
        cost_estimate=pl.CostEstimate(flops=moved, bytes_accessed=moved, transcendentals=0),
        compiler_params=pltpu.CompilerParams(vmem_limit_bytes=limit * 1024 * 1024),
    )(*[in_hbm(x) if space is pltpu.HBM else x for x, space in zip(operands, spaces)])


def in_hbm(cells):
    return pltpu.with_memory_space_constraint(cells, pltpu.HBM)


def spread_levels(size, flat, near, perturb, alpha_init, innovation, obs_weight, obs_mask):
    block = (SUBLANES, LANES)
    operands = (
        fold(perturb).reshape(size.planes, size.levels, *block),
        fold(alpha_init),
        fold(innovation),
        fold(obs_weight),
        obs_mask,
        near,
    )

    def pack(chips, flat):
        count = len(chips) * CORES * size.chunks
        return call(
            functools.partial(pack_kernel, size, chips),
            pack_shapes(size, chips),
            (flat,) + operands,
            [
                pltpu.VMEM((count, size.planes, *block), jnp.bfloat16),
                pltpu.VMEM((count, size.members, *block), jnp.float32),
                pltpu.VMEM((size.owned, *block), jnp.float32),
                pltpu.VMEM((size.owned, *block), jnp.float32),
                pltpu.VMEM(obs_mask.shape, jnp.int32),
                pltpu.VMEM(near.shape, jnp.float32),
                pltpu.VMEM((size.slots, *block), jnp.float32),
                pltpu.SemaphoreType.DMA((count,)),
                pltpu.SemaphoreType.DMA((count,)),
                pltpu.SemaphoreType.DMA((4,)),
            ],
            [pltpu.SMEM] + [pltpu.HBM] * 6,
        )

    early = list(pack(EARLY[:2], flat))
    flat, early[0], early[1] = lax.optimization_barrier((flat, early[0], early[1]))
    packed = pack(EARLY[2:] + (0,) + LATE, flat)
    early += packed[:2]
    kept, late, late_out = packed[2:4], packed[4:7], packed[7]
    crossed = shift_by(CORES, late_out)
    own_crossed = shift_by(CORES, kept[1])
    got = [shift_by(flat_offset(chip, 0), cells) for chip, cells in zip(EARLY, early)]
    got_late = []
    for chunk in range(size.chunks):
        base = size.planes_at(chunk)
        rows = slice(base, base + (size.planes if chunk else size.lead_rows))
        parts = [jnp.stack([cells[rows], crossed[place, rows]]) for place, cells in enumerate(late)]
        if chunk == 0:
            got[1], parts[0] = lax.optimization_barrier((got[1], parts[0]))
            got[2], parts[1] = lax.optimization_barrier((got[2], parts[1]))
            got[0], got[3], parts[2] = lax.optimization_barrier((got[0], got[3], parts[2]))
        else:
            prev = list(got_late[chunk - 1])
            prev[0], parts[0] = lax.optimization_barrier((prev[0], parts[0]))
            prev[1], parts[1] = lax.optimization_barrier((prev[1], parts[1]))
            prev[2], parts[2] = lax.optimization_barrier((prev[2], parts[2]))
            got_late[chunk - 1] = tuple(prev)
        got_late.append(tuple(shift_by(flat_offset(chip, 0), cells) for chip, cells in zip(LATE, parts)))
    early_crossed = shift_by(CORES, jnp.stack([cells[1, : size.all_rows] for cells in got]))
    shared = (kept[0], own_crossed, *got, early_crossed)
    return [shared + got_late[0] + (got_late[chunk] if chunk else ()) for chunk in range(size.chunks)]


def level_shards(perturb, alpha_init, innovation, obs_weight, coef, obs_mask):
    size = Sizes(perturb, innovation.shape[0])
    levels, rows, lon_cells = perturb.shape[3:]
    block = (SUBLANES, LANES)
    flat = (lax.axis_index("mem") * lax.axis_size("lat") + lax.axis_index("lat")).astype(jnp.int32).reshape(1)
    near = fold(coef)
    pieces = spread_levels(size, flat, near, perturb, alpha_init, innovation, obs_weight, obs_mask)
    common = (flat, near)
    all_fields = (size.chunks, size.fields, 2, *block)
    alpha_shape = (CHIPS // 2, 2, CORES * size.members, *block)
    chunks = range(size.chunks)
    first, second, back, held, innov, gain = [], [], None, None, None, None
    for chunk in chunks:
        kernel = functools.partial(first_kernel, chunk, size)
        if chunk:
            (mine,) = call(kernel, [(size.sums, *block)], common + (innov,) + pieces[chunk])
        else:
            shapes = [(size.sums + size.sent_gains, *block), all_fields, all_fields]
            mine, held, innov = call(kernel, shapes, common + pieces[chunk])
        first.append((mine, shift_by(GROUP, mine)))
    for chunk in chunks:
        kernel = functools.partial(middle_kernel, chunk, size)
        shapes = [(size.sums, *block), alpha_shape] + ([] if chunk else [all_fields])
        operands = common + first[chunk] + (gain if chunk else held, innov) + pieces[chunk]
        mine, alpha, *rest = call(kernel, shapes, operands)
        gain = gain if chunk else rest[0]
        second.append((mine, shift_by(GROUP, mine), gain, alpha))
    for chunk in chunks:
        (back,) = call(
            functools.partial(last_kernel, chunk, size),
            [(GROUP, (chunk + 1) * (size.members + 1), *block)],
            common + second[chunk] + (() if back is None else (back,)) + pieces[chunk],
            [pltpu.VMEM((2, size.fields, *block), jnp.float32)],
        )
    groups = [[half * GROUP + place for place in range(GROUP)] for half in range(2)]
    back = lax.all_to_all(back, ("mem", "lat"), 0, 0, axis_index_groups=groups, tiled=True)
    return tuple(
        call(
            functools.partial(place_kernel, size),
            [(size.members, levels, rows, lon_cells), (size.owned, rows, lon_cells)],
            (flat, back),
        )
    )


def solution(mesh):
    in_specs = (
        P(None, None, "mem", None, "lat", None),
        P("mem", None, "lat", None),
        P("mem", "lat", None),
        P("mem", "lat", None),
        P(None, "lat", None),
        P(None, "lat", None),
    )
    out_specs = (P("mem", None, "lat", None), P("mem", "lat", None))

    def run(*args):
        body = level_shards if fits(mesh, args[0], args[2]) else shards
        return jax.shard_map(body, mesh=mesh, in_specs=in_specs, out_specs=out_specs, check_vma=False)(*args)

    return run
```

```python
import functools
import math

import jax
import jax.numpy as jnp
from jax import lax
from jax.experimental import pallas as pl
from jax.experimental.pallas import tpu as pltpu
from jax.sharding import PartitionSpec as P

ITERS = 2
DIFF_STEPS = 4
TILE = 4


def with_halo(cells, sides, width):
    for axis, dim in sides:
        count = lax.axis_size(axis)
        ends = count - 1
        head = lax.slice_in_dim(cells, 0, width, axis=dim)
        tail = lax.slice_in_dim(cells, cells.shape[dim] - width, cells.shape[dim], axis=dim)
        cells = jnp.concatenate(
            [
                lax.ppermute(tail, axis, [(i, (i + 1) % count) for i in range(ends)]),
                cells,
                lax.ppermute(head, axis, [((i + 1) % count, i) for i in range(ends)]),
            ],
            axis=dim,
        )
    return cells


def face_weights(coef):
    klat = coef[0]
    klon = coef[1]
    zero_row = jnp.zeros_like(klat[:1])
    north_face = 0.5 * (klat + jnp.concatenate([zero_row, klat[:-1]], axis=0))
    south_face = 0.5 * (klat + jnp.concatenate([klat[1:], zero_row], axis=0))
    east_face = 0.5 * (klon + jnp.roll(klon, -1, axis=1))
    west_face = 0.5 * (klon + jnp.roll(klon, 1, axis=1))
    return (north_face, south_face, east_face, west_face)


def diffuse_once(layer_field, face_list, valid_rows):
    north_face, south_face, east_face, west_face = face_list
    zero_row = jnp.zeros_like(layer_field[..., :1, :])
    above = jnp.concatenate([zero_row, layer_field[..., :-1, :]], axis=-2)
    below = jnp.concatenate([layer_field[..., 1:, :], zero_row], axis=-2)
    east_val = jnp.roll(layer_field, -1, axis=-1)
    west_val = jnp.roll(layer_field, 1, axis=-1)
    updated = layer_field + north_face * (above - layer_field) + south_face * (below - layer_field)
    updated = updated + east_face * (east_val - layer_field) + west_face * (west_val - layer_field)
    return updated * valid_rows


def rim_rows(all_faces):
    return tuple((face for face in all_faces))


def valid_mask(margin, band_rows):
    global_row = (
        lax.axis_index("lat") * band_rows
        + jnp.arange(band_rows + 2 * margin, dtype=jnp.int32)
        - margin
    )
    total_rows = band_rows * lax.axis_size("lat")
    inside = jnp.logical_and(global_row >= 0, global_row < total_rows)
    return inside.astype(jnp.float32)[:, None]


def diffuse_field(layer_field, all_faces, band_rows):
    face_list = rim_rows(all_faces)
    valid_rows = valid_mask(DIFF_STEPS, band_rows)
    extended = with_halo(layer_field, (("lat", 2),), DIFF_STEPS)
    for sweep in range(DIFF_STEPS):
        extended = diffuse_once(extended, face_list, valid_rows)
    return extended[..., DIFF_STEPS : DIFF_STEPS + band_rows, :]


def shards(perturb, alpha_init, innovation, obs_weight, coef, obs_mask):
    slot_count, var_count, members, levels, band_rows, lon_cells = perturb.shape
    owned_rows = innovation.shape[0]
    coef_ext = with_halo(coef, (("lat", 1),), DIFF_STEPS)
    all_faces = face_weights(coef_ext)
    tile_mask = jnp.repeat(jnp.repeat(obs_mask, TILE, axis=1), TILE, axis=2).astype(jnp.float32)
    first_row = lax.axis_index("mem") * owned_rows
    slot_of_row = (first_row + jnp.arange(owned_rows, dtype=jnp.int32)) // (var_count * levels)
    one_hot = (slot_of_row[:, None] == jnp.arange(slot_count, dtype=jnp.int32)[None, :]).astype(
        jnp.float32
    )
    row_mask = jnp.sum(one_hot[:, :, None, None] * tile_mask[None], axis=1)
    row_gain = obs_weight * row_mask
    alpha = alpha_init
    misfit = jnp.zeros_like(innovation)
    for sweep in range(ITERS):
        spread = diffuse_field(alpha, all_faces, band_rows)
        partial_sum = jnp.sum(perturb.astype(jnp.float32) * spread[None, None], axis=2)
        partial_sum = partial_sum.reshape(slot_count * var_count * levels, band_rows, lon_cells)
        increment = lax.psum_scatter(partial_sum, "mem", scatter_dimension=0, tiled=True)
        misfit = row_gain * (increment - innovation)
        gathered = lax.all_gather(misfit, "mem", axis=0, tiled=True)
        misfit_rows = gathered.reshape(slot_count, var_count, levels, band_rows, lon_cells)
        adjoint = jnp.sum(perturb.astype(jnp.float32) * misfit_rows[:, :, None], axis=(0, 1))
        alpha = alpha - 0.3 * (alpha + diffuse_field(adjoint, all_faces, band_rows))
    return (alpha, misfit)


LANES = 128
SUBLANES = 8
CHIPS = 8
CORES = 2
GROUP = CHIPS * CORES
EARLY = (1, 6, 2, 5)
LATE = (4, 3, 7)


def fold(cells):
    lead, (rows, cols) = cells.shape[:-2], cells.shape[-2:]
    parts = cells.reshape(*lead, rows, cols // LANES, LANES).swapaxes(-3, -2)
    return parts.reshape(*lead, rows * cols // LANES, LANES)


def fits(mesh, perturb, innovation):
    slot_count, var_count, members, levels, rows, lon_cells = perturb.shape
    mem, lat = mesh.shape["mem"], mesh.shape["lat"]
    if lat != 2 or mem != 2 * GROUP // lat:
        return False
    if rows != lat * TILE or DIFF_STEPS > TILE or TILE * lon_cells != SUBLANES * LANES:
        return False
    total = slot_count * var_count * levels
    if members % mem or levels % GROUP or total % mem or total // mem > levels:
        return False
    return held_fields(slot_count * var_count, levels) is not None


def held_fields(fields, levels):
    chunks = []
    for chunk in range(levels // GROUP):
        halves = ([], [])
        for field in range(fields):
            rows = [field * levels + chunk * GROUP + place for place in range(GROUP)]
            sides = {2 * row // (fields * levels) for row in rows}
            if len(sides) != 1:
                return None
            halves[sides.pop()].append(field)
        if not halves[0] or not halves[1]:
            return None
        longest = max(len(half) for half in halves)
        chunks.append([half + half[-1:] * (longest - len(half)) for half in halves])
    return chunks


def flat_offset(chip, core):
    return ((chip >> 1) << 2) | (core << 1) | (chip & 1)


def shift_by(mask, cells):
    axes = ("mem", "lat")
    count = lax.axis_size("mem") * lax.axis_size("lat")
    return lax.ppermute(cells, axes, [(i, i ^ mask) for i in range(count)])


class Sizes:
    def __init__(self, perturb, owned_rows):
        slots, variables, members, levels = perturb.shape[:4]
        self.slots = slots
        self.vars = variables
        self.fields = slots * variables
        self.members = members
        self.levels = levels
        self.owned = owned_rows
        self.chunks = levels // GROUP
        self.planes = self.fields * members
        self.extras = members + 2
        self.lead_rows = self.planes + self.chunks * self.extras
        self.all_rows = self.lead_rows + (self.chunks - 1) * self.planes
        self.held = held_fields(self.fields, levels)
        self.sums = self.fields * 2
        self.sent_gains = 2 * sum(len(half[0]) for half in self.held)

    def planes_at(self, chunk):
        return self.lead_rows + (chunk - 1) * self.planes if chunk else 0

    def extras_at(self, chunk):
        return self.planes + chunk * self.extras


def row_in_block(size, level, mem_index):
    row = lax.rem(level + size.levels * size.owned - lax.rem(size.owned * mem_index, size.levels), size.levels)
    return row, row < size.owned, lax.div(size.owned * mem_index + row, size.levels)


def pack_shapes(size, chips):
    one = (size.all_rows, SUBLANES, LANES)
    shapes = []
    for chip in chips:
        if chip == 0:
            shapes += [one, one]
        elif chip in EARLY:
            shapes.append((CORES, size.all_rows + (chip == 1), SUBLANES, LANES))
        else:
            shapes.append(one)
    return shapes + [(len(LATE), *one)] * (LATE[0] in chips)


def pack_target(outs, chips, chip, core):
    place = chips.index(chip) + (0 in chips[: chips.index(chip)])
    if chip == 0:
        return outs[place + core]
    if chip in EARLY:
        return outs[place].at[core]
    return outs[place] if core == 0 else outs[-1].at[LATE.index(chip)]


def pack_kernel(size, chips, flat_ref, perturb_hbm, alpha_hbm, innov_hbm, weight_hbm, mask_hbm, near_hbm, *refs):
    outs, scratch = refs[:-10], refs[-10:]
    perturb_ref, alpha_ref, innov_ref, weight_ref, mask_ref, near_ref, tiles_ref, plane_sems, alpha_sems, sems = scratch
    flat = flat_ref[0]
    own = lax.rem(flat, GROUP)
    mem_index = lax.div(flat, 2)
    places = [(chip, core, chunk) for chip in chips for core in range(CORES) for chunk in range(size.chunks)]
    levels = [lax.bitwise_xor(own, flat_offset(chip, core)) + chunk * GROUP for chip, core, chunk in places]
    plane_copies = [
        pltpu.make_async_copy(perturb_hbm.at[:, level], perturb_ref.at[place], plane_sems.at[place])
        for place, level in enumerate(levels)
    ]
    alpha_copies = [
        pltpu.make_async_copy(alpha_hbm.at[:, level], alpha_ref.at[place], alpha_sems.at[place])
        for place, level in enumerate(levels)
    ]
    pairs = ((mask_hbm, mask_ref), (near_hbm, near_ref), (innov_hbm, innov_ref), (weight_hbm, weight_ref))
    copies = [pltpu.make_async_copy(source, target, sems.at[place]) for place, (source, target) in enumerate(pairs)]
    for copy in plane_copies + copies + alpha_copies:
        copy.start()
    copies[0].wait()
    tiles = mask_ref.shape[-1]
    shape = (tiles, tiles * TILE)
    spread_out = lax.broadcasted_iota(jnp.int32, shape, 0) == lax.div(lax.broadcasted_iota(jnp.int32, shape, 1), TILE)
    line = lax.broadcasted_iota(jnp.int32, (SUBLANES, LANES), 0)
    for slot in range(size.slots):
        cells = jnp.dot(
            mask_ref[slot].astype(jnp.float32), spread_out.astype(jnp.float32), preferred_element_type=jnp.float32
        )
        tiles_ref[slot] = jnp.where(line < TILE, cells[:, :LANES], cells[:, LANES:])
    copies[1].wait()
    if 1 in chips:
        coef_out = outs[chips.index(1)]
        coef_out[0, size.all_rows] = near_ref[0]
        coef_out[1, size.all_rows] = near_ref[1]
    for place, (chip, core, chunk) in enumerate(places):
        plane_copies[place].wait()
        base = size.planes_at(chunk)
        pack_target(outs, chips, chip, core)[base : base + size.planes] = perturb_ref[place].astype(jnp.float32)
    copies[2].wait()
    copies[3].wait()
    for place, (chip, core, chunk) in enumerate(places):
        out = pack_target(outs, chips, chip, core)
        base = size.extras_at(chunk)
        alpha_copies[place].wait()
        out[base : base + size.members] = alpha_ref[place]
        row, inside, field = row_in_block(size, levels[place], mem_index)
        row = jnp.minimum(row, size.owned - 1)
        slot = jnp.minimum(lax.div(field, size.vars), size.slots - 1)
        kept = jnp.where(inside, 1.0, 0.0).astype(jnp.float32)
        out[base + size.members] = innov_ref[row] * kept
        out[base + size.members + 1] = weight_ref[row] * tiles_ref[slot] * kept


class Pieces:
    def __init__(self, size, chunk, refs):
        self.size = size
        self.chunk = chunk
        self.refs = refs
        self.far_ref = refs[2 + EARLY.index(1)]

    def place(self, chip, core):
        if chip == 0:
            return self.refs[core], (), True
        if chip in EARLY:
            place = EARLY.index(chip)
            if core == 0:
                return self.refs[2 + place], (0,), True
            return self.refs[2 + len(EARLY)], (place,), True
        return self.refs[3 + len(EARLY) + LATE.index(chip)], (core,), False

    def plane(self, chip, core, row):
        ref, lead, whole = self.place(chip, core)
        if not whole and self.chunk:
            ref = self.refs[3 + len(EARLY) + len(LATE) + LATE.index(chip)]
        base = self.size.planes_at(self.chunk) if whole else 0
        return ref[lead + (base + row,)]

    def extra(self, chip, core, chunk, row):
        ref, lead, _ = self.place(chip, core)
        return ref[lead + (self.size.extras_at(chunk) + row,)]

    def alpha(self, chip, core):
        ref, lead, _ = self.place(chip, core)
        base = self.size.extras_at(self.chunk)
        return ref[lead + (slice(base, base + self.size.members),)]

    def far(self):
        return [self.far_ref[part, self.size.all_rows] for part in range(2)]


def roll(cells, shift, axis):
    return pltpu.roll(cells, shift, axis=cells.ndim + axis)


def neighbours(own, other, edges):
    row0, row3, lane0, lane_last = edges
    turned = roll(own, SUBLANES // 2, -2)
    across = roll(other, SUBLANES // 2, -2)
    above = roll(jnp.where(row3, across, own), 1, -2)
    below = roll(jnp.where(row0, across, own), SUBLANES - 1, -2)
    east = roll(jnp.where(lane0, turned, own), LANES - 1, -1)
    west = roll(jnp.where(lane_last, turned, own), 1, -1)
    return above, below, east, west


def stencils(flat, near, far):
    shape = (SUBLANES, LANES)
    line = lax.rem(lax.broadcasted_iota(jnp.int32, shape, 0), TILE)
    lane = lax.broadcasted_iota(jnp.int32, shape, 1)
    edges = (line == 0, line == TILE - 1, lane == 0, lane == LANES - 1)
    band = lax.rem(flat, 2)
    weights = []
    for half, (own, other) in enumerate(((near, far), (far, near))):
        here = lax.bitwise_xor(band, half)
        open_top = jnp.where(jnp.logical_and(edges[0], here == 0), 0.0, 1.0).astype(jnp.float32)
        open_end = jnp.where(jnp.logical_and(edges[1], here == 1), 0.0, 1.0).astype(jnp.float32)
        above, below, _, _ = neighbours(own[0], other[0], edges)
        _, _, east, west = neighbours(own[1], other[1], edges)
        north = 0.5 * (own[0] + above * open_top)
        south = 0.5 * (own[0] + below * open_end)
        east = 0.5 * (own[1] + east)
        west = 0.5 * (own[1] + west)
        centre = 1.0 - north - south - east - west
        weights.append((centre, north * open_top, south * open_end, east, west))
    return edges, weights


def diffuse_pair(near, far, stencil):
    edges, weights = stencil
    for _ in range(DIFF_STEPS):
        pair = []
        for (own, other), (centre, north, south, east, west) in zip(((near, far), (far, near)), weights):
            above, below, right, left = neighbours(own, other, edges)
            pair.append(centre * own + north * above + south * below + east * right + west * left)
        near, far = pair
    return near, far


def add_chip(size, pieces, chip, spread, sums):
    for core in range(CORES):
        for field in range(size.fields):
            for member in range(size.members):
                plane = pieces.plane(chip, core, field * size.members + member)
                term = plane * spread[core * size.members + member]
                sums[field] = term if sums[field] is None else sums[field] + term


def add_products(size, pieces, pair, spread, sums):
    for half in range(2):
        add_chip(size, pieces, 2 * pair + half, spread[half], sums[half])


def adjoint_of(size, pieces, pair, misfit):
    halves = []
    for half in range(2):
        found = []
        for core in range(CORES):
            for member in range(size.members):
                total = None
                for field in range(size.fields):
                    plane = pieces.plane(2 * pair + half, core, field * size.members + member)
                    term = plane * misfit[half][field]
                    total = term if total is None else total + term
                found.append(total)
        halves.append(jnp.stack(found))
    return halves


def first_alpha(pieces, pair):
    return [
        jnp.concatenate([pieces.alpha(2 * pair + half, core) for core in range(CORES)]) for half in range(2)
    ]


def gather_slots(size, pieces, mem_index, own, gain_ref, innov_ref):
    gain_ref[...] = jnp.zeros_like(gain_ref)
    innov_ref[...] = jnp.zeros_like(innov_ref)
    for chunk in range(size.chunks):
        for chip in range(0, CHIPS, 2):
            for core in range(CORES):
                source = lax.bitwise_xor(mem_index, (chip & 6) | core)
                _, inside, field = row_in_block(size, own + chunk * GROUP, source)

                @pl.when(inside)
                def _(chip=chip, core=core, chunk=chunk, field=field):
                    for half in range(2):
                        innov_ref[chunk, field, half] = pieces.extra(chip + half, core, chunk, size.members)
                        gain_ref[chunk, field, half] = pieces.extra(chip + half, core, chunk, size.members + 1)


def gain_places(size):
    row, found = size.sums, []
    for chunk, halves in enumerate(size.held):
        for first, second in zip(*halves):
            found.append((row, chunk, first, second))
            row += 2
    return found


def first_kernel(size, flat_ref, near_ref, *refs):
    sum_ref, gain_ref, innov_ref = refs[-3:]
    pieces = Pieces(size, 0, refs[:-3])
    flat = flat_ref[0]
    stencil = stencils(flat, [near_ref[0], near_ref[1]], pieces.far())
    side = lax.div(flat, GROUP)
    gather_slots(size, pieces, lax.div(flat, 2), lax.rem(flat, GROUP), gain_ref, innov_ref)
    for row, part, first, second in gain_places(size):
        sum_ref[pl.ds(row, 2)] = gain_ref[part, jnp.where(side == 0, first, second)]
    sums = [[None] * size.fields for _ in range(2)]
    for pair in range(CHIPS // 2):
        spread = diffuse_pair(*first_alpha(pieces, pair), stencil)
        add_products(size, pieces, pair, spread, sums)
    for field in range(size.fields):
        for half in range(2):
            sum_ref[field * 2 + half] = sums[half][field] - innov_ref[0, field, half]


def ahead_kernel(chunk, size, flat_ref, near_ref, innov_ref, *refs):
    part_ref, spread_ref = refs[-2:]
    pieces = Pieces(size, chunk, refs[:-2])
    stencil = stencils(flat_ref[0], [near_ref[0], near_ref[1]], pieces.far())
    sums = [[None] * size.fields for _ in range(2)]
    for pair in range(CHIPS // 2):
        spread = diffuse_pair(*first_alpha(pieces, pair), stencil)
        for half in range(2):
            chip = 2 * pair + half
            if chip in LATE:
                spread_ref[LATE.index(chip)] = spread[half]
            else:
                add_chip(size, pieces, chip, spread[half], sums[half])
    for field in range(size.fields):
        for half in range(2):
            part_ref[field * 2 + half] = sums[half][field] - innov_ref[chunk, field, half]


def rest_kernel(size, flat_ref, part_ref, spread_ref, *refs):
    late, sum_ref = refs[:-1], refs[-1]
    sums = [[part_ref[field * 2 + half] for field in range(size.fields)] for half in range(2)]
    for place, chip in enumerate(LATE):
        for core in range(CORES):
            for field in range(size.fields):
                for member in range(size.members):
                    plane = late[place][core, field * size.members + member]
                    sums[chip & 1][field] += plane * spread_ref[place, core * size.members + member]
    for field in range(size.fields):
        for half in range(2):
            sum_ref[field * 2 + half] = sums[half][field]


def misfit_of(size, chunk, gain_ref, mine_ref, theirs_ref):
    return [
        [
            gain_ref[chunk, field, half] * (mine_ref[field * 2 + half] + theirs_ref[field * 2 + half])
            for field in range(size.fields)
        ]
        for half in range(2)
    ]


def middle_kernel(chunk, size, flat_ref, near_ref, mine_ref, theirs_ref, gain_in_ref, innov_ref, *refs):
    if chunk:
        gain_ref, (sum_ref, alpha_ref) = gain_in_ref, refs[-2:]
        pieces = Pieces(size, chunk, refs[:-2])
    else:
        sum_ref, alpha_ref, gain_ref = refs[-3:]
        pieces = Pieces(size, chunk, refs[:-3])
    flat = flat_ref[0]
    stencil = stencils(flat, [near_ref[0], near_ref[1]], pieces.far())
    if not chunk:
        side = lax.div(flat, GROUP)
        gain_ref[...] = gain_in_ref[...]
        for row, part, first, second in gain_places(size):
            gain_ref[part, jnp.where(side == 0, second, first)] = theirs_ref[pl.ds(row, 2)]
    misfit = misfit_of(size, chunk, gain_ref, mine_ref, theirs_ref)
    sums = [[None] * size.fields for _ in range(2)]
    for pair in range(CHIPS // 2):
        change = diffuse_pair(*adjoint_of(size, pieces, pair, misfit), stencil)
        before = first_alpha(pieces, pair)
        alpha = [old - 0.3 * (old + new) for old, new in zip(before, change)]
        for half in range(2):
            alpha_ref[pair, half] = alpha[half]
        add_products(size, pieces, pair, diffuse_pair(*alpha, stencil), sums)
    for field in range(size.fields):
        for half in range(2):
            sum_ref[field * 2 + half] = sums[half][field] - innov_ref[chunk, field, half]


def last_kernel(chunk, size, flat_ref, near_ref, mine_ref, theirs_ref, gain_ref, alpha_ref, *refs):
    refs, (out_ref, misfit_ref) = refs[:-2], refs[-2:]
    flat = flat_ref[0]
    own = lax.rem(flat, GROUP)
    mem_index = lax.div(flat, 2)
    base = chunk * (size.members + 1)
    if chunk:
        out_ref[:, :base] = refs[0][...]
        refs = refs[1:]
    pieces = Pieces(size, chunk, refs)
    stencil = stencils(flat, [near_ref[0], near_ref[1]], pieces.far())
    misfit = misfit_of(size, chunk, gain_ref, mine_ref, theirs_ref)
    for half in range(2):
        for field in range(size.fields):
            misfit_ref[half, field] = misfit[half][field]
    level = own + chunk * GROUP
    for pair in range(CHIPS // 2):
        change = diffuse_pair(*adjoint_of(size, pieces, pair, misfit), stencil)
        for half in range(2):
            old = alpha_ref[pair, half]
            alpha = old - 0.3 * (old + change[half])
            chip = 2 * pair + half
            for core in range(CORES):
                target = lax.bitwise_xor(own, flat_offset(chip, core))
                out_ref[target, base : base + size.members] = alpha[core * size.members : (core + 1) * size.members]
                _, _, field = row_in_block(size, level, lax.bitwise_xor(mem_index, (chip & 6) | core))
                out_ref[target, base + size.members] = misfit_ref[half, jnp.minimum(field, size.fields - 1)]


def unfold_into(out, at, block):
    rows = block.shape[-2] // 2
    out[at + (slice(None), slice(0, LANES))] = block[..., :rows, :]
    out[at + (slice(None), slice(LANES, 2 * LANES))] = block[..., rows:, :]


def place_kernel(size, flat_ref, back_ref, alpha_ref, misfit_ref):
    mem_index = lax.div(flat_ref[0], 2)
    for source in range(GROUP):
        for chunk in range(size.chunks):
            base = chunk * (size.members + 1)
            level = source + chunk * GROUP
            for member in range(size.members):
                unfold_into(alpha_ref, (member, level), back_ref[source, base + member])
            row, inside, _ = row_in_block(size, level, mem_index)

            @pl.when(inside)
            def _(source=source, base=base, row=row):
                unfold_into(misfit_ref, (row,), back_ref[source, base + size.members])


def call(kernel, outs, operands, scratch=(), spaces=None, limit=24):
    spaces = spaces or [pltpu.VMEM] * len(operands)
    moved = 4 * sum(math.prod(shape) for shape in outs) + sum(x.size * x.dtype.itemsize for x in operands)
    return pl.pallas_call(
        kernel,
        out_shape=[jax.ShapeDtypeStruct(shape, jnp.float32) for shape in outs],
        in_specs=[pl.BlockSpec(memory_space=space) for space in [pltpu.SMEM] + spaces[1:]],
        out_specs=[pl.BlockSpec(memory_space=pltpu.VMEM)] * len(outs),
        scratch_shapes=scratch,
        cost_estimate=pl.CostEstimate(flops=moved, bytes_accessed=moved, transcendentals=0),
        compiler_params=pltpu.CompilerParams(vmem_limit_bytes=limit * 1024 * 1024),
    )(*[in_hbm(x) if space is pltpu.HBM else x for x, space in zip(operands, spaces)])


def in_hbm(cells):
    return pltpu.with_memory_space_constraint(cells, pltpu.HBM)


def spread_levels(size, flat, near, perturb, alpha_init, innovation, obs_weight, obs_mask):
    block = (SUBLANES, LANES)
    operands = (
        fold(perturb).reshape(size.planes, size.levels, *block),
        fold(alpha_init),
        fold(innovation),
        fold(obs_weight),
        obs_mask,
        near,
    )

    def pack(chips, flat):
        count = len(chips) * CORES * size.chunks
        return call(
            functools.partial(pack_kernel, size, chips),
            pack_shapes(size, chips),
            (flat,) + operands,
            [
                pltpu.VMEM((count, size.planes, *block), jnp.bfloat16),
                pltpu.VMEM((count, size.members, *block), jnp.float32),
                pltpu.VMEM((size.owned, *block), jnp.float32),
                pltpu.VMEM((size.owned, *block), jnp.float32),
                pltpu.VMEM(obs_mask.shape, jnp.int32),
                pltpu.VMEM(near.shape, jnp.float32),
                pltpu.VMEM((size.slots, *block), jnp.float32),
                pltpu.SemaphoreType.DMA((count,)),
                pltpu.SemaphoreType.DMA((count,)),
                pltpu.SemaphoreType.DMA((4,)),
            ],
            [pltpu.SMEM] + [pltpu.HBM] * 6,
        )

    early = list(pack(EARLY[:2], flat))
    flat, early[0], early[1] = lax.optimization_barrier((flat, early[0], early[1]))
    packed = pack(EARLY[2:] + (0,) + LATE, flat)
    early += packed[:2]
    kept, late, late_out = packed[2:4], packed[4:7], packed[7]
    crossed = shift_by(CORES, late_out)
    own_crossed = shift_by(CORES, kept[1])
    got = [shift_by(flat_offset(chip, 0), cells) for chip, cells in zip(EARLY, early)]
    got_late = []
    for chunk in range(size.chunks):
        base = size.planes_at(chunk)
        rows = slice(base, base + (size.planes if chunk else size.lead_rows))
        parts = [jnp.stack([cells[rows], crossed[place, rows]]) for place, cells in enumerate(late)]
        if chunk == 0:
            got[1], parts[0] = lax.optimization_barrier((got[1], parts[0]))
            got[2], parts[1] = lax.optimization_barrier((got[2], parts[1]))
            got[0], got[3], parts[2] = lax.optimization_barrier((got[0], got[3], parts[2]))
        else:
            prev = list(got_late[chunk - 1])
            prev[0], parts[0] = lax.optimization_barrier((prev[0], parts[0]))
            prev[1], parts[1] = lax.optimization_barrier((prev[1], parts[1]))
            prev[2], parts[2] = lax.optimization_barrier((prev[2], parts[2]))
            got_late[chunk - 1] = tuple(prev)
        got_late.append(tuple(shift_by(flat_offset(chip, 0), cells) for chip, cells in zip(LATE, parts)))
    early_crossed = shift_by(CORES, jnp.stack([cells[1, : size.all_rows] for cells in got]))
    shared = (kept[0], own_crossed, *got, early_crossed)
    return [shared + got_late[0] + (got_late[chunk] if chunk else ()) for chunk in range(size.chunks)]


def level_shards(perturb, alpha_init, innovation, obs_weight, coef, obs_mask):
    size = Sizes(perturb, innovation.shape[0])
    levels, rows, lon_cells = perturb.shape[3:]
    block = (SUBLANES, LANES)
    flat = (lax.axis_index("mem") * lax.axis_size("lat") + lax.axis_index("lat")).astype(jnp.int32).reshape(1)
    near = fold(coef)
    pieces = spread_levels(size, flat, near, perturb, alpha_init, innovation, obs_weight, obs_mask)
    common = (flat, near)
    all_fields = (size.chunks, size.fields, 2, *block)
    alpha_shape = (CHIPS // 2, 2, CORES * size.members, *block)
    chunks = range(size.chunks)
    first, second, back, held, innov, gain = [], [], None, None, None, None
    shapes = [(size.sums + size.sent_gains, *block), all_fields, all_fields]
    mine, held, innov = call(functools.partial(first_kernel, size), shapes, common + pieces[0])
    first.append((mine, shift_by(GROUP, mine)))
    for chunk in chunks[1:]:
        shapes = [(size.sums, *block), (len(LATE), CORES * size.members, *block)]
        known = call(functools.partial(ahead_kernel, chunk, size), shapes, common + (innov,) + pieces[0])
        late = pieces[chunk][-len(LATE) :]
        (mine,) = call(functools.partial(rest_kernel, size), [(size.sums, *block)], (flat, *known, *late))
        first.append((mine, shift_by(GROUP, mine)))
    for chunk in chunks:
        kernel = functools.partial(middle_kernel, chunk, size)
        shapes = [(size.sums, *block), alpha_shape] + ([] if chunk else [all_fields])
        operands = common + first[chunk] + (gain if chunk else held, innov) + pieces[chunk]
        mine, alpha, *rest = call(kernel, shapes, operands)
        gain = gain if chunk else rest[0]
        second.append((mine, shift_by(GROUP, mine), gain, alpha))
    for chunk in chunks:
        (back,) = call(
            functools.partial(last_kernel, chunk, size),
            [(GROUP, (chunk + 1) * (size.members + 1), *block)],
            common + second[chunk] + (() if back is None else (back,)) + pieces[chunk],
            [pltpu.VMEM((2, size.fields, *block), jnp.float32)],
        )
    groups = [[half * GROUP + place for place in range(GROUP)] for half in range(2)]
    back = lax.all_to_all(back, ("mem", "lat"), 0, 0, axis_index_groups=groups, tiled=True)
    return tuple(
        call(
            functools.partial(place_kernel, size),
            [(size.members, levels, rows, lon_cells), (size.owned, rows, lon_cells)],
            (flat, back),
        )
    )


def solution(mesh):
    in_specs = (
        P(None, None, "mem", None, "lat", None),
        P("mem", None, "lat", None),
        P("mem", "lat", None),
        P("mem", "lat", None),
        P(None, "lat", None),
        P(None, "lat", None),
    )
    out_specs = (P("mem", None, "lat", None), P("mem", "lat", None))

    def run(*args):
        body = level_shards if fits(mesh, args[0], args[2]) else shards
        return jax.shard_map(body, mesh=mesh, in_specs=in_specs, out_specs=out_specs, check_vma=False)(*args)

    return run
```

```python
import functools
import math

import jax
import jax.numpy as jnp
from jax import lax
from jax.experimental import pallas as pl
from jax.experimental.pallas import tpu as pltpu
from jax.sharding import PartitionSpec as P

ITERS = 2
DIFF_STEPS = 4
TILE = 4


def with_halo(cells, sides, width):
    for axis, dim in sides:
        count = lax.axis_size(axis)
        ends = count - 1
        head = lax.slice_in_dim(cells, 0, width, axis=dim)
        tail = lax.slice_in_dim(cells, cells.shape[dim] - width, cells.shape[dim], axis=dim)
        cells = jnp.concatenate(
            [
                lax.ppermute(tail, axis, [(i, (i + 1) % count) for i in range(ends)]),
                cells,
                lax.ppermute(head, axis, [((i + 1) % count, i) for i in range(ends)]),
            ],
            axis=dim,
        )
    return cells


def face_weights(coef):
    klat = coef[0]
    klon = coef[1]
    zero_row = jnp.zeros_like(klat[:1])
    north_face = 0.5 * (klat + jnp.concatenate([zero_row, klat[:-1]], axis=0))
    south_face = 0.5 * (klat + jnp.concatenate([klat[1:], zero_row], axis=0))
    east_face = 0.5 * (klon + jnp.roll(klon, -1, axis=1))
    west_face = 0.5 * (klon + jnp.roll(klon, 1, axis=1))
    return (north_face, south_face, east_face, west_face)


def diffuse_once(layer_field, face_list, valid_rows):
    north_face, south_face, east_face, west_face = face_list
    zero_row = jnp.zeros_like(layer_field[..., :1, :])
    above = jnp.concatenate([zero_row, layer_field[..., :-1, :]], axis=-2)
    below = jnp.concatenate([layer_field[..., 1:, :], zero_row], axis=-2)
    east_val = jnp.roll(layer_field, -1, axis=-1)
    west_val = jnp.roll(layer_field, 1, axis=-1)
    updated = layer_field + north_face * (above - layer_field) + south_face * (below - layer_field)
    updated = updated + east_face * (east_val - layer_field) + west_face * (west_val - layer_field)
    return updated * valid_rows


def rim_rows(all_faces):
    return tuple((face for face in all_faces))


def valid_mask(margin, band_rows):
    global_row = (
        lax.axis_index("lat") * band_rows
        + jnp.arange(band_rows + 2 * margin, dtype=jnp.int32)
        - margin
    )
    total_rows = band_rows * lax.axis_size("lat")
    inside = jnp.logical_and(global_row >= 0, global_row < total_rows)
    return inside.astype(jnp.float32)[:, None]


def diffuse_field(layer_field, all_faces, band_rows):
    face_list = rim_rows(all_faces)
    valid_rows = valid_mask(DIFF_STEPS, band_rows)
    extended = with_halo(layer_field, (("lat", 2),), DIFF_STEPS)
    for sweep in range(DIFF_STEPS):
        extended = diffuse_once(extended, face_list, valid_rows)
    return extended[..., DIFF_STEPS : DIFF_STEPS + band_rows, :]


def shards(perturb, alpha_init, innovation, obs_weight, coef, obs_mask):
    slot_count, var_count, members, levels, band_rows, lon_cells = perturb.shape
    owned_rows = innovation.shape[0]
    coef_ext = with_halo(coef, (("lat", 1),), DIFF_STEPS)
    all_faces = face_weights(coef_ext)
    tile_mask = jnp.repeat(jnp.repeat(obs_mask, TILE, axis=1), TILE, axis=2).astype(jnp.float32)
    first_row = lax.axis_index("mem") * owned_rows
    slot_of_row = (first_row + jnp.arange(owned_rows, dtype=jnp.int32)) // (var_count * levels)
    one_hot = (slot_of_row[:, None] == jnp.arange(slot_count, dtype=jnp.int32)[None, :]).astype(
        jnp.float32
    )
    row_mask = jnp.sum(one_hot[:, :, None, None] * tile_mask[None], axis=1)
    row_gain = obs_weight * row_mask
    alpha = alpha_init
    misfit = jnp.zeros_like(innovation)
    for sweep in range(ITERS):
        spread = diffuse_field(alpha, all_faces, band_rows)
        partial_sum = jnp.sum(perturb.astype(jnp.float32) * spread[None, None], axis=2)
        partial_sum = partial_sum.reshape(slot_count * var_count * levels, band_rows, lon_cells)
        increment = lax.psum_scatter(partial_sum, "mem", scatter_dimension=0, tiled=True)
        misfit = row_gain * (increment - innovation)
        gathered = lax.all_gather(misfit, "mem", axis=0, tiled=True)
        misfit_rows = gathered.reshape(slot_count, var_count, levels, band_rows, lon_cells)
        adjoint = jnp.sum(perturb.astype(jnp.float32) * misfit_rows[:, :, None], axis=(0, 1))
        alpha = alpha - 0.3 * (alpha + diffuse_field(adjoint, all_faces, band_rows))
    return (alpha, misfit)


LANES = 128
SUBLANES = 8
CHIPS = 8
CORES = 2
GROUP = CHIPS * CORES
EARLY = (1, 6, 2, 5)
LATE = (4, 3, 7)


def fold(cells):
    lead, (rows, cols) = cells.shape[:-2], cells.shape[-2:]
    parts = cells.reshape(*lead, rows, cols // LANES, LANES).swapaxes(-3, -2)
    return parts.reshape(*lead, rows * cols // LANES, LANES)


def fits(mesh, perturb, innovation):
    slot_count, var_count, members, levels, rows, lon_cells = perturb.shape
    mem, lat = mesh.shape["mem"], mesh.shape["lat"]
    if lat != 2 or mem != 2 * GROUP // lat:
        return False
    if rows != lat * TILE or DIFF_STEPS > TILE or TILE * lon_cells != SUBLANES * LANES:
        return False
    total = slot_count * var_count * levels
    if members % mem or levels % GROUP or total % mem or total // mem > levels:
        return False
    return held_fields(slot_count * var_count, levels) is not None


def held_fields(fields, levels):
    chunks = []
    for chunk in range(levels // GROUP):
        halves = ([], [])
        for field in range(fields):
            rows = [field * levels + chunk * GROUP + place for place in range(GROUP)]
            sides = {2 * row // (fields * levels) for row in rows}
            if len(sides) != 1:
                return None
            halves[sides.pop()].append(field)
        if not halves[0] or not halves[1]:
            return None
        longest = max(len(half) for half in halves)
        chunks.append([half + half[-1:] * (longest - len(half)) for half in halves])
    return chunks


def flat_offset(chip, core):
    return ((chip >> 1) << 2) | (core << 1) | (chip & 1)


def shift_by(mask, cells):
    axes = ("mem", "lat")
    count = lax.axis_size("mem") * lax.axis_size("lat")
    return lax.ppermute(cells, axes, [(i, i ^ mask) for i in range(count)])


class Sizes:
    def __init__(self, perturb, owned_rows):
        slots, variables, members, levels = perturb.shape[:4]
        self.slots = slots
        self.vars = variables
        self.fields = slots * variables
        self.members = members
        self.levels = levels
        self.owned = owned_rows
        self.chunks = levels // GROUP
        self.planes = self.fields * members
        self.extras = members + 2
        self.lead_rows = self.planes + self.chunks * self.extras
        self.all_rows = self.lead_rows + (self.chunks - 1) * self.planes
        self.held = held_fields(self.fields, levels)
        self.sums = self.fields * 2
        self.sent_gains = 2 * sum(len(half[0]) for half in self.held)

    def planes_at(self, chunk):
        return self.lead_rows + (chunk - 1) * self.planes if chunk else 0

    def extras_at(self, chunk):
        return self.planes + chunk * self.extras


def row_in_block(size, level, mem_index):
    row = lax.rem(level + size.levels * size.owned - lax.rem(size.owned * mem_index, size.levels), size.levels)
    return row, row < size.owned, lax.div(size.owned * mem_index + row, size.levels)


def pack_shapes(size, chips):
    one = (size.all_rows, SUBLANES, LANES)
    shapes = []
    for chip in chips:
        if chip == 0:
            shapes += [one, one]
        elif chip in EARLY:
            shapes.append((CORES, size.all_rows + (chip == 1), SUBLANES, LANES))
        else:
            shapes.append(one)
    return shapes + [(len(LATE), *one)] * (LATE[0] in chips)


def pack_target(outs, chips, chip, core):
    place = chips.index(chip) + (0 in chips[: chips.index(chip)])
    if chip == 0:
        return outs[place + core]
    if chip in EARLY:
        return outs[place].at[core]
    return outs[place] if core == 0 else outs[-1].at[LATE.index(chip)]


def pack_kernel(size, chips, fetch, flat_ref, *refs):
    flat = flat_ref[0]
    own = lax.rem(flat, GROUP)
    mem_index = lax.div(flat, 2)
    places = [(chip, core, chunk) for chip in chips for core in range(CORES) for chunk in range(size.chunks)]
    levels = [lax.bitwise_xor(own, flat_offset(chip, core)) + chunk * GROUP for chip, core, chunk in places]
    sources = refs[:6]
    if fetch:
        outs, scratch = refs[6:-10], refs[-10:]
        perturb_ref, alpha_ref, *held, tiles_ref, plane_sems, alpha_sems, sems = scratch
        plane_copies = [
            pltpu.make_async_copy(sources[0].at[:, level], perturb_ref.at[place], plane_sems.at[place])
            for place, level in enumerate(levels)
        ]
        alpha_copies = [
            pltpu.make_async_copy(sources[1].at[:, level], alpha_ref.at[place], alpha_sems.at[place])
            for place, level in enumerate(levels)
        ]
        copies = [pltpu.make_async_copy(sources[2 + n], held[n], sems.at[n]) for n in range(4)]
        for copy in plane_copies + copies + alpha_copies:
            copy.start()
        copies[2].wait()
    else:
        outs, tiles_ref, held = refs[6:-1], refs[-1], sources[2:]
    innov_ref, weight_ref, mask_ref, near_ref = held
    tiles = mask_ref.shape[-1]
    shape = (tiles, tiles * TILE)
    spread_out = lax.broadcasted_iota(jnp.int32, shape, 0) == lax.div(lax.broadcasted_iota(jnp.int32, shape, 1), TILE)
    line = lax.broadcasted_iota(jnp.int32, (SUBLANES, LANES), 0)
    for slot in range(size.slots):
        cells = jnp.dot(
            mask_ref[slot].astype(jnp.float32), spread_out.astype(jnp.float32), preferred_element_type=jnp.float32
        )
        tiles_ref[slot] = jnp.where(line < TILE, cells[:, :LANES], cells[:, LANES:])
    if fetch:
        copies[3].wait()
    if 1 in chips:
        coef_out = outs[chips.index(1)]
        coef_out[0, size.all_rows] = near_ref[0]
        coef_out[1, size.all_rows] = near_ref[1]
    for place, (chip, core, chunk) in enumerate(places):
        if fetch:
            plane_copies[place].wait()
        planes = perturb_ref[place] if fetch else sources[0][:, levels[place]]
        base = size.planes_at(chunk)
        pack_target(outs, chips, chip, core)[base : base + size.planes] = planes.astype(jnp.float32)
    if fetch:
        copies[0].wait()
        copies[1].wait()
    for place, (chip, core, chunk) in enumerate(places):
        out = pack_target(outs, chips, chip, core)
        base = size.extras_at(chunk)
        if fetch:
            alpha_copies[place].wait()
        out[base : base + size.members] = alpha_ref[place] if fetch else sources[1][:, levels[place]]
        row, inside, field = row_in_block(size, levels[place], mem_index)
        row = jnp.minimum(row, size.owned - 1)
        slot = jnp.minimum(lax.div(field, size.vars), size.slots - 1)
        kept = jnp.where(inside, 1.0, 0.0).astype(jnp.float32)
        out[base + size.members] = innov_ref[row] * kept
        out[base + size.members + 1] = weight_ref[row] * tiles_ref[slot] * kept


class Pieces:
    def __init__(self, size, chunk, refs):
        self.size = size
        self.chunk = chunk
        self.refs = refs
        self.far_ref = refs[2 + EARLY.index(1)]

    def place(self, chip, core):
        if chip == 0:
            return self.refs[core], (), True
        if chip in EARLY:
            place = EARLY.index(chip)
            if core == 0:
                return self.refs[2 + place], (0,), True
            return self.refs[2 + len(EARLY)], (place,), True
        return self.refs[3 + len(EARLY) + LATE.index(chip)], (core,), False

    def plane(self, chip, core, row):
        ref, lead, whole = self.place(chip, core)
        if not whole and self.chunk:
            ref = self.refs[3 + len(EARLY) + len(LATE) + LATE.index(chip)]
        base = self.size.planes_at(self.chunk) if whole else 0
        return ref[lead + (base + row,)]

    def extra(self, chip, core, chunk, row):
        ref, lead, _ = self.place(chip, core)
        return ref[lead + (self.size.extras_at(chunk) + row,)]

    def alpha(self, chip, core):
        ref, lead, _ = self.place(chip, core)
        base = self.size.extras_at(self.chunk)
        return ref[lead + (slice(base, base + self.size.members),)]

    def far(self):
        return [self.far_ref[part, self.size.all_rows] for part in range(2)]


def roll(cells, shift, axis):
    return pltpu.roll(cells, shift, axis=cells.ndim + axis)


def neighbours(own, other, edges):
    row0, row3, lane0, lane_last = edges
    turned = roll(own, SUBLANES // 2, -2)
    across = roll(other, SUBLANES // 2, -2)
    above = roll(jnp.where(row3, across, own), 1, -2)
    below = roll(jnp.where(row0, across, own), SUBLANES - 1, -2)
    east = roll(jnp.where(lane0, turned, own), LANES - 1, -1)
    west = roll(jnp.where(lane_last, turned, own), 1, -1)
    return above, below, east, west


def stencils(flat, near, far):
    shape = (SUBLANES, LANES)
    line = lax.rem(lax.broadcasted_iota(jnp.int32, shape, 0), TILE)
    lane = lax.broadcasted_iota(jnp.int32, shape, 1)
    edges = (line == 0, line == TILE - 1, lane == 0, lane == LANES - 1)
    band = lax.rem(flat, 2)
    weights = []
    for half, (own, other) in enumerate(((near, far), (far, near))):
        here = lax.bitwise_xor(band, half)
        open_top = jnp.where(jnp.logical_and(edges[0], here == 0), 0.0, 1.0).astype(jnp.float32)
        open_end = jnp.where(jnp.logical_and(edges[1], here == 1), 0.0, 1.0).astype(jnp.float32)
        above, below, _, _ = neighbours(own[0], other[0], edges)
        _, _, east, west = neighbours(own[1], other[1], edges)
        north = 0.5 * (own[0] + above * open_top)
        south = 0.5 * (own[0] + below * open_end)
        east = 0.5 * (own[1] + east)
        west = 0.5 * (own[1] + west)
        centre = 1.0 - north - south - east - west
        weights.append((centre, north * open_top, south * open_end, east, west))
    return edges, weights


def diffuse_pair(near, far, stencil):
    edges, weights = stencil
    for _ in range(DIFF_STEPS):
        pair = []
        for (own, other), (centre, north, south, east, west) in zip(((near, far), (far, near)), weights):
            above, below, right, left = neighbours(own, other, edges)
            pair.append(centre * own + north * above + south * below + east * right + west * left)
        near, far = pair
    return near, far


def add_chip(size, pieces, chip, spread, sums):
    for core in range(CORES):
        for field in range(size.fields):
            for member in range(size.members):
                plane = pieces.plane(chip, core, field * size.members + member)
                term = plane * spread[core * size.members + member]
                sums[field] = term if sums[field] is None else sums[field] + term


def add_products(size, pieces, pair, spread, sums):
    for half in range(2):
        add_chip(size, pieces, 2 * pair + half, spread[half], sums[half])


def adjoint_of(size, pieces, pair, misfit):
    halves = []
    for half in range(2):
        found = []
        for core in range(CORES):
            for member in range(size.members):
                total = None
                for field in range(size.fields):
                    plane = pieces.plane(2 * pair + half, core, field * size.members + member)
                    term = plane * misfit[half][field]
                    total = term if total is None else total + term
                found.append(total)
        halves.append(jnp.stack(found))
    return halves


def first_alpha(pieces, pair):
    return [
        jnp.concatenate([pieces.alpha(2 * pair + half, core) for core in range(CORES)]) for half in range(2)
    ]


def gather_slots(size, pieces, mem_index, own, gain_ref, innov_ref):
    gain_ref[...] = jnp.zeros_like(gain_ref)
    innov_ref[...] = jnp.zeros_like(innov_ref)
    for chunk in range(size.chunks):
        for chip in range(0, CHIPS, 2):
            for core in range(CORES):
                source = lax.bitwise_xor(mem_index, (chip & 6) | core)
                _, inside, field = row_in_block(size, own + chunk * GROUP, source)

                @pl.when(inside)
                def _(chip=chip, core=core, chunk=chunk, field=field):
                    for half in range(2):
                        innov_ref[chunk, field, half] = pieces.extra(chip + half, core, chunk, size.members)
                        gain_ref[chunk, field, half] = pieces.extra(chip + half, core, chunk, size.members + 1)


def gain_places(size):
    row, found = size.sums, []
    for chunk, halves in enumerate(size.held):
        for first, second in zip(*halves):
            found.append((row, chunk, first, second))
            row += 2
    return found


def first_kernel(size, flat_ref, near_ref, *refs):
    sum_ref, gain_ref, innov_ref = refs[-3:]
    pieces = Pieces(size, 0, refs[:-3])
    flat = flat_ref[0]
    stencil = stencils(flat, [near_ref[0], near_ref[1]], pieces.far())
    side = lax.div(flat, GROUP)
    gather_slots(size, pieces, lax.div(flat, 2), lax.rem(flat, GROUP), gain_ref, innov_ref)
    for row, part, first, second in gain_places(size):
        sum_ref[pl.ds(row, 2)] = gain_ref[part, jnp.where(side == 0, first, second)]
    sums = [[None] * size.fields for _ in range(2)]
    for pair in range(CHIPS // 2):
        spread = diffuse_pair(*first_alpha(pieces, pair), stencil)
        add_products(size, pieces, pair, spread, sums)
    for field in range(size.fields):
        for half in range(2):
            sum_ref[field * 2 + half] = sums[half][field] - innov_ref[0, field, half]


def ahead_kernel(chunk, size, flat_ref, near_ref, innov_ref, *refs):
    part_ref, spread_ref = refs[-2:]
    pieces = Pieces(size, chunk, refs[:-2])
    stencil = stencils(flat_ref[0], [near_ref[0], near_ref[1]], pieces.far())
    sums = [[None] * size.fields for _ in range(2)]
    for pair in range(CHIPS // 2):
        spread = diffuse_pair(*first_alpha(pieces, pair), stencil)
        for half in range(2):
            chip = 2 * pair + half
            if chip in LATE:
                spread_ref[LATE.index(chip)] = spread[half]
            else:
                add_chip(size, pieces, chip, spread[half], sums[half])
    for field in range(size.fields):
        for half in range(2):
            part_ref[field * 2 + half] = sums[half][field] - innov_ref[chunk, field, half]


def rest_kernel(size, flat_ref, part_ref, spread_ref, *refs):
    late, sum_ref = refs[:-1], refs[-1]
    sums = [[part_ref[field * 2 + half] for field in range(size.fields)] for half in range(2)]
    for place, chip in enumerate(LATE):
        for core in range(CORES):
            for field in range(size.fields):
                for member in range(size.members):
                    plane = late[place][core, field * size.members + member]
                    sums[chip & 1][field] += plane * spread_ref[place, core * size.members + member]
    for field in range(size.fields):
        for half in range(2):
            sum_ref[field * 2 + half] = sums[half][field]


def misfit_of(size, chunk, gain_ref, mine_ref, theirs_ref):
    return [
        [
            gain_ref[chunk, field, half] * (mine_ref[field * 2 + half] + theirs_ref[field * 2 + half])
            for field in range(size.fields)
        ]
        for half in range(2)
    ]


def middle_kernel(chunk, size, flat_ref, near_ref, mine_ref, theirs_ref, gain_in_ref, innov_ref, *refs):
    if chunk:
        gain_ref, (sum_ref, alpha_ref) = gain_in_ref, refs[-2:]
        pieces = Pieces(size, chunk, refs[:-2])
    else:
        sum_ref, alpha_ref, gain_ref = refs[-3:]
        pieces = Pieces(size, chunk, refs[:-3])
    flat = flat_ref[0]
    stencil = stencils(flat, [near_ref[0], near_ref[1]], pieces.far())
    if not chunk:
        side = lax.div(flat, GROUP)
        gain_ref[...] = gain_in_ref[...]
        for row, part, first, second in gain_places(size):
            gain_ref[part, jnp.where(side == 0, second, first)] = theirs_ref[pl.ds(row, 2)]
    misfit = misfit_of(size, chunk, gain_ref, mine_ref, theirs_ref)
    sums = [[None] * size.fields for _ in range(2)]
    for pair in range(CHIPS // 2):
        change = diffuse_pair(*adjoint_of(size, pieces, pair, misfit), stencil)
        before = first_alpha(pieces, pair)
        alpha = [old - 0.3 * (old + new) for old, new in zip(before, change)]
        for half in range(2):
            alpha_ref[pair, half] = alpha[half]
        add_products(size, pieces, pair, diffuse_pair(*alpha, stencil), sums)
    for field in range(size.fields):
        for half in range(2):
            sum_ref[field * 2 + half] = sums[half][field] - innov_ref[chunk, field, half]


def last_kernel(chunk, size, flat_ref, near_ref, mine_ref, theirs_ref, gain_ref, alpha_ref, *refs):
    refs, (out_ref, misfit_ref) = refs[:-2], refs[-2:]
    flat = flat_ref[0]
    own = lax.rem(flat, GROUP)
    mem_index = lax.div(flat, 2)
    base = chunk * (size.members + 1)
    if chunk:
        out_ref[:, :base] = refs[0][...]
        refs = refs[1:]
    pieces = Pieces(size, chunk, refs)
    stencil = stencils(flat, [near_ref[0], near_ref[1]], pieces.far())
    misfit = misfit_of(size, chunk, gain_ref, mine_ref, theirs_ref)
    for half in range(2):
        for field in range(size.fields):
            misfit_ref[half, field] = misfit[half][field]
    level = own + chunk * GROUP
    for pair in range(CHIPS // 2):
        change = diffuse_pair(*adjoint_of(size, pieces, pair, misfit), stencil)
        for half in range(2):
            old = alpha_ref[pair, half]
            alpha = old - 0.3 * (old + change[half])
            chip = 2 * pair + half
            for core in range(CORES):
                target = lax.bitwise_xor(own, flat_offset(chip, core))
                out_ref[target, base : base + size.members] = alpha[core * size.members : (core + 1) * size.members]
                _, _, field = row_in_block(size, level, lax.bitwise_xor(mem_index, (chip & 6) | core))
                out_ref[target, base + size.members] = misfit_ref[half, jnp.minimum(field, size.fields - 1)]


def unfold_into(out, at, block):
    rows = block.shape[-2] // 2
    out[at + (slice(None), slice(0, LANES))] = block[..., :rows, :]
    out[at + (slice(None), slice(LANES, 2 * LANES))] = block[..., rows:, :]


def place_kernel(size, flat_ref, back_ref, alpha_ref, misfit_ref):
    mem_index = lax.div(flat_ref[0], 2)
    for source in range(GROUP):
        for chunk in range(size.chunks):
            base = chunk * (size.members + 1)
            level = source + chunk * GROUP
            for member in range(size.members):
                unfold_into(alpha_ref, (member, level), back_ref[source, base + member])
            row, inside, _ = row_in_block(size, level, mem_index)

            @pl.when(inside)
            def _(source=source, base=base, row=row):
                unfold_into(misfit_ref, (row,), back_ref[source, base + size.members])


def call(kernel, outs, operands, scratch=(), spaces=None, limit=24):
    spaces = spaces or [pltpu.VMEM] * len(operands)
    moved = 4 * sum(math.prod(shape) for shape in outs) + sum(x.size * x.dtype.itemsize for x in operands)
    return pl.pallas_call(
        kernel,
        out_shape=[jax.ShapeDtypeStruct(shape, jnp.float32) for shape in outs],
        in_specs=[pl.BlockSpec(memory_space=space) for space in [pltpu.SMEM] + spaces[1:]],
        out_specs=[pl.BlockSpec(memory_space=pltpu.VMEM)] * len(outs),
        scratch_shapes=scratch,
        cost_estimate=pl.CostEstimate(flops=moved, bytes_accessed=moved, transcendentals=0),
        compiler_params=pltpu.CompilerParams(vmem_limit_bytes=limit * 1024 * 1024),
    )(*[in_hbm(x) if space is pltpu.HBM else x for x, space in zip(operands, spaces)])


def in_hbm(cells):
    return pltpu.with_memory_space_constraint(cells, pltpu.HBM)


def spread_levels(size, flat, near, perturb, alpha_init, innovation, obs_weight, obs_mask):
    block = (SUBLANES, LANES)
    operands = (
        fold(perturb).reshape(size.planes, size.levels, *block),
        fold(alpha_init),
        fold(innovation),
        fold(obs_weight),
        obs_mask,
        near,
    )

    def pack(chips, flat, fetch):
        count = len(chips) * CORES * size.chunks
        scratch = [pltpu.VMEM((size.slots, *block), jnp.float32)]
        if fetch:
            scratch = [
                pltpu.VMEM((count, size.planes, *block), jnp.bfloat16),
                pltpu.VMEM((count, size.members, *block), jnp.float32),
                *(pltpu.VMEM(cells.shape, cells.dtype) for cells in operands[2:]),
                *scratch,
                pltpu.SemaphoreType.DMA((count,)),
                pltpu.SemaphoreType.DMA((count,)),
                pltpu.SemaphoreType.DMA((4,)),
            ]
        spaces = [pltpu.SMEM] + [pltpu.HBM if fetch else pltpu.VMEM] * 6
        kernel = functools.partial(pack_kernel, size, chips, fetch)
        return call(kernel, pack_shapes(size, chips), (flat,) + operands, scratch, spaces)

    early = list(pack(EARLY[:2], flat, True))
    flat, early[0], early[1] = lax.optimization_barrier((flat, early[0], early[1]))
    packed = pack(EARLY[2:] + (0,) + LATE, flat, False)
    early += packed[:2]
    kept, late, late_out = packed[2:4], packed[4:7], packed[7]
    crossed = shift_by(CORES, late_out)
    got = [shift_by(flat_offset(chip, 0), cells) for chip, cells in zip(EARLY, early)]
    got[1], own_out = lax.optimization_barrier((got[1], kept[1]))
    own_crossed = shift_by(CORES, own_out)
    got_late = []
    for chunk in range(size.chunks):
        base = size.planes_at(chunk)
        rows = slice(base, base + (size.planes if chunk else size.lead_rows))
        parts = [jnp.stack([cells[rows], crossed[place, rows]]) for place, cells in enumerate(late)]
        if chunk == 0:
            got[1], parts[0] = lax.optimization_barrier((got[1], parts[0]))
            got[2], parts[1] = lax.optimization_barrier((got[2], parts[1]))
            got[0], got[3], parts[2] = lax.optimization_barrier((got[0], got[3], parts[2]))
        else:
            prev = list(got_late[chunk - 1])
            prev[0], parts[0] = lax.optimization_barrier((prev[0], parts[0]))
            prev[1], parts[1] = lax.optimization_barrier((prev[1], parts[1]))
            prev[2], parts[2] = lax.optimization_barrier((prev[2], parts[2]))
            got_late[chunk - 1] = tuple(prev)
        got_late.append(tuple(shift_by(flat_offset(chip, 0), cells) for chip, cells in zip(LATE, parts)))
    early_crossed = shift_by(CORES, jnp.stack([cells[1, : size.all_rows] for cells in got]))
    shared = (kept[0], own_crossed, *got, early_crossed)
    return [shared + got_late[0] + (got_late[chunk] if chunk else ()) for chunk in range(size.chunks)]


def level_shards(perturb, alpha_init, innovation, obs_weight, coef, obs_mask):
    size = Sizes(perturb, innovation.shape[0])
    levels, rows, lon_cells = perturb.shape[3:]
    block = (SUBLANES, LANES)
    flat = (lax.axis_index("mem") * lax.axis_size("lat") + lax.axis_index("lat")).astype(jnp.int32).reshape(1)
    near = fold(coef)
    pieces = spread_levels(size, flat, near, perturb, alpha_init, innovation, obs_weight, obs_mask)
    common = (flat, near)
    all_fields = (size.chunks, size.fields, 2, *block)
    alpha_shape = (CHIPS // 2, 2, CORES * size.members, *block)
    chunks = range(size.chunks)
    first, second, back, held, innov, gain = [], [], None, None, None, None
    shapes = [(size.sums + size.sent_gains, *block), all_fields, all_fields]
    mine, held, innov = call(functools.partial(first_kernel, size), shapes, common + pieces[0])
    first.append((mine, shift_by(GROUP, mine)))
    for chunk in chunks[1:]:
        shapes = [(size.sums, *block), (len(LATE), CORES * size.members, *block)]
        known = call(functools.partial(ahead_kernel, chunk, size), shapes, common + (innov,) + pieces[0])
        late = pieces[chunk][-len(LATE) :]
        (mine,) = call(functools.partial(rest_kernel, size), [(size.sums, *block)], (flat, *known, *late))
        first.append((mine, shift_by(GROUP, mine)))
    for chunk in chunks:
        kernel = functools.partial(middle_kernel, chunk, size)
        shapes = [(size.sums, *block), alpha_shape] + ([] if chunk else [all_fields])
        operands = common + first[chunk] + (gain if chunk else held, innov) + pieces[chunk]
        mine, alpha, *rest = call(kernel, shapes, operands)
        gain = gain if chunk else rest[0]
        second.append((mine, shift_by(GROUP, mine), gain, alpha))
    for chunk in chunks:
        (back,) = call(
            functools.partial(last_kernel, chunk, size),
            [(GROUP, (chunk + 1) * (size.members + 1), *block)],
            common + second[chunk] + (() if back is None else (back,)) + pieces[chunk],
            [pltpu.VMEM((2, size.fields, *block), jnp.float32)],
        )
    groups = [[half * GROUP + place for place in range(GROUP)] for half in range(2)]
    back = lax.all_to_all(back, ("mem", "lat"), 0, 0, axis_index_groups=groups, tiled=True)
    return tuple(
        call(
            functools.partial(place_kernel, size),
            [(size.members, levels, rows, lon_cells), (size.owned, rows, lon_cells)],
            (flat, back),
        )
    )


def solution(mesh):
    in_specs = (
        P(None, None, "mem", None, "lat", None),
        P("mem", None, "lat", None),
        P("mem", "lat", None),
        P("mem", "lat", None),
        P(None, "lat", None),
        P(None, "lat", None),
    )
    out_specs = (P("mem", None, "lat", None), P("mem", "lat", None))

    def run(*args):
        body = level_shards if fits(mesh, args[0], args[2]) else shards
        return jax.shard_map(body, mesh=mesh, in_specs=in_specs, out_specs=out_specs, check_vma=False)(*args)

    return run
```

```python
import functools
import math

import jax
import jax.numpy as jnp
from jax import lax
from jax.experimental import pallas as pl
from jax.experimental.pallas import tpu as pltpu
from jax.sharding import PartitionSpec as P

ITERS = 2
DIFF_STEPS = 4
TILE = 4


def with_halo(cells, sides, width):
    for axis, dim in sides:
        count = lax.axis_size(axis)
        ends = count - 1
        head = lax.slice_in_dim(cells, 0, width, axis=dim)
        tail = lax.slice_in_dim(cells, cells.shape[dim] - width, cells.shape[dim], axis=dim)
        cells = jnp.concatenate(
            [
                lax.ppermute(tail, axis, [(i, (i + 1) % count) for i in range(ends)]),
                cells,
                lax.ppermute(head, axis, [((i + 1) % count, i) for i in range(ends)]),
            ],
            axis=dim,
        )
    return cells


def face_weights(coef):
    klat = coef[0]
    klon = coef[1]
    zero_row = jnp.zeros_like(klat[:1])
    north_face = 0.5 * (klat + jnp.concatenate([zero_row, klat[:-1]], axis=0))
    south_face = 0.5 * (klat + jnp.concatenate([klat[1:], zero_row], axis=0))
    east_face = 0.5 * (klon + jnp.roll(klon, -1, axis=1))
    west_face = 0.5 * (klon + jnp.roll(klon, 1, axis=1))
    return (north_face, south_face, east_face, west_face)


def diffuse_once(layer_field, face_list, valid_rows):
    north_face, south_face, east_face, west_face = face_list
    zero_row = jnp.zeros_like(layer_field[..., :1, :])
    above = jnp.concatenate([zero_row, layer_field[..., :-1, :]], axis=-2)
    below = jnp.concatenate([layer_field[..., 1:, :], zero_row], axis=-2)
    east_val = jnp.roll(layer_field, -1, axis=-1)
    west_val = jnp.roll(layer_field, 1, axis=-1)
    updated = layer_field + north_face * (above - layer_field) + south_face * (below - layer_field)
    updated = updated + east_face * (east_val - layer_field) + west_face * (west_val - layer_field)
    return updated * valid_rows


def rim_rows(all_faces):
    return tuple((face for face in all_faces))


def valid_mask(margin, band_rows):
    global_row = (
        lax.axis_index("lat") * band_rows
        + jnp.arange(band_rows + 2 * margin, dtype=jnp.int32)
        - margin
    )
    total_rows = band_rows * lax.axis_size("lat")
    inside = jnp.logical_and(global_row >= 0, global_row < total_rows)
    return inside.astype(jnp.float32)[:, None]


def diffuse_field(layer_field, all_faces, band_rows):
    face_list = rim_rows(all_faces)
    valid_rows = valid_mask(DIFF_STEPS, band_rows)
    extended = with_halo(layer_field, (("lat", 2),), DIFF_STEPS)
    for sweep in range(DIFF_STEPS):
        extended = diffuse_once(extended, face_list, valid_rows)
    return extended[..., DIFF_STEPS : DIFF_STEPS + band_rows, :]


def shards(perturb, alpha_init, innovation, obs_weight, coef, obs_mask):
    slot_count, var_count, members, levels, band_rows, lon_cells = perturb.shape
    owned_rows = innovation.shape[0]
    coef_ext = with_halo(coef, (("lat", 1),), DIFF_STEPS)
    all_faces = face_weights(coef_ext)
    tile_mask = jnp.repeat(jnp.repeat(obs_mask, TILE, axis=1), TILE, axis=2).astype(jnp.float32)
    first_row = lax.axis_index("mem") * owned_rows
    slot_of_row = (first_row + jnp.arange(owned_rows, dtype=jnp.int32)) // (var_count * levels)
    one_hot = (slot_of_row[:, None] == jnp.arange(slot_count, dtype=jnp.int32)[None, :]).astype(
        jnp.float32
    )
    row_mask = jnp.sum(one_hot[:, :, None, None] * tile_mask[None], axis=1)
    row_gain = obs_weight * row_mask
    alpha = alpha_init
    misfit = jnp.zeros_like(innovation)
    for sweep in range(ITERS):
        spread = diffuse_field(alpha, all_faces, band_rows)
        partial_sum = jnp.sum(perturb.astype(jnp.float32) * spread[None, None], axis=2)
        partial_sum = partial_sum.reshape(slot_count * var_count * levels, band_rows, lon_cells)
        increment = lax.psum_scatter(partial_sum, "mem", scatter_dimension=0, tiled=True)
        misfit = row_gain * (increment - innovation)
        gathered = lax.all_gather(misfit, "mem", axis=0, tiled=True)
        misfit_rows = gathered.reshape(slot_count, var_count, levels, band_rows, lon_cells)
        adjoint = jnp.sum(perturb.astype(jnp.float32) * misfit_rows[:, :, None], axis=(0, 1))
        alpha = alpha - 0.3 * (alpha + diffuse_field(adjoint, all_faces, band_rows))
    return (alpha, misfit)


LANES = 128
SUBLANES = 8
CHIPS = 8
CORES = 2
GROUP = CHIPS * CORES
EARLY = (1, 6, 2, 5)
LATE = (4, 3, 7)


def fold(cells):
    lead, (rows, cols) = cells.shape[:-2], cells.shape[-2:]
    parts = cells.reshape(*lead, rows, cols // LANES, LANES).swapaxes(-3, -2)
    return parts.reshape(*lead, rows * cols // LANES, LANES)


def fits(mesh, perturb, innovation):
    slot_count, var_count, members, levels, rows, lon_cells = perturb.shape
    mem, lat = mesh.shape["mem"], mesh.shape["lat"]
    if lat != 2 or mem != 2 * GROUP // lat:
        return False
    if rows != lat * TILE or DIFF_STEPS > TILE or TILE * lon_cells != SUBLANES * LANES:
        return False
    total = slot_count * var_count * levels
    if members % mem or levels % GROUP or total % mem or total // mem > levels:
        return False
    return held_fields(slot_count * var_count, levels) is not None


def held_fields(fields, levels):
    chunks = []
    for chunk in range(levels // GROUP):
        halves = ([], [])
        for field in range(fields):
            rows = [field * levels + chunk * GROUP + place for place in range(GROUP)]
            sides = {2 * row // (fields * levels) for row in rows}
            if len(sides) != 1:
                return None
            halves[sides.pop()].append(field)
        if not halves[0] or not halves[1]:
            return None
        longest = max(len(half) for half in halves)
        chunks.append([half + half[-1:] * (longest - len(half)) for half in halves])
    return chunks


def flat_offset(chip, core):
    return ((chip >> 1) << 2) | (core << 1) | (chip & 1)


def shift_by(mask, cells):
    axes = ("mem", "lat")
    count = lax.axis_size("mem") * lax.axis_size("lat")
    return lax.ppermute(cells, axes, [(i, i ^ mask) for i in range(count)])


class Sizes:
    def __init__(self, perturb, owned_rows):
        slots, variables, members, levels = perturb.shape[:4]
        self.slots = slots
        self.vars = variables
        self.fields = slots * variables
        self.members = members
        self.levels = levels
        self.owned = owned_rows
        self.chunks = levels // GROUP
        self.planes = self.fields * members
        self.extras = members + 2
        self.lead_rows = self.planes + self.chunks * self.extras
        self.all_rows = self.lead_rows + (self.chunks - 1) * self.planes
        self.held = held_fields(self.fields, levels)
        self.sums = self.fields * 2
        self.sent_gains = 2 * sum(len(half[0]) for half in self.held)

    def planes_at(self, chunk):
        return self.lead_rows + (chunk - 1) * self.planes if chunk else 0

    def extras_at(self, chunk):
        return self.planes + chunk * self.extras


def row_in_block(size, level, mem_index):
    row = lax.rem(level + size.levels * size.owned - lax.rem(size.owned * mem_index, size.levels), size.levels)
    return row, row < size.owned, lax.div(size.owned * mem_index + row, size.levels)


def pack_shapes(size, chips):
    one = (size.all_rows, SUBLANES, LANES)
    shapes = []
    for chip in chips:
        if chip == 0:
            shapes += [one, one]
        elif chip in EARLY:
            shapes.append((CORES, size.all_rows + (chip == 1), SUBLANES, LANES))
        else:
            shapes.append(one)
    return shapes + [(len(LATE), *one)] * (LATE[0] in chips)


def pack_target(outs, chips, chip, core):
    place = chips.index(chip) + (0 in chips[: chips.index(chip)])
    if chip == 0:
        return outs[place + core]
    if chip in EARLY:
        return outs[place].at[core]
    return outs[place] if core == 0 else outs[-1].at[LATE.index(chip)]


def pack_kernel(size, chips, flat_ref, perturb_hbm, alpha_hbm, innov_hbm, weight_hbm, mask_hbm, near_hbm, *refs):
    outs, scratch = refs[:-10], refs[-10:]
    perturb_ref, alpha_ref, innov_ref, weight_ref, mask_ref, near_ref, tiles_ref, plane_sems, alpha_sems, sems = scratch
    flat = flat_ref[0]
    own = lax.rem(flat, GROUP)
    mem_index = lax.div(flat, 2)
    places = [(chip, core, chunk) for chip in chips for core in range(CORES) for chunk in range(size.chunks)]
    levels = [lax.bitwise_xor(own, flat_offset(chip, core)) + chunk * GROUP for chip, core, chunk in places]
    plane_copies = [
        pltpu.make_async_copy(perturb_hbm.at[:, level], perturb_ref.at[place], plane_sems.at[place])
        for place, level in enumerate(levels)
    ]
    alpha_copies = [
        pltpu.make_async_copy(alpha_hbm.at[:, level], alpha_ref.at[place], alpha_sems.at[place])
        for place, level in enumerate(levels)
    ]
    pairs = ((mask_hbm, mask_ref), (near_hbm, near_ref), (innov_hbm, innov_ref), (weight_hbm, weight_ref))
    copies = [pltpu.make_async_copy(source, target, sems.at[place]) for place, (source, target) in enumerate(pairs)]
    for copy in plane_copies + copies + alpha_copies:
        copy.start()
    copies[0].wait()
    tiles = mask_ref.shape[-1]
    shape = (tiles, tiles * TILE)
    spread_out = lax.broadcasted_iota(jnp.int32, shape, 0) == lax.div(lax.broadcasted_iota(jnp.int32, shape, 1), TILE)
    line = lax.broadcasted_iota(jnp.int32, (SUBLANES, LANES), 0)
    for slot in range(size.slots):
        cells = jnp.dot(
            mask_ref[slot].astype(jnp.float32), spread_out.astype(jnp.float32), preferred_element_type=jnp.float32
        )
        tiles_ref[slot] = jnp.where(line < TILE, cells[:, :LANES], cells[:, LANES:])
    copies[1].wait()
    if 1 in chips:
        coef_out = outs[chips.index(1)]
        coef_out[0, size.all_rows] = near_ref[0]
        coef_out[1, size.all_rows] = near_ref[1]
    for place, (chip, core, chunk) in enumerate(places):
        plane_copies[place].wait()
        base = size.planes_at(chunk)
        pack_target(outs, chips, chip, core)[base : base + size.planes] = perturb_ref[place].astype(jnp.float32)
    copies[2].wait()
    copies[3].wait()
    for place, (chip, core, chunk) in enumerate(places):
        out = pack_target(outs, chips, chip, core)
        base = size.extras_at(chunk)
        alpha_copies[place].wait()
        out[base : base + size.members] = alpha_ref[place]
        row, inside, field = row_in_block(size, levels[place], mem_index)
        row = jnp.minimum(row, size.owned - 1)
        slot = jnp.minimum(lax.div(field, size.vars), size.slots - 1)
        kept = jnp.where(inside, 1.0, 0.0).astype(jnp.float32)
        out[base + size.members] = innov_ref[row] * kept
        out[base + size.members + 1] = weight_ref[row] * tiles_ref[slot] * kept


class Pieces:
    def __init__(self, size, chunk, refs):
        self.size = size
        self.chunk = chunk
        self.refs = refs
        self.far_ref = refs[2 + EARLY.index(1)]

    def place(self, chip, core):
        if chip == 0:
            return self.refs[core], (), True
        if chip in EARLY:
            place = EARLY.index(chip)
            if core == 0:
                return self.refs[2 + place], (0,), True
            return self.refs[2 + len(EARLY)], (place,), True
        return self.refs[3 + len(EARLY) + LATE.index(chip)], (core,), False

    def plane(self, chip, core, row):
        ref, lead, whole = self.place(chip, core)
        if not whole and self.chunk:
            ref = self.refs[3 + len(EARLY) + len(LATE) + LATE.index(chip)]
        base = self.size.planes_at(self.chunk) if whole else 0
        return ref[lead + (base + row,)]

    def extra(self, chip, core, chunk, row):
        ref, lead, _ = self.place(chip, core)
        return ref[lead + (self.size.extras_at(chunk) + row,)]

    def alpha(self, chip, core):
        ref, lead, _ = self.place(chip, core)
        base = self.size.extras_at(self.chunk)
        return ref[lead + (slice(base, base + self.size.members),)]

    def far(self):
        return [self.far_ref[part, self.size.all_rows] for part in range(2)]


def roll(cells, shift, axis):
    return pltpu.roll(cells, shift, axis=cells.ndim + axis)


def neighbours(own, other, edges):
    row0, row3, lane0, lane_last = edges
    turned = roll(own, SUBLANES // 2, -2)
    across = roll(other, SUBLANES // 2, -2)
    above = roll(jnp.where(row3, across, own), 1, -2)
    below = roll(jnp.where(row0, across, own), SUBLANES - 1, -2)
    east = roll(jnp.where(lane0, turned, own), LANES - 1, -1)
    west = roll(jnp.where(lane_last, turned, own), 1, -1)
    return above, below, east, west


def stencils(flat, near, far):
    shape = (SUBLANES, LANES)
    line = lax.rem(lax.broadcasted_iota(jnp.int32, shape, 0), TILE)
    lane = lax.broadcasted_iota(jnp.int32, shape, 1)
    edges = (line == 0, line == TILE - 1, lane == 0, lane == LANES - 1)
    band = lax.rem(flat, 2)
    weights = []
    for half, (own, other) in enumerate(((near, far), (far, near))):
        here = lax.bitwise_xor(band, half)
        open_top = jnp.where(jnp.logical_and(edges[0], here == 0), 0.0, 1.0).astype(jnp.float32)
        open_end = jnp.where(jnp.logical_and(edges[1], here == 1), 0.0, 1.0).astype(jnp.float32)
        above, below, _, _ = neighbours(own[0], other[0], edges)
        _, _, east, west = neighbours(own[1], other[1], edges)
        north = 0.5 * (own[0] + above * open_top)
        south = 0.5 * (own[0] + below * open_end)
        east = 0.5 * (own[1] + east)
        west = 0.5 * (own[1] + west)
        centre = 1.0 - north - south - east - west
        weights.append((centre, north * open_top, south * open_end, east, west))
    return edges, weights


def diffuse_pair(near, far, stencil):
    edges, weights = stencil
    for _ in range(DIFF_STEPS):
        pair = []
        for (own, other), (centre, north, south, east, west) in zip(((near, far), (far, near)), weights):
            above, below, right, left = neighbours(own, other, edges)
            pair.append(centre * own + north * above + south * below + east * right + west * left)
        near, far = pair
    return near, far


def add_chip(size, pieces, chip, spread, sums):
    for core in range(CORES):
        for field in range(size.fields):
            for member in range(size.members):
                plane = pieces.plane(chip, core, field * size.members + member)
                term = plane * spread[core * size.members + member]
                sums[field] = term if sums[field] is None else sums[field] + term


def add_products(size, pieces, pair, spread, sums):
    for half in range(2):
        add_chip(size, pieces, 2 * pair + half, spread[half], sums[half])


def adjoint_of(size, pieces, pair, misfit):
    halves = []
    for half in range(2):
        found = []
        for core in range(CORES):
            for member in range(size.members):
                total = None
                for field in range(size.fields):
                    plane = pieces.plane(2 * pair + half, core, field * size.members + member)
                    term = plane * misfit[half][field]
                    total = term if total is None else total + term
                found.append(total)
        halves.append(jnp.stack(found))
    return halves


def first_alpha(pieces, pair):
    return [
        jnp.concatenate([pieces.alpha(2 * pair + half, core) for core in range(CORES)]) for half in range(2)
    ]


def gather_slots(size, pieces, mem_index, own, gain_ref, innov_ref):
    gain_ref[...] = jnp.zeros_like(gain_ref)
    innov_ref[...] = jnp.zeros_like(innov_ref)
    for chunk in range(size.chunks):
        for chip in range(0, CHIPS, 2):
            for core in range(CORES):
                source = lax.bitwise_xor(mem_index, (chip & 6) | core)
                _, inside, field = row_in_block(size, own + chunk * GROUP, source)

                @pl.when(inside)
                def _(chip=chip, core=core, chunk=chunk, field=field):
                    for half in range(2):
                        innov_ref[chunk, field, half] = pieces.extra(chip + half, core, chunk, size.members)
                        gain_ref[chunk, field, half] = pieces.extra(chip + half, core, chunk, size.members + 1)


def gain_places(size):
    row, found = size.sums, []
    for chunk, halves in enumerate(size.held):
        for first, second in zip(*halves):
            found.append((row, chunk, first, second))
            row += 2
    return found


def first_kernel(size, flat_ref, near_ref, *refs):
    sum_ref, gain_ref, innov_ref = refs[-3:]
    pieces = Pieces(size, 0, refs[:-3])
    flat = flat_ref[0]
    stencil = stencils(flat, [near_ref[0], near_ref[1]], pieces.far())
    side = lax.div(flat, GROUP)
    gather_slots(size, pieces, lax.div(flat, 2), lax.rem(flat, GROUP), gain_ref, innov_ref)
    for row, part, first, second in gain_places(size):
        sum_ref[pl.ds(row, 2)] = gain_ref[part, jnp.where(side == 0, first, second)]
    sums = [[None] * size.fields for _ in range(2)]
    for pair in range(CHIPS // 2):
        spread = diffuse_pair(*first_alpha(pieces, pair), stencil)
        add_products(size, pieces, pair, spread, sums)
    for field in range(size.fields):
        for half in range(2):
            sum_ref[field * 2 + half] = sums[half][field] - innov_ref[0, field, half]


def ahead_kernel(chunk, size, flat_ref, near_ref, innov_ref, *refs):
    part_ref, spread_ref = refs[-2:]
    pieces = Pieces(size, chunk, refs[:-2])
    stencil = stencils(flat_ref[0], [near_ref[0], near_ref[1]], pieces.far())
    sums = [[None] * size.fields for _ in range(2)]
    for pair in range(CHIPS // 2):
        spread = diffuse_pair(*first_alpha(pieces, pair), stencil)
        for half in range(2):
            chip = 2 * pair + half
            if chip in LATE:
                spread_ref[LATE.index(chip)] = spread[half]
            else:
                add_chip(size, pieces, chip, spread[half], sums[half])
    for field in range(size.fields):
        for half in range(2):
            part_ref[field * 2 + half] = sums[half][field] - innov_ref[chunk, field, half]


def rest_kernel(size, flat_ref, part_ref, spread_ref, *refs):
    late, sum_ref = refs[:-1], refs[-1]
    sums = [[part_ref[field * 2 + half] for field in range(size.fields)] for half in range(2)]
    for place, chip in enumerate(LATE):
        for core in range(CORES):
            for field in range(size.fields):
                for member in range(size.members):
                    plane = late[place][core, field * size.members + member]
                    sums[chip & 1][field] += plane * spread_ref[place, core * size.members + member]
    for field in range(size.fields):
        for half in range(2):
            sum_ref[field * 2 + half] = sums[half][field]


def misfit_of(size, chunk, gain_ref, mine_ref, theirs_ref):
    return [
        [
            gain_ref[chunk, field, half] * (mine_ref[field * 2 + half] + theirs_ref[field * 2 + half])
            for field in range(size.fields)
        ]
        for half in range(2)
    ]


def middle_kernel(chunk, size, flat_ref, near_ref, mine_ref, theirs_ref, gain_in_ref, innov_ref, *refs):
    if chunk:
        gain_ref, (sum_ref, alpha_ref) = gain_in_ref, refs[-2:]
        pieces = Pieces(size, chunk, refs[:-2])
    else:
        sum_ref, alpha_ref, gain_ref = refs[-3:]
        pieces = Pieces(size, chunk, refs[:-3])
    flat = flat_ref[0]
    stencil = stencils(flat, [near_ref[0], near_ref[1]], pieces.far())
    if not chunk:
        side = lax.div(flat, GROUP)
        gain_ref[...] = gain_in_ref[...]
        for row, part, first, second in gain_places(size):
            gain_ref[part, jnp.where(side == 0, second, first)] = theirs_ref[pl.ds(row, 2)]
    misfit = misfit_of(size, chunk, gain_ref, mine_ref, theirs_ref)
    sums = [[None] * size.fields for _ in range(2)]
    for pair in range(CHIPS // 2):
        change = diffuse_pair(*adjoint_of(size, pieces, pair, misfit), stencil)
        before = first_alpha(pieces, pair)
        alpha = [old - 0.3 * (old + new) for old, new in zip(before, change)]
        for half in range(2):
            alpha_ref[pair, half] = alpha[half]
        add_products(size, pieces, pair, diffuse_pair(*alpha, stencil), sums)
    for field in range(size.fields):
        for half in range(2):
            sum_ref[field * 2 + half] = sums[half][field] - innov_ref[chunk, field, half]


def last_kernel(chunk, size, flat_ref, near_ref, mine_ref, theirs_ref, gain_ref, alpha_ref, *refs):
    refs, (out_ref, misfit_ref) = refs[:-2], refs[-2:]
    flat = flat_ref[0]
    own = lax.rem(flat, GROUP)
    mem_index = lax.div(flat, 2)
    base = chunk * (size.members + 1)
    if chunk:
        out_ref[:, :base] = refs[0][...]
        refs = refs[1:]
    pieces = Pieces(size, chunk, refs)
    stencil = stencils(flat, [near_ref[0], near_ref[1]], pieces.far())
    misfit = misfit_of(size, chunk, gain_ref, mine_ref, theirs_ref)
    for half in range(2):
        for field in range(size.fields):
            misfit_ref[half, field] = misfit[half][field]
    level = own + chunk * GROUP
    for pair in range(CHIPS // 2):
        change = diffuse_pair(*adjoint_of(size, pieces, pair, misfit), stencil)
        for half in range(2):
            old = alpha_ref[pair, half]
            alpha = old - 0.3 * (old + change[half])
            chip = 2 * pair + half
            for core in range(CORES):
                target = lax.bitwise_xor(own, flat_offset(chip, core))
                out_ref[target, base : base + size.members] = alpha[core * size.members : (core + 1) * size.members]
                _, _, field = row_in_block(size, level, lax.bitwise_xor(mem_index, (chip & 6) | core))
                out_ref[target, base + size.members] = misfit_ref[half, jnp.minimum(field, size.fields - 1)]


def unfold_into(out, at, block):
    rows = block.shape[-2] // 2
    out[at + (slice(None), slice(0, LANES))] = block[..., :rows, :]
    out[at + (slice(None), slice(LANES, 2 * LANES))] = block[..., rows:, :]


def place_kernel(size, flat_ref, back_ref, alpha_hbm, misfit_hbm, alpha_ref, misfit_ref, sems):
    mem_index = lax.div(flat_ref[0], 2)
    for source in range(GROUP):
        for chunk in range(size.chunks):
            slot = chunk * (size.members + 1) + size.members
            row, inside, _ = row_in_block(size, source + chunk * GROUP, mem_index)

            @pl.when(inside)
            def _(source=source, slot=slot, row=row):
                unfold_into(misfit_ref, (row,), back_ref[source, slot])

    copies = [pltpu.make_async_copy(misfit_ref, misfit_hbm, sems.at[size.members])]
    copies[0].start()
    for member in range(size.members):
        for source in range(GROUP):
            for chunk in range(size.chunks):
                block = back_ref[source, chunk * (size.members + 1) + member]
                unfold_into(alpha_ref, (member, source + chunk * GROUP), block)
        copies.append(pltpu.make_async_copy(alpha_ref.at[member], alpha_hbm.at[member], sems.at[member]))
        copies[-1].start()
    for copy in copies:
        copy.wait()


def call(kernel, outs, operands, scratch=(), spaces=None, out_space=pltpu.VMEM, limit=24):
    spaces = spaces or [pltpu.VMEM] * len(operands)
    moved = 4 * sum(math.prod(shape) for shape in outs) + sum(x.size * x.dtype.itemsize for x in operands)
    return pl.pallas_call(
        kernel,
        out_shape=[jax.ShapeDtypeStruct(shape, jnp.float32) for shape in outs],
        in_specs=[pl.BlockSpec(memory_space=space) for space in [pltpu.SMEM] + spaces[1:]],
        out_specs=[pl.BlockSpec(memory_space=out_space)] * len(outs),
        scratch_shapes=scratch,
        cost_estimate=pl.CostEstimate(flops=moved, bytes_accessed=moved, transcendentals=0),
        compiler_params=pltpu.CompilerParams(vmem_limit_bytes=limit * 1024 * 1024),
    )(*[in_hbm(x) if space is pltpu.HBM else x for x, space in zip(operands, spaces)])


def in_hbm(cells):
    return pltpu.with_memory_space_constraint(cells, pltpu.HBM)


def spread_levels(size, flat, near, perturb, alpha_init, innovation, obs_weight, obs_mask):
    block = (SUBLANES, LANES)
    operands = (
        fold(perturb).reshape(size.planes, size.levels, *block),
        fold(alpha_init),
        fold(innovation),
        fold(obs_weight),
        obs_mask,
        near,
    )

    def pack(chips, flat):
        count = len(chips) * CORES * size.chunks
        return call(
            functools.partial(pack_kernel, size, chips),
            pack_shapes(size, chips),
            (flat,) + operands,
            [
                pltpu.VMEM((count, size.planes, *block), jnp.bfloat16),
                pltpu.VMEM((count, size.members, *block), jnp.float32),
                pltpu.VMEM((size.owned, *block), jnp.float32),
                pltpu.VMEM((size.owned, *block), jnp.float32),
                pltpu.VMEM(obs_mask.shape, jnp.int32),
                pltpu.VMEM(near.shape, jnp.float32),
                pltpu.VMEM((size.slots, *block), jnp.float32),
                pltpu.SemaphoreType.DMA((count,)),
                pltpu.SemaphoreType.DMA((count,)),
                pltpu.SemaphoreType.DMA((4,)),
            ],
            [pltpu.SMEM] + [pltpu.HBM] * 6,
        )

    early = list(pack(EARLY[:2], flat))
    flat, early[0], early[1] = lax.optimization_barrier((flat, early[0], early[1]))
    packed = pack(EARLY[2:] + (0,) + LATE, flat)
    early += packed[:2]
    kept, late, late_out = packed[2:4], packed[4:7], packed[7]
    crossed = shift_by(CORES, late_out)
    own_crossed = shift_by(CORES, kept[1])
    got = [shift_by(flat_offset(chip, 0), cells) for chip, cells in zip(EARLY, early)]
    got_late = []
    for chunk in range(size.chunks):
        base = size.planes_at(chunk)
        rows = slice(base, base + (size.planes if chunk else size.lead_rows))
        parts = [jnp.stack([cells[rows], crossed[place, rows]]) for place, cells in enumerate(late)]
        if chunk == 0:
            got[1], parts[0] = lax.optimization_barrier((got[1], parts[0]))
            got[2], parts[1] = lax.optimization_barrier((got[2], parts[1]))
            got[0], got[3], parts[2] = lax.optimization_barrier((got[0], got[3], parts[2]))
        else:
            prev = list(got_late[chunk - 1])
            prev[0], parts[0] = lax.optimization_barrier((prev[0], parts[0]))
            prev[1], parts[1] = lax.optimization_barrier((prev[1], parts[1]))
            prev[2], parts[2] = lax.optimization_barrier((prev[2], parts[2]))
            got_late[chunk - 1] = tuple(prev)
        got_late.append(tuple(shift_by(flat_offset(chip, 0), cells) for chip, cells in zip(LATE, parts)))
    early_crossed = shift_by(CORES, jnp.stack([cells[1, : size.all_rows] for cells in got]))
    shared = (kept[0], own_crossed, *got, early_crossed)
    return [shared + got_late[0] + (got_late[chunk] if chunk else ()) for chunk in range(size.chunks)]


def level_shards(perturb, alpha_init, innovation, obs_weight, coef, obs_mask):
    size = Sizes(perturb, innovation.shape[0])
    levels, rows, lon_cells = perturb.shape[3:]
    block = (SUBLANES, LANES)
    flat = (lax.axis_index("mem") * lax.axis_size("lat") + lax.axis_index("lat")).astype(jnp.int32).reshape(1)
    near = fold(coef)
    pieces = spread_levels(size, flat, near, perturb, alpha_init, innovation, obs_weight, obs_mask)
    common = (flat, near)
    all_fields = (size.chunks, size.fields, 2, *block)
    alpha_shape = (CHIPS // 2, 2, CORES * size.members, *block)
    chunks = range(size.chunks)
    first, second, back, held, innov, gain = [], [], None, None, None, None
    shapes = [(size.sums + size.sent_gains, *block), all_fields, all_fields]
    mine, held, innov = call(functools.partial(first_kernel, size), shapes, common + pieces[0])
    first.append((mine, shift_by(GROUP, mine)))
    for chunk in chunks[1:]:
        shapes = [(size.sums, *block), (len(LATE), CORES * size.members, *block)]
        known = call(functools.partial(ahead_kernel, chunk, size), shapes, common + (innov,) + pieces[0])
        late = pieces[chunk][-len(LATE) :]
        (mine,) = call(functools.partial(rest_kernel, size), [(size.sums, *block)], (flat, *known, *late))
        first.append((mine, shift_by(GROUP, mine)))
    for chunk in chunks:
        kernel = functools.partial(middle_kernel, chunk, size)
        shapes = [(size.sums, *block), alpha_shape] + ([] if chunk else [all_fields])
        operands = common + first[chunk] + (gain if chunk else held, innov) + pieces[chunk]
        mine, alpha, *rest = call(kernel, shapes, operands)
        gain = gain if chunk else rest[0]
        second.append((mine, shift_by(GROUP, mine), gain, alpha))
    for chunk in chunks:
        (back,) = call(
            functools.partial(last_kernel, chunk, size),
            [(GROUP, (chunk + 1) * (size.members + 1), *block)],
            common + second[chunk] + (() if back is None else (back,)) + pieces[chunk],
            [pltpu.VMEM((2, size.fields, *block), jnp.float32)],
        )
    groups = [[half * GROUP + place for place in range(GROUP)] for half in range(2)]
    back = lax.all_to_all(back, ("mem", "lat"), 0, 0, axis_index_groups=groups, tiled=True)
    places = [(size.members, levels, rows, lon_cells), (size.owned, rows, lon_cells)]
    return tuple(
        call(
            functools.partial(place_kernel, size),
            places,
            (flat, back),
            [*(pltpu.VMEM(place, jnp.float32) for place in places), pltpu.SemaphoreType.DMA((size.members + 1,))],
            out_space=pltpu.HBM,
        )
    )


def solution(mesh):
    in_specs = (
        P(None, None, "mem", None, "lat", None),
        P("mem", None, "lat", None),
        P("mem", "lat", None),
        P("mem", "lat", None),
        P(None, "lat", None),
        P(None, "lat", None),
    )
    out_specs = (P("mem", None, "lat", None), P("mem", "lat", None))

    def run(*args):
        body = level_shards if fits(mesh, args[0], args[2]) else shards
        return jax.shard_map(body, mesh=mesh, in_specs=in_specs, out_specs=out_specs, check_vma=False)(*args)

    return run
```
